256 devices in a mesh: lat: 64 (over x, z, core), chan: 4 (over y).
Axes of the slice: x: 4, y: 4, z: 8, core: 2. Of those that a mesh axis runs over, the one named last changes fastest.
Arguments:
- field_in: bfloat16 [768, 384, 720], P('lat', 'chan'), may hold values from -6 to 6
- cotangent: bfloat16 [768, 384, 720], P('lat', 'chan'), may hold values from -1.1953125 to 1.1953125
- weights: bfloat16 [512, 384, 384], P(('lat', 'chan')), may hold values from -0.3125 to 0.3125
- row_counts: int32 [64], replicated, may hold values from 0 to 12, as said below
- slot_degree: int32 [512], replicated, may hold values from 0 to 360, as said below
Outputs:
- field_grad: bfloat16 [768, 384, 720], P('lat', 'chan')
- weight_grad: float32 [512, 384, 384], P(('lat', 'chan'))
The draws below stay inside these ranges and needn't reach their ends.
Inputs may be any that keep to these rules, and one draw needn't show every extreme that they name: `row_counts`: lat devices 2p and 2p+1 together hold exactly 12 live rows; some device holds 12. `slot_degree`: each degree 0 to 359 stands in exactly one slot; the other slots hold 360.
All inputs are finite; a program needn't handle non-finite values.
Results may differ from the reference program's by a relative error of at most 0.015.
Values may be sent and summed in bfloat16 or wider, within the bound.
No kernel may reach another device: no remote copies, remote signals or barrier semaphores. Data moves between devices by JAX's collectives and lax.ppermute only.
A program may use at most 128 MiB of HBM per device.

```python
import math
import jax
import jax.numpy as jnp
from jax import lax

C = 384
NLON = 720
L = 360
M = 360
ROWS = 6
NLAT = 384
GRIDROWS = 768
SLOTS = 512
N_LAT = 64


def draw_row_counts(key, part):
    key = jax.random.fold_in(key, 7)
    pair_count = N_LAT // 2
    shifts = jax.random.randint(jax.random.fold_in(key, 1), (pair_count,), -ROWS, ROWS + 1)
    chosen = jax.random.randint(jax.random.fold_in(key, 2), (), 0, pair_count)
    direction = jax.random.randint(jax.random.fold_in(key, 3), (), 0, 2) * 2 - 1
    shifts = jnp.where(jnp.arange(pair_count) == chosen, direction * ROWS, shifts)
    return jnp.stack([ROWS + shifts, ROWS - shifts], axis=1).reshape(N_LAT).astype(jnp.int32)


def draw_slot_degree(key, part):
    key = jax.random.fold_in(key, 13)
    shuffled = jax.random.permutation(key, SLOTS)
    return jnp.where(shuffled < L, shuffled, L).astype(jnp.int32)


def steps_of(rng, shape, cuts, least, high):
    level = 1.0
    for axis_at, parts in cuts:
        steps = jax.random.uniform(jax.random.fold_in(jax.random.fold_in(rng, 6), axis_at), (parts,), jnp.float32, least / len(cuts), high / len(cuts))
        level = level * jnp.repeat(jnp.exp(steps), shape[axis_at] // parts).reshape((-1,) + (1,) * (len(shape) - 1 - axis_at))
    return level


def centred(stream_key, dims, width, limit, cuts=(), kind=jnp.bfloat16):
    gain = steps_of(stream_key, dims, cuts, -0.22, 0.18) if cuts else 1.0
    values = jax.random.normal(stream_key, dims, jnp.float32) * width * gain
    return jnp.minimum(jnp.maximum(values, -limit), limit).astype(kind)


def setup_inputs(seed: int = 0) -> dict:
    seeds = jax.random.split(jax.random.key(seed), 6)
    return {
        "field_in": centred(seeds[0], (GRIDROWS, C, NLON), 1.0, 6.0, ((0, 64), (1, 4))),
        "cotangent": centred(seeds[1], (GRIDROWS, C, NLON), 0.2, 1.1953125, ((0, 64), (1, 4))),
        "weights": centred(seeds[2], (SLOTS, C, C), C ** -0.5, 0.3125, ((0, 256),)),
        "row_counts": draw_row_counts(jax.random.fold_in(seeds[5], 71), 0),
        "slot_degree": draw_slot_degree(jax.random.fold_in(seeds[5], 71), 0),
    }


RESCALE = 2.0 ** 40
RESCALE_LOG = 40.0 * math.log(2.0)

def legendre_rows(orders, cosine, logsine, degrees, latitudes):
    order_col = orders[:, None]
    start_log = 0.5 * jnp.log((2.0 * order_col + 1.0) / (4.0 * math.pi)) + 0.5 * lax.lgamma(2.0 * order_col + 1.0) - order_col * math.log(2.0) - lax.lgamma(order_col + 1.0) + order_col * logsine[None, :] + 0.5 * math.log(2.0 * math.pi * math.pi / latitudes) + 0.5 * logsine[None, :]
    grid_shape = start_log.shape
    cos_grid = jnp.broadcast_to(cosine[None, :], grid_shape)
    degree_list = jnp.arange(degrees).astype(jnp.float32)
    degree_col = degree_list[:, None]
    square = (orders * orders)[None, :]
    upper_all = jnp.sqrt(jnp.maximum(4.0 * degree_col * degree_col - 1.0, 1.0) / jnp.maximum(degree_col * degree_col - square, 1.0))
    lower_all = jnp.sqrt(jnp.maximum((degree_col - 1.0) * (degree_col - 1.0) - square, 0.0) / jnp.maximum(4.0 * (degree_col - 1.0) * (degree_col - 1.0) - 1.0, 1.0))

    def advance(carry, inputs):
        previous, current, scale_log = carry
        degree, coef_upper, coef_lower = inputs
        fresh_value = coef_upper[:, None] * (cos_grid * current - coef_lower[:, None] * previous)
        rising = degree > order_col
        previous = jnp.where(rising, current, previous)
        current = jnp.where(rising, fresh_value, current)
        too_large = jnp.abs(current) > RESCALE
        factor = jnp.where(too_large, 1.0 / RESCALE, 1.0)
        previous = previous * factor
        current = current * factor
        scale_log = scale_log + jnp.where(too_large, RESCALE_LOG, 0.0)
        result = jnp.where(degree >= order_col, current * jnp.exp(scale_log), 0.0)
        return ((previous, current, scale_log), result)
    initial = (jnp.zeros(grid_shape, jnp.float32), jnp.ones(grid_shape, jnp.float32), start_log)
    final_state, values = lax.scan(advance, initial, (degree_list, upper_all, lower_all))
    return values

def fourier_table(orders, live_mask, length_lon):
    longitude = jnp.arange(length_lon, dtype=jnp.int32)[:, None]
    turn_count = longitude * orders[None, :] % length_lon
    angles = turn_count.astype(jnp.float32) * (2.0 * math.pi / length_lon)
    scaling = 1.0 / math.sqrt(length_lon)
    paired = jnp.stack([jnp.cos(angles) * scaling, -jnp.sin(angles) * scaling], axis=-1) * live_mask[None, :, None]
    return paired.reshape(length_lon, 2 * orders.shape[0]).astype(jnp.bfloat16)

def reference(field_in, cotangent, weights, row_counts, slot_degree):
    lat_devices = row_counts.shape[0]
    rowmax = field_in.shape[0] // lat_devices
    offsets = jnp.cumsum(row_counts) - row_counts
    global_row = jnp.arange(lat_devices * rowmax, dtype=jnp.int32)
    owner_dev = global_row // rowmax
    within = global_row % rowmax
    live_rows = within < row_counts[owner_dev]
    target = jnp.where(live_rows, offsets[owner_dev] + within, NLAT).astype(jnp.int32)
    field_grid = jnp.zeros((NLAT, C, NLON), jnp.bfloat16).at[target].set(field_in, mode='drop')
    cotan_grid = jnp.zeros((NLAT, C, NLON), jnp.bfloat16).at[target].set(cotangent, mode='drop')
    orders = jnp.arange(M, dtype=jnp.int32)
    fourier = fourier_table(orders, jnp.ones((M,), jnp.float32), NLON)
    doubled = fourier * jnp.repeat(jnp.where(orders == 0, 1.0, 2.0), 2).astype(jnp.bfloat16)
    spectra = jnp.dot(field_grid, fourier, preferred_element_type=jnp.float32).astype(jnp.bfloat16).reshape(NLAT, C, M, 2)
    dspectra = jnp.dot(cotan_grid, doubled, preferred_element_type=jnp.float32).astype(jnp.bfloat16).reshape(NLAT, C, M, 2)
    colatitude = (jnp.arange(NLAT).astype(jnp.float32) + 0.5) * (math.pi / NLAT)
    cosine = jnp.cos(colatitude)
    logsine = jnp.log(jnp.sin(colatitude))
    order_blocks = orders.reshape(M // 8, 8)

    def analysis(order_block):
        legendre = legendre_rows(order_block.astype(jnp.float32), cosine, logsine, L, NLAT).astype(jnp.bfloat16)
        legendre_wide = legendre.astype(jnp.float32)
        inputs = jnp.take(spectra, order_block, axis=2).astype(jnp.float32)
        dinputs = jnp.take(dspectra, order_block, axis=2).astype(jnp.float32)
        coeff_block = jnp.einsum('lpk,kcpr->lprc', legendre_wide, inputs, precision=lax.Precision.HIGHEST).astype(jnp.bfloat16)
        dcoeff_block = jnp.einsum('lpk,kcpr->lprc', legendre_wide, dinputs, precision=lax.Precision.HIGHEST).astype(jnp.bfloat16)
        return (coeff_block, dcoeff_block)
    coeffs, dcoeffs = lax.map(analysis, order_blocks)
    coeffs = coeffs.transpose(1, 0, 2, 3, 4).reshape(L, M, 2, C)
    dcoeffs = dcoeffs.transpose(1, 0, 2, 3, 4).reshape(L, M, 2, C)
    degree_weights = jnp.zeros((L, C, C), jnp.bfloat16).at[slot_degree].set(weights, mode='drop')

    def spectral(items):
        coeff_row, dcoeff_row, weight_row = items
        grad_row = jnp.einsum('mri,mrc->ic', coeff_row.astype(jnp.float32), dcoeff_row.astype(jnp.float32), precision=lax.Precision.HIGHEST)
        back_row = jnp.einsum('mrc,ic->mri', dcoeff_row.astype(jnp.float32), weight_row.astype(jnp.float32), precision=lax.Precision.HIGHEST).astype(jnp.bfloat16)
        return (grad_row, back_row)
    degree_grads, dcoeffs_in = lax.map(spectral, (coeffs, dcoeffs, degree_weights))
    slot_live = slot_degree < L
    weight_grad = jnp.where(slot_live[:, None, None], degree_grads[jnp.minimum(slot_degree, L - 1)], 0.0)

    def synthesis(order_block):
        legendre = legendre_rows(order_block.astype(jnp.float32), cosine, logsine, L, NLAT).astype(jnp.bfloat16)
        piece = jnp.take(dcoeffs_in, order_block, axis=1).astype(jnp.float32)
        return jnp.einsum('lpk,lprc->kcpr', legendre.astype(jnp.float32), piece, precision=lax.Precision.HIGHEST).astype(jnp.bfloat16)
    pieces = lax.map(synthesis, order_blocks)
    dspectra_in = pieces.transpose(1, 2, 0, 3, 4).reshape(NLAT, C, 2 * M)
    grad_grid = jnp.dot(dspectra_in, fourier.T, preferred_element_type=jnp.float32).astype(jnp.bfloat16)
    field_grad = jnp.where(live_rows[:, None, None], grad_grid[jnp.minimum(target, NLAT - 1)], 0).astype(jnp.bfloat16)
    return (field_grad, weight_grad)
```

```python
import functools
import math

import jax
import jax.numpy as jnp
import ml_dtypes
import numpy as np
from jax import lax
from jax.experimental import pallas as pl
from jax.experimental.pallas import tpu as pltpu
from jax.sharding import PartitionSpec as P

NLON = 720
L = 360
M = 360
LPAD = 384
ROWS = 6
GROUPS = 6
RESCALE = 2.0**40
RESCALE_LOG = 40.0 * math.log(2.0)
BF16 = jnp.bfloat16
F32 = jnp.float32
VMEM_BYTES = 56 * 1024 * 1024


def fourier_rows(lat_count):
    orders = np.arange(GROUPS * lat_count)
    turns = orders[:, None] * np.arange(NLON)[None, :] % NLON
    angles = turns * (2.0 * math.pi / NLON)
    live = (orders < M)[:, None] / math.sqrt(NLON)
    parts = np.stack([np.cos(angles) * live, -np.sin(angles) * live], axis=0)
    parts = parts.reshape(2, GROUPS, lat_count, NLON).transpose(1, 0, 2, 3)
    return parts.reshape(2 * GROUPS * lat_count, NLON).astype(ml_dtypes.bfloat16)


def order_norms(lat_count):
    orders = np.arange(8)[None, :] * lat_count + np.arange(lat_count)[:, None]
    logs = [
        0.5 * math.log((2.0 * m + 1.0) / (4.0 * math.pi))
        + 0.5 * math.lgamma(2.0 * m + 1.0)
        - m * math.log(2.0)
        - math.lgamma(m + 1.0)
        for m in orders.reshape(-1).tolist()
    ]
    latitudes = ROWS * lat_count
    total = np.array(logs).reshape(orders.shape) + 0.5 * math.log(2.0 * math.pi**2 / latitudes)
    return total.astype(np.float32)


def latitude_rows(lat_count):
    order = np.arange(lat_count)[None, :] * ROWS + np.arange(ROWS)[:, None]
    theta = (order.reshape(1, -1) + 0.5) * (math.pi / (ROWS * lat_count))
    return np.cos(theta).astype(np.float32), np.log(np.sin(theta)).astype(np.float32)


def whole(count):
    return [pl.BlockSpec(memory_space=pltpu.VMEM)] * count


def params():
    return pltpu.CompilerParams(vmem_limit_bytes=VMEM_BYTES)


def legendre_kernel(cosine_ref, logsine_ref, order_ref, norm_ref, slot_ref, out_ref, rows_ref):
    order = order_ref[...]
    square = order * order
    tiles = cosine_ref.shape[1] // 128
    cosines, scales = [], []
    for t in range(tiles):
        lanes = slice(128 * t, 128 * (t + 1))
        cosines.append(jnp.broadcast_to(cosine_ref[:, lanes], order.shape))
        logsine = jnp.broadcast_to(logsine_ref[:, lanes], order.shape)
        scales.append(norm_ref[...] + order * logsine + 0.5 * logsine)
    zero = jnp.zeros(order.shape, F32)
    one = jnp.ones(order.shape, F32)

    def advance(l, carry):
        degree = l.astype(F32)
        below = degree - 1.0
        upper = jnp.sqrt(
            jnp.maximum(4.0 * degree * degree - 1.0, 1.0)
            / jnp.maximum(degree * degree - square, 1.0)
        )
        lower = jnp.sqrt(
            jnp.maximum(below * below - square, 0.0)
            / jnp.maximum(4.0 * below * below - 1.0, 1.0)
        )
        rising = degree > order
        reached = degree >= order
        fresh = []
        for t in range(tiles):
            previous, current, scale = carry[3 * t : 3 * t + 3]
            value = upper * (cosines[t] * current - lower * previous)
            previous = jnp.where(rising, current, previous)
            current = jnp.where(rising, value, current)
            too_large = jnp.abs(current) > RESCALE
            factor = jnp.where(too_large, 1.0 / RESCALE, 1.0)
            previous = previous * factor
            current = current * factor
            scale = scale + jnp.where(too_large, RESCALE_LOG, 0.0)
            rows_ref[l, :, 128 * t : 128 * (t + 1)] = jnp.where(
                reached, current * jnp.exp(scale), 0.0
            )
            fresh += [previous, current, scale]
        return tuple(fresh)

    start = []
    for t in range(tiles):
        start += [zero, one, scales[t]]
    lax.fori_loop(0, L, advance, tuple(start), unroll=4)
    rows_ref[L:, :, :] = jnp.zeros((LPAD - L,) + rows_ref.shape[1:], F32)
    slots = slot_ref.shape[0]
    degrees = lax.broadcasted_iota(jnp.int32, (slots, LPAD), 1)
    pick = jnp.where((degrees == slot_ref[...]) & (degrees < L), 1.0, 0.0).astype(BF16)
    for j in range(GROUPS):
        table = rows_ref[:, j, :].astype(BF16)
        out_ref[j] = jnp.dot(pick, table, preferred_element_type=F32).astype(BF16)


def legendre_slots(rank, lat_count, slot_degree):
    slots = slot_degree.shape[0]
    latitudes = ROWS * lat_count
    cosine, logsine = latitude_rows(lat_count)
    norms = lax.dynamic_slice_in_dim(jnp.asarray(order_norms(lat_count)), rank, 1)
    order = (rank + lat_count * jnp.arange(8, dtype=jnp.int32)).astype(F32)
    return pl.pallas_call(
        legendre_kernel,
        out_shape=jax.ShapeDtypeStruct((GROUPS, slots, latitudes), BF16),
        in_specs=whole(5),
        out_specs=whole(1)[0],
        scratch_shapes=[pltpu.VMEM((LPAD, 8, latitudes), F32)],
        compiler_params=params(),
        name="legendre",
    )(
        jnp.asarray(cosine),
        jnp.asarray(logsine),
        jnp.broadcast_to(order[:, None], (8, 128)),
        jnp.broadcast_to(norms.reshape(8, 1), (8, 128)),
        slot_degree[:, None],
    )


def analysis_kernel(
    first_ref, rank_ref, field_ref, cotan_ref, field_in_ref, cotan_in_ref, fourier_ref,
    out_ref, rows_ref,
):
    narrow = field_ref.shape[1]
    lat_count = out_ref.shape[0]
    span = 2 * narrow
    first = first_ref[0]
    odd = rank_ref[0] % 2
    for k in range(ROWS):
        own = k + odd * (ROWS - first)
        mine = (own >= 0) & ((odd == 1) | (k < first))
        theirs = jnp.where(odd == 1, k, k - first)
        for w, (here, there) in enumerate(((field_ref, field_in_ref), (cotan_ref, cotan_in_ref))):
            at = slice((2 * k + w) * narrow, (2 * k + w + 1) * narrow)

            @pl.when(mine)
            def _():
                rows_ref[at, :] = here[jnp.clip(own, 0, 2 * ROWS - 1)]

            @pl.when(jnp.logical_not(mine))
            def _():
                rows_ref[at, :] = there[jnp.clip(theirs, 0, ROWS - 1)]

    rows = rows_ref[...]
    lane = lax.broadcasted_iota(jnp.int32, (2 * lat_count, 2 * ROWS * narrow), 1)
    line = lax.broadcasted_iota(jnp.int32, (2 * lat_count, 2 * ROWS * narrow), 0)
    cotangent = (lane // narrow) % 2 == 1
    for j in range(GROUPS):
        modes = lax.dot_general(
            fourier_ref[2 * lat_count * j : 2 * lat_count * (j + 1), :],
            rows,
            (((1,), (1,)), ((), ())),
            preferred_element_type=F32,
        )
        doubled = cotangent if j > 0 else cotangent & (line % lat_count > 0)
        modes = jnp.where(doubled, 2.0 * modes, modes).astype(BF16)
        for k in range(ROWS):
            slab = jnp.concatenate(
                [
                    modes[p * lat_count : (p + 1) * lat_count, k * span : (k + 1) * span]
                    for p in range(2)
                ],
                axis=1,
            )
            out_ref[:, (j * ROWS + k) * 2 * span : (j * ROWS + k + 1) * 2 * span] = slab


def forward_kernel(modes_ref, legendre_ref, out_ref):
    width = modes_ref.shape[1] // (GROUPS * ROWS)
    for j in range(GROUPS):
        slab = jnp.concatenate(
            [
                modes_ref[:, (j * ROWS + k) * width : (j * ROWS + k + 1) * width]
                for k in range(ROWS)
            ],
            axis=0,
        )
        out_ref[:, j * width : (j + 1) * width] = jnp.dot(
            legendre_ref[j], slab, preferred_element_type=F32
        ).astype(BF16)


def degree_kernel(coeffs_ref, weights_ref, grad_ref, back_ref):
    chans, lat_count = coeffs_ref.shape[1:3]
    narrow = coeffs_ref.shape[3] // (4 * GROUPS)
    sides = [[], []]
    for jp in range(2 * GROUPS):
        for w in range(2):
            at = (2 * jp + w) * narrow
            sides[w].append(
                jnp.concatenate(
                    [coeffs_ref[0, y, :, at : at + narrow] for y in range(chans)], axis=1
                )
            )
    coeffs = jnp.concatenate(sides[0], axis=0)
    dcoeffs = jnp.concatenate(sides[1], axis=0)
    grad_ref[0] = lax.dot_general(
        coeffs, dcoeffs, (((0,), (0,)), ((), ())), preferred_element_type=F32
    )
    back = lax.dot_general(
        dcoeffs, weights_ref[0], (((1,), (1,)), ((), ())), preferred_element_type=F32
    ).astype(BF16)
    for y in range(chans):
        back_ref[0, y] = jnp.concatenate(
            [
                back[jp * lat_count : (jp + 1) * lat_count, y * narrow : (y + 1) * narrow]
                for jp in range(2 * GROUPS)
            ],
            axis=1,
        )


def backward_kernel(back_ref, legendre_ref, out_ref):
    lat_count = out_ref.shape[0]
    span = back_ref.shape[1] // GROUPS
    narrow = span // 2
    for j in range(GROUPS):
        modes = lax.dot_general(
            legendre_ref[j],
            back_ref[:, j * span : (j + 1) * span],
            (((0,), (0,)), ((), ())),
            preferred_element_type=F32,
        ).astype(BF16)
        for p in range(2):
            out_ref[:, (2 * j + p) * ROWS * narrow : (2 * j + p + 1) * ROWS * narrow] = (
                jnp.concatenate(
                    [
                        modes[k * lat_count : (k + 1) * lat_count, p * narrow : (p + 1) * narrow]
                        for k in range(ROWS)
                    ],
                    axis=1,
                )
            )


def synthesis_kernel(modes_ref, fourier_ref, out_ref):
    narrow = out_ref.shape[1]
    width = ROWS * narrow
    modes = jnp.concatenate(
        [modes_ref[:, jp * width : (jp + 1) * width] for jp in range(2 * GROUPS)], axis=0
    )
    grad = lax.dot_general(
        modes, fourier_ref[...], (((0,), (0,)), ((), ())), preferred_element_type=F32
    ).astype(BF16)
    for k in range(ROWS):
        out_ref[k] = grad[k * narrow : (k + 1) * narrow, :]


def placing_kernel(first_ref, rank_ref, mine_ref, theirs_ref, out_ref):
    odd = rank_ref[0] % 2
    first = first_ref[0]
    start = odd * first
    count = jnp.where(odd == 1, 2 * ROWS - first, first)
    for r in range(2 * ROWS):
        at = start + r
        live = r < count
        own = (at // ROWS) == odd

        @pl.when(live & own)
        def _():
            out_ref[r] = mine_ref[jnp.clip(at - odd * ROWS, 0, ROWS - 1)]

        @pl.when(live & jnp.logical_not(own))
        def _():
            out_ref[r] = theirs_ref[jnp.clip(at - (1 - odd) * ROWS, 0, ROWS - 1)]

        @pl.when(jnp.logical_not(live))
        def _():
            out_ref[r] = jnp.zeros_like(out_ref[r])


def on_device(field_in, cotangent, weights, row_counts, slot_degree):
    lat_count = lax.axis_size("lat")
    chan_count = lax.axis_size("chan")
    rank = lax.axis_index("lat")
    narrow = field_in.shape[1]
    slots = slot_degree.shape[0]
    pairs = [(i, i ^ 1) for i in range(lat_count)]
    odd = rank % 2
    first = lax.dynamic_slice_in_dim(row_counts, rank - odd, 1)
    at_rank = jnp.reshape(rank, (1,)).astype(jnp.int32)
    fourier = jnp.asarray(fourier_rows(lat_count))
    scalar = pl.BlockSpec(memory_space=pltpu.SMEM)

    field_swap = lax.ppermute(
        lax.dynamic_slice_in_dim(field_in, (1 - odd) * ROWS, ROWS), "lat", pairs
    )
    cotan_swap = lax.ppermute(
        lax.dynamic_slice_in_dim(cotangent, (1 - odd) * ROWS, ROWS), "lat", pairs
    )
    modes = pl.pallas_call(
        analysis_kernel,
        out_shape=jax.ShapeDtypeStruct((lat_count, 4 * GROUPS * ROWS * narrow), BF16),
        in_specs=[scalar, scalar] + whole(5),
        out_specs=whole(1)[0],
        scratch_shapes=[pltpu.VMEM((2 * ROWS * narrow, NLON), BF16)],
        compiler_params=params(),
        name="analysis",
    )(first, at_rank, field_in, cotangent, field_swap, cotan_swap, fourier)
    modes = lax.all_to_all(
        modes.reshape(lat_count, 2, -1), "lat", split_axis=0, concat_axis=0, tiled=True
    ).reshape(lat_count, -1)
    legendre = legendre_slots(rank, lat_count, slot_degree)
    coeffs = pl.pallas_call(
        forward_kernel,
        out_shape=jax.ShapeDtypeStruct((slots, 4 * GROUPS * narrow), BF16),
        in_specs=whole(2),
        out_specs=whole(1)[0],
        compiler_params=params(),
        name="forward",
    )(modes, legendre)
    held = weights.shape[0]
    devices = lat_count * chan_count
    coeffs = lax.all_to_all(
        coeffs.reshape(devices, held, -1), ("lat", "chan"), split_axis=0, concat_axis=0, tiled=True
    )
    coeffs = coeffs.reshape(lat_count, chan_count, held, -1).transpose(2, 1, 0, 3)
    width = weights.shape[1]
    weight_grad, back = pl.pallas_call(
        degree_kernel,
        grid=(held,),
        out_shape=(
            jax.ShapeDtypeStruct((held, width, width), F32),
            jax.ShapeDtypeStruct((held, chan_count, lat_count, 2 * GROUPS * narrow), BF16),
        ),
        in_specs=[
            pl.BlockSpec((1, chan_count, lat_count, 4 * GROUPS * narrow), lambda s: (s, 0, 0, 0)),
            pl.BlockSpec((1, width, width), lambda s: (s, 0, 0)),
        ],
        out_specs=(
            pl.BlockSpec((1, width, width), lambda s: (s, 0, 0)),
            pl.BlockSpec((1, chan_count, lat_count, 2 * GROUPS * narrow), lambda s: (s, 0, 0, 0)),
        ),
        compiler_params=params(),
        name="degree",
    )(coeffs, weights)
    back = back.transpose(2, 1, 0, 3).reshape(devices, held, -1)
    back = lax.all_to_all(back, ("lat", "chan"), split_axis=0, concat_axis=0, tiled=True)
    back = back.reshape(slots, -1)
    modes_back = pl.pallas_call(
        backward_kernel,
        out_shape=jax.ShapeDtypeStruct((lat_count, 2 * GROUPS * ROWS * narrow), BF16),
        in_specs=whole(2),
        out_specs=whole(1)[0],
        compiler_params=params(),
        name="backward",
    )(back, legendre)
    modes_back = lax.all_to_all(
        modes_back.reshape(lat_count, 2, -1), "lat", split_axis=0, concat_axis=0, tiled=True
    ).reshape(lat_count, -1)
    grad = pl.pallas_call(
        synthesis_kernel,
        out_shape=jax.ShapeDtypeStruct((ROWS, narrow, NLON), BF16),
        in_specs=whole(2),
        out_specs=whole(1)[0],
        compiler_params=params(),
        name="synthesis",
    )(modes_back, fourier)
    grad_swap = lax.ppermute(grad, "lat", pairs)
    field_grad = pl.pallas_call(
        placing_kernel,
        out_shape=jax.ShapeDtypeStruct(field_in.shape, BF16),
        in_specs=[scalar, scalar] + whole(2),
        out_specs=whole(1)[0],
        compiler_params=params(),
        name="placing",
    )(first, at_rank, grad, grad_swap)
    return field_grad, weight_grad


def solution(mesh):
    placed = (
        P("lat", "chan", None),
        P("lat", "chan", None),
        P(("lat", "chan"), None, None),
        P(),
        P(),
    )
    return jax.shard_map(
        on_device,
        mesh=mesh,
        in_specs=placed,
        out_specs=(P("lat", "chan", None), P(("lat", "chan"), None, None)),
        check_vma=False,
    )
```

```python
import functools
import math

import jax
import jax.numpy as jnp
import ml_dtypes
import numpy as np
from jax import lax
from jax.experimental import pallas as pl
from jax.experimental.pallas import tpu as pltpu
from jax.sharding import PartitionSpec as P

NLON = 720
L = 360
M = 360
LPAD = 384
ROWS = 6
GROUPS = 6
RESCALE = 2.0**40
RESCALE_LOG = 40.0 * math.log(2.0)
BF16 = jnp.bfloat16
F32 = jnp.float32
VMEM_BYTES = 56 * 1024 * 1024


def fourier_rows(lat_count):
    orders = np.arange(GROUPS * lat_count)
    turns = orders[:, None] * np.arange(NLON)[None, :] % NLON
    angles = turns * (2.0 * math.pi / NLON)
    live = (orders < M)[:, None] / math.sqrt(NLON)
    parts = np.stack([np.cos(angles) * live, -np.sin(angles) * live], axis=0)
    parts = parts.reshape(2, GROUPS, lat_count, NLON).transpose(1, 0, 2, 3)
    return parts.astype(ml_dtypes.bfloat16)


def order_norms(lat_count):
    orders = np.arange(8)[None, :] * lat_count + np.arange(lat_count)[:, None]
    logs = [
        0.5 * math.log((2.0 * m + 1.0) / (4.0 * math.pi))
        + 0.5 * math.lgamma(2.0 * m + 1.0)
        - m * math.log(2.0)
        - math.lgamma(m + 1.0)
        for m in orders.reshape(-1).tolist()
    ]
    latitudes = ROWS * lat_count
    total = np.array(logs).reshape(orders.shape) + 0.5 * math.log(2.0 * math.pi**2 / latitudes)
    return np.broadcast_to(total[:, :, None], total.shape + (128,)).astype(np.float32)


def latitude_rows(lat_count):
    grid = np.arange(lat_count)[None, :] * ROWS + np.arange(ROWS)[:, None]
    paired = grid.reshape(ROWS // 2, 2, lat_count).transpose(0, 2, 1)
    order = np.concatenate([grid.reshape(-1), paired.reshape(-1)])[None, :]
    theta = (order + 0.5) * (math.pi / (ROWS * lat_count))
    return np.cos(theta).astype(np.float32), np.log(np.sin(theta)).astype(np.float32)


def params():
    return pltpu.CompilerParams(vmem_limit_bytes=VMEM_BYTES)


def legendre_kernel(
    rank_ref, cosine_ref, logsine_ref, norm_ref, slot_ref, rows_out_ref, pairs_out_ref, rows_ref
):
    rank = rank_ref[0]
    lat_count = norm_ref.shape[0]
    latitudes = rows_out_ref.shape[2]
    shape = (8, 128)
    groups = lax.broadcasted_iota(jnp.int32, shape, 0)
    order = (rank + groups * lat_count).astype(F32)
    square = order * order
    tiles = cosine_ref.shape[1] // 128
    cosines, scales = [], []
    for t in range(tiles):
        lanes = slice(128 * t, 128 * (t + 1))
        cosines.append(jnp.broadcast_to(cosine_ref[:, lanes], shape))
        logsine = jnp.broadcast_to(logsine_ref[:, lanes], shape)
        scales.append(norm_ref[rank] + order * logsine + 0.5 * logsine)
    zero = jnp.zeros(shape, F32)
    one = jnp.ones(shape, F32)

    def advance(l, carry):
        degree = l.astype(F32)
        below = degree - 1.0
        upper = jnp.sqrt(
            jnp.maximum(4.0 * degree * degree - 1.0, 1.0)
            / jnp.maximum(degree * degree - square, 1.0)
        )
        lower = jnp.sqrt(
            jnp.maximum(below * below - square, 0.0)
            / jnp.maximum(4.0 * below * below - 1.0, 1.0)
        )
        rising = degree > order
        reached = degree >= order
        fresh = []
        for t in range(tiles):
            previous, current, scale = carry[3 * t : 3 * t + 3]
            value = upper * (cosines[t] * current - lower * previous)
            previous = jnp.where(rising, current, previous)
            current = jnp.where(rising, value, current)
            too_large = jnp.abs(current) > RESCALE
            factor = jnp.where(too_large, 1.0 / RESCALE, 1.0)
            previous = previous * factor
            current = current * factor
            scale = scale + jnp.where(too_large, RESCALE_LOG, 0.0)
            rows_ref[l, :, 128 * t : 128 * (t + 1)] = jnp.where(
                reached, current * jnp.exp(scale), 0.0
            )
            fresh += [previous, current, scale]
        return tuple(fresh)

    start = []
    for t in range(tiles):
        start += [zero, one, scales[t]]
    lax.fori_loop(0, L, advance, tuple(start), unroll=4)
    rows_ref[L:, :, :] = jnp.zeros((LPAD - L,) + rows_ref.shape[1:], F32)
    slots = slot_ref.shape[0]
    degrees = lax.broadcasted_iota(jnp.int32, (slots, LPAD), 1)
    pick = jnp.where((degrees == slot_ref[...]) & (degrees < L), 1.0, 0.0).astype(BF16)
    for j in range(GROUPS):
        for half, out_ref in enumerate((rows_out_ref, pairs_out_ref)):
            table = rows_ref[:, j, half * latitudes : (half + 1) * latitudes].astype(BF16)
            out_ref[j] = jnp.dot(pick, table, preferred_element_type=F32).astype(BF16)


def legendre_slots(at_rank, lat_count, slot_rows):
    slots = slot_rows.shape[0]
    latitudes = ROWS * lat_count
    cosine, logsine = latitude_rows(lat_count)
    vmem = pl.BlockSpec(memory_space=pltpu.VMEM)
    table = jax.ShapeDtypeStruct((GROUPS, slots, latitudes), BF16)
    return pl.pallas_call(
        legendre_kernel,
        out_shape=(table, table),
        in_specs=[pl.BlockSpec(memory_space=pltpu.SMEM)] + [vmem] * 4,
        out_specs=(vmem, vmem),
        scratch_shapes=[pltpu.VMEM((LPAD, 8, 2 * latitudes), F32)],
        compiler_params=params(),
        name="legendre",
    )(
        at_rank,
        jnp.asarray(cosine),
        jnp.asarray(logsine),
        jnp.asarray(order_norms(lat_count)),
        slot_rows[:, None],
    )


def analysis_kernel(
    counts_ref, rank_ref, field_ref, cotan_ref, field_in_ref, cotan_in_ref, fourier_ref,
    out_ref, rows_ref, sems,
):
    narrow = field_ref.shape[1]
    lat_count = out_ref.shape[0]
    width = 2 * ROWS * narrow

    @pl.when(pl.program_id(0) == 0)
    def _():
        rank = rank_ref[0]
        odd = rank % 2
        first = counts_ref[rank - odd]
        copies = []
        for k in range(ROWS):
            own = k + odd * (ROWS - first)
            mine = (own >= 0) & ((odd == 1) | (k < first))
            theirs = jnp.where(odd == 1, k, k - first)
            for w, (here, there) in enumerate(
                ((field_ref, field_in_ref), (cotan_ref, cotan_in_ref))
            ):
                target = rows_ref.at[pl.ds((2 * k + w) * narrow, narrow), :]
                sem = sems.at[2 * k + w]
                near = pltpu.make_async_copy(here.at[jnp.clip(own, 0, 2 * ROWS - 1)], target, sem)
                far = pltpu.make_async_copy(there.at[jnp.clip(theirs, 0, ROWS - 1)], target, sem)
                pl.when(mine)(near.start)
                pl.when(jnp.logical_not(mine))(far.start)
                copies.append(near)
        for copy in copies:
            copy.wait()

    modes = lax.dot_general(
        fourier_ref[...], rows_ref[...], (((1,), (1,)), ((), ())), preferred_element_type=F32
    ).astype(BF16)
    for j in range(modes.shape[0] // (2 * lat_count)):
        out_ref[:, :, j * width : (j + 1) * width] = modes[
            2 * lat_count * j : 2 * lat_count * (j + 1)
        ].reshape(lat_count, 2, width)


def forward_kernel(rank_ref, modes_ref, legendre_ref, out_ref):
    groups = legendre_ref.shape[0]
    lat_count = modes_ref.shape[1]
    width = modes_ref.shape[2] // (groups * ROWS)
    narrow = width // 2
    owners = out_ref.shape[0]
    step = pl.program_id(0)
    for w in range(2):
        for j in range(groups):
            slab = jnp.concatenate(
                [
                    jnp.concatenate(
                        [
                            modes_ref[
                                p,
                                :,
                                (j * ROWS + k) * width + w * narrow : (j * ROWS + k) * width
                                + (w + 1) * narrow,
                            ]
                            for p in range(2)
                        ],
                        axis=1,
                    )
                    for k in range(ROWS)
                ],
                axis=0,
            )
            coeffs = jnp.dot(legendre_ref[j], slab, preferred_element_type=F32)
            if w == 1:
                zonal = (rank_ref[0] == 0) & (step == 0) & (j == 0)
                coeffs = coeffs * jnp.where(zonal, 1.0, 2.0)
            at = (w * groups + j) * width
            out_ref[:, :, at : at + width] = coeffs.astype(BF16).reshape(owners, 2, width)


def side(coeffs_ref, w, steps, groups, narrow):
    chans = coeffs_ref.shape[1]
    rows = []
    for i in range(steps):
        for j in range(groups):
            for p in range(2):
                at = (((i * 2 + w) * groups + j) * 2 + p) * narrow
                rows.append(
                    jnp.concatenate(
                        [coeffs_ref[0, y, :, at : at + narrow] for y in range(chans)], axis=1
                    )
                )
    return jnp.concatenate(rows, axis=0)


def degree_kernel(steps, coeffs_ref, weights_ref, back_ref):
    chans, lat_count = coeffs_ref.shape[1:3]
    narrow = coeffs_ref.shape[3] // (4 * GROUPS)
    dcoeffs = side(coeffs_ref, 1, steps, GROUPS // steps, narrow)
    back = lax.dot_general(
        dcoeffs, weights_ref[0], (((1,), (1,)), ((), ())), preferred_element_type=F32
    ).astype(BF16)
    messages = [
        jnp.concatenate(
            [
                back[jp * lat_count : (jp + 1) * lat_count, y * narrow : (y + 1) * narrow]
                for jp in range(2 * GROUPS)
            ],
            axis=1,
        )
        for y in range(chans)
    ]
    for s in range(2):

        @pl.when(pl.program_id(0) == s)
        def _():
            for y in range(chans):
                back_ref[y * lat_count : (y + 1) * lat_count, s, :] = messages[y]


def gradient_kernel(steps, coeffs_ref, grad_ref):
    narrow = coeffs_ref.shape[3] // (4 * GROUPS)
    coeffs = side(coeffs_ref, 0, steps, GROUPS // steps, narrow)
    dcoeffs = side(coeffs_ref, 1, steps, GROUPS // steps, narrow)
    grad_ref[0] = lax.dot_general(
        coeffs, dcoeffs, (((0,), (0,)), ((), ())), preferred_element_type=F32
    )


def backward_kernel(back_ref, legendre_ref, out_ref):
    groups = legendre_ref.shape[0]
    slots = legendre_ref.shape[1]
    lat_count = out_ref.shape[0]
    span = back_ref.shape[2] // groups
    half = ROWS // 2
    for j in range(groups):
        held = back_ref[:, :, j * span : (j + 1) * span].reshape(slots, span)
        modes = lax.dot_general(
            legendre_ref[j], held, (((0,), (0,)), ((), ())), preferred_element_type=F32
        ).astype(BF16)
        for k in range(half):
            out_ref[:, :, (j * half + k) * span : (j * half + k + 1) * span] = modes[
                2 * lat_count * k : 2 * lat_count * (k + 1)
            ].reshape(lat_count, 2, span)


def synthesis_kernel(modes_ref, fourier_ref, out_ref):
    narrow = out_ref.shape[1]
    half = ROWS // 2
    modes = jnp.concatenate(
        [
            jnp.concatenate(
                [
                    modes_ref[k % 2, :, at : at + narrow]
                    for k in range(ROWS)
                    for at in [((j * half + k // 2) * 2 + p) * narrow]
                ],
                axis=1,
            )
            for j in range(GROUPS)
            for p in range(2)
        ],
        axis=0,
    )
    grad = lax.dot_general(
        modes, fourier_ref[...], (((0,), (0,)), ((), ())), preferred_element_type=F32
    ).astype(BF16)
    for k in range(ROWS):
        out_ref[k] = grad[k * narrow : (k + 1) * narrow, :]


def placing_kernel(counts_ref, rank_ref, mine_ref, theirs_ref, out_ref, empty_ref, sems):
    rank = rank_ref[0]
    odd = rank % 2
    first = counts_ref[rank - odd]
    start = odd * first
    count = jnp.where(odd == 1, 2 * ROWS - first, first)
    empty_ref[...] = jnp.zeros_like(empty_ref)
    copies = []
    for r in range(2 * ROWS):
        at = start + r
        live = r < count
        own = (at // ROWS) == odd
        target, sem = out_ref.at[r], sems.at[r]
        near = pltpu.make_async_copy(
            mine_ref.at[jnp.clip(at - odd * ROWS, 0, ROWS - 1)], target, sem
        )
        far = pltpu.make_async_copy(
            theirs_ref.at[jnp.clip(at - (1 - odd) * ROWS, 0, ROWS - 1)], target, sem
        )
        dead = pltpu.make_async_copy(empty_ref, target, sem)
        pl.when(live & own)(near.start)
        pl.when(live & jnp.logical_not(own))(far.start)
        pl.when(jnp.logical_not(live))(dead.start)
        copies.append(near)
    for copy in copies:
        copy.wait()


def on_device(field_in, cotangent, weights, row_counts, slot_degree):
    lat_count = lax.axis_size("lat")
    chan_count = lax.axis_size("chan")
    rank = lax.axis_index("lat")
    narrow = field_in.shape[1]
    slots = slot_degree.shape[0]
    held = weights.shape[0]
    devices = lat_count * chan_count
    latitudes = ROWS * lat_count
    pairs = [(i, i ^ 1) for i in range(lat_count)]
    odd = rank % 2
    at_rank = jnp.reshape(rank, (1,)).astype(jnp.int32)
    table = fourier_rows(lat_count)
    by_part = jnp.asarray(table.reshape(-1, NLON))
    by_rank = jnp.asarray(table.transpose(0, 2, 1, 3).reshape(-1, NLON))
    scalar = pl.BlockSpec(memory_space=pltpu.SMEM)
    vmem = pl.BlockSpec(memory_space=pltpu.VMEM)
    hbm = pl.BlockSpec(memory_space=pl.ANY)
    step = 2
    steps = GROUPS // step
    everyone = ("chan", "lat")

    field_swap = lax.ppermute(
        lax.dynamic_slice_in_dim(field_in, (1 - odd) * ROWS, ROWS), "lat", pairs
    )
    cotan_swap = lax.ppermute(
        lax.dynamic_slice_in_dim(cotangent, (1 - odd) * ROWS, ROWS), "lat", pairs
    )
    width = 2 * ROWS * narrow
    modes = pl.pallas_call(
        analysis_kernel,
        grid=(steps,),
        out_shape=jax.ShapeDtypeStruct((lat_count, 2, GROUPS * width), BF16),
        in_specs=[scalar, scalar, hbm, hbm, hbm, hbm]
        + [pl.BlockSpec((2 * step * lat_count, NLON), lambda i: (i, 0))],
        out_specs=pl.BlockSpec((lat_count, 2, step * width), lambda i: (0, 0, i)),
        scratch_shapes=[
            pltpu.VMEM((width, NLON), BF16),
            pltpu.SemaphoreType.DMA((2 * ROWS,)),
        ],
        compiler_params=params(),
        name="analysis",
    )(row_counts, at_rank, field_in, cotangent, field_swap, cotan_swap, by_rank)
    modes = lax.all_to_all(modes, "lat", split_axis=0, concat_axis=0, tiled=True)
    modes = modes.transpose(1, 0, 2)
    slot_rows = slot_degree.reshape(lat_count, chan_count, held).transpose(1, 0, 2).reshape(-1)
    legendre, legendre_pairs = legendre_slots(at_rank, lat_count, slot_rows)
    coeffs = pl.pallas_call(
        forward_kernel,
        grid=(steps,),
        out_shape=jax.ShapeDtypeStruct((devices, held, 4 * GROUPS * narrow), BF16),
        in_specs=[
            scalar,
            pl.BlockSpec((2, lat_count, step * width), lambda i: (0, 0, i)),
            pl.BlockSpec((step, slots, latitudes), lambda i: (i, 0, 0)),
        ],
        out_specs=pl.BlockSpec((devices, held, step * 4 * narrow), lambda i: (0, 0, i)),
        compiler_params=params(),
        name="forward",
    )(at_rank, modes, legendre)
    coeffs = lax.all_to_all(coeffs, everyone, split_axis=0, concat_axis=0, tiled=True)
    coeffs = coeffs.transpose(1, 0, 2).reshape(held, chan_count, lat_count, 4 * GROUPS * narrow)
    full = weights.shape[1]
    slot_block = pl.BlockSpec(
        (1, chan_count, lat_count, 4 * GROUPS * narrow), lambda s: (s, 0, 0, 0)
    )
    back = pl.pallas_call(
        functools.partial(degree_kernel, steps),
        grid=(held,),
        out_shape=jax.ShapeDtypeStruct((devices, held, 2 * GROUPS * narrow), BF16),
        in_specs=[slot_block, pl.BlockSpec((1, full, full), lambda s: (s, 0, 0))],
        out_specs=pl.BlockSpec((devices, held, 2 * GROUPS * narrow), lambda s: (0, 0, 0)),
        compiler_params=params(),
        name="degree",
    )(coeffs, weights)
    back = lax.all_to_all(back, everyone, split_axis=0, concat_axis=0, tiled=True)
    weight_grad = pl.pallas_call(
        functools.partial(gradient_kernel, steps),
        grid=(held,),
        out_shape=jax.ShapeDtypeStruct((held, full, full), F32),
        in_specs=[slot_block],
        out_specs=pl.BlockSpec((1, full, full), lambda s: (s, 0, 0)),
        compiler_params=params(),
        name="gradient",
    )(coeffs)
    modes_back = pl.pallas_call(
        backward_kernel,
        grid=(steps,),
        out_shape=jax.ShapeDtypeStruct((lat_count, 2, GROUPS * ROWS * narrow), BF16),
        in_specs=[
            pl.BlockSpec((devices, held, step * 2 * narrow), lambda i: (0, 0, i)),
            pl.BlockSpec((step, slots, latitudes), lambda i: (i, 0, 0)),
        ],
        out_specs=pl.BlockSpec((lat_count, 2, step * ROWS * narrow), lambda i: (0, 0, i)),
        compiler_params=params(),
        name="backward",
    )(back, legendre_pairs)
    modes_back = lax.all_to_all(modes_back, "lat", split_axis=0, concat_axis=0, tiled=True)
    grad = pl.pallas_call(
        synthesis_kernel,
        out_shape=jax.ShapeDtypeStruct((ROWS, narrow, NLON), BF16),
        in_specs=[vmem, vmem],
        out_specs=vmem,
        compiler_params=params(),
        name="synthesis",
    )(modes_back.transpose(1, 0, 2), by_part)
    grad_swap = lax.ppermute(grad, "lat", pairs)
    field_grad = pl.pallas_call(
        placing_kernel,
        out_shape=jax.ShapeDtypeStruct(field_in.shape, BF16),
        in_specs=[scalar, scalar, hbm, hbm],
        out_specs=hbm,
        scratch_shapes=[
            pltpu.VMEM((narrow, NLON), BF16),
            pltpu.SemaphoreType.DMA((2 * ROWS,)),
        ],
        compiler_params=params(),
        name="placing",
    )(row_counts, at_rank, grad, grad_swap)
    return field_grad, weight_grad


def solution(mesh):
    placed = (
        P("lat", "chan", None),
        P("lat", "chan", None),
        P(("lat", "chan"), None, None),
        P(),
        P(),
    )
    return jax.shard_map(
        on_device,
        mesh=mesh,
        in_specs=placed,
        out_specs=(P("lat", "chan", None), P(("lat", "chan"), None, None)),
        check_vma=False,
    )
```

```python
import math

import jax
import jax.numpy as jnp
import ml_dtypes
import numpy as np
from jax import lax
from jax.experimental import pallas as pl
from jax.experimental.pallas import tpu as pltpu
from jax.sharding import PartitionSpec as P

NLON = 720
L = 360
M = 360
LPAD = 384
ROWS = 6
GROUPS = 6
RESCALE = 2.0**40
RESCALE_LOG = 40.0 * math.log(2.0)
BF16 = jnp.bfloat16
F32 = jnp.float32
VMEM_BYTES = 30 * 1024 * 1024


def fourier_rows(lat_count):
    orders = np.arange(GROUPS * lat_count)
    turns = orders[:, None] * np.arange(NLON)[None, :] % NLON
    angles = turns * (2.0 * math.pi / NLON)
    live = (orders < M)[:, None] / math.sqrt(NLON)
    parts = np.stack([np.cos(angles) * live, -np.sin(angles) * live], axis=0)
    parts = parts.reshape(2, GROUPS, lat_count, NLON).transpose(1, 0, 2, 3)
    return parts.astype(ml_dtypes.bfloat16)


def order_norms(lat_count):
    orders = np.arange(8)[None, :] * lat_count + np.arange(lat_count)[:, None]
    logs = [
        0.5 * math.log((2.0 * m + 1.0) / (4.0 * math.pi))
        + 0.5 * math.lgamma(2.0 * m + 1.0)
        - m * math.log(2.0)
        - math.lgamma(m + 1.0)
        for m in orders.reshape(-1).tolist()
    ]
    latitudes = ROWS * lat_count
    total = np.array(logs).reshape(orders.shape) + 0.5 * math.log(2.0 * math.pi**2 / latitudes)
    return np.broadcast_to(total[:, :, None], total.shape + (128,)).astype(np.float32)


def latitude_rows(lat_count):
    grid = np.arange(lat_count)[None, :] * ROWS + np.arange(ROWS)[:, None]
    paired = grid.reshape(ROWS // 2, 2, lat_count).transpose(0, 2, 1)
    order = np.concatenate([grid.reshape(-1), paired.reshape(-1)])[None, :]
    theta = (order + 0.5) * (math.pi / (ROWS * lat_count))
    return np.cos(theta).astype(np.float32), np.log(np.sin(theta)).astype(np.float32)


def run(kernel, name, outs, args, scratch=(), home=pltpu.VMEM):
    vmem = pl.BlockSpec(memory_space=pltpu.VMEM)
    scalar = pl.BlockSpec(memory_space=pltpu.SMEM)
    specs, operands = [], []
    for arg in args:
        small = arg.dtype == jnp.int32 and arg.ndim == 1
        specs.append(scalar if small else vmem)
        operands.append(arg if small else pltpu.with_memory_space_constraint(arg, pltpu.VMEM))
    results = pl.pallas_call(
        kernel,
        out_shape=tuple(outs),
        in_specs=specs,
        out_specs=tuple(pl.BlockSpec(memory_space=home) for _ in outs),
        scratch_shapes=list(scratch),
        compiler_params=pltpu.CompilerParams(vmem_limit_bytes=VMEM_BYTES),
        name=name,
    )(*operands)
    return results if len(outs) > 1 else results[0]


def legendre_kernel(
    rank_ref, cosine_ref, logsine_ref, norm_ref, slot_ref, rows_out_ref, pairs_out_ref, rows_ref
):
    rank = rank_ref[0]
    lat_count = norm_ref.shape[0]
    latitudes = rows_out_ref.shape[2]
    shape = (8, 128)
    groups = lax.broadcasted_iota(jnp.int32, shape, 0)
    order = (rank + groups * lat_count).astype(F32)
    square = order * order
    tiles = cosine_ref.shape[1] // 128
    cosines, scales = [], []
    for t in range(tiles):
        lanes = slice(128 * t, 128 * (t + 1))
        cosines.append(jnp.broadcast_to(cosine_ref[:, lanes], shape))
        logsine = jnp.broadcast_to(logsine_ref[:, lanes], shape)
        scales.append(norm_ref[rank] + order * logsine + 0.5 * logsine)
    zero = jnp.zeros(shape, F32)
    one = jnp.ones(shape, F32)

    def advance(l, carry):
        degree = l.astype(F32)
        below = degree - 1.0
        upper = jnp.sqrt(
            jnp.maximum(4.0 * degree * degree - 1.0, 1.0)
            / jnp.maximum(degree * degree - square, 1.0)
        )
        lower = jnp.sqrt(
            jnp.maximum(below * below - square, 0.0)
            / jnp.maximum(4.0 * below * below - 1.0, 1.0)
        )
        rising = degree > order
        reached = degree >= order
        fresh = []
        for t in range(tiles):
            previous, current, scale = carry[3 * t : 3 * t + 3]
            value = upper * (cosines[t] * current - lower * previous)
            previous = jnp.where(rising, current, previous)
            current = jnp.where(rising, value, current)
            too_large = jnp.abs(current) > RESCALE
            factor = jnp.where(too_large, 1.0 / RESCALE, 1.0)
            previous = previous * factor
            current = current * factor
            scale = scale + jnp.where(too_large, RESCALE_LOG, 0.0)
            rows_ref[l, :, 128 * t : 128 * (t + 1)] = jnp.where(
                reached, current * jnp.exp(scale), 0.0
            )
            fresh += [previous, current, scale]
        return tuple(fresh)

    start = []
    for t in range(tiles):
        start += [zero, one, scales[t]]
    lax.fori_loop(0, L, advance, tuple(start), unroll=4)
    rows_ref[L:, :, :] = jnp.zeros((LPAD - L,) + rows_ref.shape[1:], F32)
    slots = slot_ref.shape[0]
    degrees = lax.broadcasted_iota(jnp.int32, (slots, LPAD), 1)
    pick = jnp.where((degrees == slot_ref[...]) & (degrees < L), 1.0, 0.0).astype(BF16)
    for j in range(GROUPS):
        table = rows_ref[:, j, :latitudes].astype(BF16)
        rows_out_ref[j] = jnp.dot(pick, table, preferred_element_type=F32).astype(BF16)
        table = rows_ref[:, j, latitudes:].astype(BF16)
        pairs_out_ref[j] = lax.dot_general(
            table, pick, (((0,), (1,)), ((), ())), preferred_element_type=F32
        ).astype(BF16)


def legendre_slots(at_rank, lat_count, slot_rows):
    slots = slot_rows.shape[0]
    latitudes = ROWS * lat_count
    cosine, logsine = latitude_rows(lat_count)
    return run(
        legendre_kernel,
        "legendre",
        [pltpu.VMEM((GROUPS, slots, latitudes), BF16), pltpu.VMEM((GROUPS, latitudes, slots), BF16)],
        [
            at_rank,
            jnp.asarray(cosine),
            jnp.asarray(logsine),
            jnp.asarray(order_norms(lat_count)),
            slot_rows[:, None],
        ],
        [pltpu.VMEM((LPAD, 8, 2 * latitudes), F32)],
    )


def analysis_kernel(
    counts_ref, rank_ref, field_ref, cotan_ref, field_in_ref, cotan_in_ref, fourier_ref,
    out_ref, rows_ref,
):
    narrow = field_ref.shape[1]
    lat_count = out_ref.shape[0]
    width = 2 * ROWS * narrow
    rank = rank_ref[0]
    odd = rank % 2
    first = counts_ref[rank - odd]
    for k in range(ROWS):
        own = k + odd * (ROWS - first)
        mine = (own >= 0) & ((odd == 1) | (k < first))
        theirs = jnp.where(odd == 1, k, k - first)
        for w, (here, there) in enumerate(((field_ref, field_in_ref), (cotan_ref, cotan_in_ref))):
            at = slice((2 * k + w) * narrow, (2 * k + w + 1) * narrow)

            @pl.when(mine)
            def _():
                rows_ref[at, :] = here[jnp.clip(own, 0, 2 * ROWS - 1)]

            @pl.when(jnp.logical_not(mine))
            def _():
                rows_ref[at, :] = there[jnp.clip(theirs, 0, ROWS - 1)]

    modes = lax.dot_general(
        fourier_ref[...], rows_ref[...], (((1,), (1,)), ((), ())), preferred_element_type=F32
    ).astype(BF16)
    for j in range(GROUPS):
        out_ref[:, :, j * width : (j + 1) * width] = modes[
            2 * lat_count * j : 2 * lat_count * (j + 1)
        ].reshape(lat_count, 2, width)


def forward_kernel(rank_ref, modes_ref, legendre_ref, out_ref):
    width = modes_ref.shape[2] // (GROUPS * ROWS)
    owners = out_ref.shape[0]
    slots = legendre_ref.shape[1]
    lane = lax.broadcasted_iota(jnp.int32, (slots, 2 * width), 1)
    cotangent = lane // (width // 2) % 2 == 1
    for j in range(GROUPS):
        slab = jnp.concatenate(
            [
                jnp.concatenate(
                    [
                        modes_ref[p, :, (j * ROWS + k) * width : (j * ROWS + k + 1) * width]
                        for p in range(2)
                    ],
                    axis=1,
                )
                for k in range(ROWS)
            ],
            axis=0,
        )
        coeffs = jnp.dot(legendre_ref[j], slab, preferred_element_type=F32)
        doubled = jnp.where(rank_ref[0] + j == 0, 1.0, 2.0)
        coeffs = jnp.where(cotangent, coeffs * doubled, coeffs)
        out_ref[:, :, 2 * j * width : 2 * (j + 1) * width] = coeffs.astype(BF16).reshape(
            owners, 2, 2 * width
        )


def side(coeffs_ref, s, w):
    chans = coeffs_ref.shape[1]
    narrow = coeffs_ref.shape[3] // (4 * GROUPS)
    return jnp.concatenate(
        [
            jnp.concatenate(
                [
                    coeffs_ref[s, y, :, (2 * jp + w) * narrow : (2 * jp + w + 1) * narrow]
                    for y in range(chans)
                ],
                axis=1,
            )
            for jp in range(2 * GROUPS)
        ],
        axis=0,
    )


def degree_kernel(coeffs_ref, weights_ref, back_ref):
    chans, lat_count = coeffs_ref.shape[1:3]
    narrow = coeffs_ref.shape[3] // (4 * GROUPS)
    for s in range(2):
        back = lax.dot_general(
            side(coeffs_ref, s, 1),
            weights_ref[s],
            (((1,), (1,)), ((), ())),
            preferred_element_type=F32,
        ).astype(BF16)
        for y in range(chans):
            back_ref[y * lat_count : (y + 1) * lat_count, s, :] = jnp.concatenate(
                [
                    back[jp * lat_count : (jp + 1) * lat_count, y * narrow : (y + 1) * narrow]
                    for jp in range(2 * GROUPS)
                ],
                axis=1,
            )


def gradient_kernel(coeffs_ref, grad_ref):
    for s in range(2):
        grad_ref[s] = lax.dot_general(
            side(coeffs_ref, s, 0),
            side(coeffs_ref, s, 1),
            (((0,), (0,)), ((), ())),
            preferred_element_type=F32,
        )


def backward_kernel(back_ref, legendre_ref, out_ref):
    slots = legendre_ref.shape[2]
    lat_count = out_ref.shape[0]
    span = back_ref.shape[2] // GROUPS
    half = ROWS // 2
    for j in range(GROUPS):
        held = back_ref[:, :, j * span : (j + 1) * span].reshape(slots, span)
        modes = jnp.dot(legendre_ref[j], held, preferred_element_type=F32).astype(BF16)
        for k in range(half):
            out_ref[:, :, (j * half + k) * span : (j * half + k + 1) * span] = modes[
                2 * lat_count * k : 2 * lat_count * (k + 1)
            ].reshape(lat_count, 2, span)


def synthesis_kernel(modes_ref, fourier_ref, out_ref):
    narrow = out_ref.shape[1]
    half = ROWS // 2
    modes = jnp.concatenate(
        [
            jnp.concatenate(
                [
                    modes_ref[k % 2, :, at : at + narrow]
                    for k in range(ROWS)
                    for at in [((j * half + k // 2) * 2 + p) * narrow]
                ],
                axis=1,
            )
            for j in range(GROUPS)
            for p in range(2)
        ],
        axis=0,
    )
    grad = lax.dot_general(
        modes, fourier_ref[...], (((0,), (0,)), ((), ())), preferred_element_type=F32
    ).astype(BF16)
    for k in range(ROWS):
        out_ref[k] = grad[k * narrow : (k + 1) * narrow, :]


def placing_kernel(counts_ref, rank_ref, mine_ref, theirs_ref, out_ref, empty_ref, sems):
    rank = rank_ref[0]
    odd = rank % 2
    first = counts_ref[rank - odd]
    start = odd * first
    count = jnp.where(odd == 1, 2 * ROWS - first, first)
    empty_ref[...] = jnp.zeros_like(empty_ref)
    copies = []
    for r in range(2 * ROWS):
        at = start + r
        live = r < count
        own = (at // ROWS) == odd
        target, sem = out_ref.at[r], sems.at[r]
        near = pltpu.make_async_copy(
            mine_ref.at[jnp.clip(at - odd * ROWS, 0, ROWS - 1)], target, sem
        )
        far = pltpu.make_async_copy(
            theirs_ref.at[jnp.clip(at - (1 - odd) * ROWS, 0, ROWS - 1)], target, sem
        )
        dead = pltpu.make_async_copy(empty_ref, target, sem)
        pl.when(live & own)(near.start)
        pl.when(live & jnp.logical_not(own))(far.start)
        pl.when(jnp.logical_not(live))(dead.start)
        copies.append(near)
    for copy in copies:
        copy.wait()


def on_device(field_in, cotangent, weights, row_counts, slot_degree):
    lat_count = lax.axis_size("lat")
    chan_count = lax.axis_size("chan")
    rank = lax.axis_index("lat")
    narrow = field_in.shape[1]
    held, full = weights.shape[:2]
    devices = lat_count * chan_count
    pairs = [(i, i ^ 1) for i in range(lat_count)]
    odd = rank % 2
    at_rank = jnp.reshape(rank, (1,)).astype(jnp.int32)
    table = fourier_rows(lat_count)
    by_part = jnp.asarray(table.reshape(-1, NLON))
    by_rank = jnp.asarray(table.transpose(0, 2, 1, 3).reshape(-1, NLON))
    everyone = ("chan", "lat")

    field_swap = lax.ppermute(
        lax.dynamic_slice_in_dim(field_in, (1 - odd) * ROWS, ROWS), "lat", pairs
    )
    cotan_swap = lax.ppermute(
        lax.dynamic_slice_in_dim(cotangent, (1 - odd) * ROWS, ROWS), "lat", pairs
    )
    width = 2 * ROWS * narrow
    modes = run(
        analysis_kernel,
        "analysis",
        [pltpu.VMEM((lat_count, 2, GROUPS * width), BF16)],
        [row_counts, at_rank, field_in, cotangent, field_swap, cotan_swap, by_rank],
        [pltpu.VMEM((width, NLON), BF16)],
    )
    modes = lax.all_to_all(modes, "lat", split_axis=0, concat_axis=0, tiled=True)
    modes = modes.transpose(1, 0, 2)
    slot_rows = slot_degree.reshape(lat_count, chan_count, held).transpose(1, 0, 2).reshape(-1)
    legendre, legendre_pairs = legendre_slots(at_rank, lat_count, slot_rows)
    coeffs = run(
        forward_kernel,
        "forward",
        [pltpu.VMEM((devices, held, 4 * GROUPS * narrow), BF16)],
        [at_rank, modes, legendre],
    )
    coeffs = lax.all_to_all(coeffs, everyone, split_axis=0, concat_axis=0, tiled=True)
    coeffs = coeffs.transpose(1, 0, 2).reshape(held, chan_count, lat_count, 4 * GROUPS * narrow)
    back = run(
        degree_kernel,
        "degree",
        [pltpu.VMEM((devices, held, 2 * GROUPS * narrow), BF16)],
        [coeffs, weights],
    )
    back, coeffs = lax.optimization_barrier((back, coeffs))
    back = lax.all_to_all(back, everyone, split_axis=0, concat_axis=0, tiled=True)
    weight_grad = run(
        gradient_kernel, "gradient", [jax.ShapeDtypeStruct((held, full, full), F32)], [coeffs]
    )
    back, weight_grad = lax.optimization_barrier((back, weight_grad))
    modes_back = run(
        backward_kernel,
        "backward",
        [pltpu.VMEM((lat_count, 2, GROUPS * ROWS * narrow), BF16)],
        [back, legendre_pairs],
    )
    modes_back = lax.all_to_all(modes_back, "lat", split_axis=0, concat_axis=0, tiled=True)
    grad = run(
        synthesis_kernel,
        "synthesis",
        [pltpu.VMEM((ROWS, narrow, NLON), BF16)],
        [modes_back.transpose(1, 0, 2), by_part],
    )
    grad_swap = lax.ppermute(grad, "lat", pairs)
    field_grad = run(
        placing_kernel,
        "placing",
        [jax.ShapeDtypeStruct(field_in.shape, BF16)],
        [row_counts, at_rank, grad, grad_swap],
        [pltpu.VMEM((narrow, NLON), BF16), pltpu.SemaphoreType.DMA((2 * ROWS,))],
        pl.ANY,
    )
    return field_grad, weight_grad


def solution(mesh):
    placed = (
        P("lat", "chan", None),
        P("lat", "chan", None),
        P(("lat", "chan"), None, None),
        P(),
        P(),
    )
    return jax.shard_map(
        on_device,
        mesh=mesh,
        in_specs=placed,
        out_specs=(P("lat", "chan", None), P(("lat", "chan"), None, None)),
        check_vma=False,
    )
```

```python
import math

import jax
import jax.numpy as jnp
import ml_dtypes
import numpy as np
from jax import lax
from jax.experimental import pallas as pl
from jax.experimental.pallas import tpu as pltpu
from jax.sharding import PartitionSpec as P

NLON = 720
L = 360
M = 360
LPAD = 384
ROWS = 6
GROUPS = 6
RESCALE = 2.0**40
RESCALE_LOG = 40.0 * math.log(2.0)
BF16 = jnp.bfloat16
F32 = jnp.float32
VMEM_BYTES = 30 * 1024 * 1024


def fourier_rows(lat_count):
    orders = np.arange(GROUPS * lat_count)
    turns = orders[:, None] * np.arange(NLON)[None, :] % NLON
    angles = turns * (2.0 * math.pi / NLON)
    live = (orders < M)[:, None] / math.sqrt(NLON)
    parts = np.stack([np.cos(angles) * live, -np.sin(angles) * live], axis=0)
    parts = parts.reshape(2, GROUPS, lat_count, NLON).transpose(1, 0, 2, 3)
    return parts.astype(ml_dtypes.bfloat16)


def order_norms(lat_count):
    orders = np.arange(8)[None, :] * lat_count + np.arange(lat_count)[:, None]
    logs = [
        0.5 * math.log((2.0 * m + 1.0) / (4.0 * math.pi))
        + 0.5 * math.lgamma(2.0 * m + 1.0)
        - m * math.log(2.0)
        - math.lgamma(m + 1.0)
        for m in orders.reshape(-1).tolist()
    ]
    latitudes = ROWS * lat_count
    total = np.array(logs).reshape(orders.shape) + 0.5 * math.log(2.0 * math.pi**2 / latitudes)
    return np.broadcast_to(total[:, :, None], total.shape + (128,)).astype(np.float32)


def latitude_rows(lat_count):
    grid = np.arange(lat_count)[None, :] * ROWS + np.arange(ROWS)[:, None]
    paired = grid.reshape(ROWS // 2, 2, lat_count).transpose(0, 2, 1)
    order = np.concatenate([grid.reshape(-1), paired.reshape(-1)])[None, :]
    theta = (order + 0.5) * (math.pi / (ROWS * lat_count))
    return np.cos(theta).astype(np.float32), np.log(np.sin(theta)).astype(np.float32)


def run(kernel, name, outs, args, scratch=(), far=(), home=pltpu.VMEM):
    specs, operands = [], []
    for at, arg in enumerate(args):
        if arg.dtype == jnp.int32 and arg.ndim == 1:
            specs.append(pl.BlockSpec(memory_space=pltpu.SMEM))
        elif at in far:
            specs.append(pl.BlockSpec(memory_space=pl.ANY))
        else:
            specs.append(pl.BlockSpec(memory_space=pltpu.VMEM))
            arg = pltpu.with_memory_space_constraint(arg, pltpu.VMEM)
        operands.append(arg)
    results = pl.pallas_call(
        kernel,
        out_shape=tuple(outs),
        in_specs=specs,
        out_specs=tuple(pl.BlockSpec(memory_space=home) for _ in outs),
        scratch_shapes=list(scratch),
        compiler_params=pltpu.CompilerParams(vmem_limit_bytes=VMEM_BYTES),
        name=name,
    )(*operands)
    return results if len(outs) > 1 else results[0]


def legendre_kernel(
    rank_ref, cosine_ref, logsine_ref, norm_ref, slot_ref, rows_out_ref, pairs_out_ref, rows_ref
):
    rank = rank_ref[0]
    lat_count = norm_ref.shape[0]
    latitudes = rows_out_ref.shape[2]
    shape = (8, 128)
    groups = lax.broadcasted_iota(jnp.int32, shape, 0)
    order = (rank + groups * lat_count).astype(F32)
    square = order * order
    tiles = cosine_ref.shape[1] // 128
    cosines, scales = [], []
    for t in range(tiles):
        lanes = slice(128 * t, 128 * (t + 1))
        cosines.append(jnp.broadcast_to(cosine_ref[:, lanes], shape))
        logsine = jnp.broadcast_to(logsine_ref[:, lanes], shape)
        scales.append(norm_ref[rank] + order * logsine + 0.5 * logsine)
    zero = jnp.zeros(shape, F32)
    one = jnp.ones(shape, F32)

    def advance(l, carry):
        degree = l.astype(F32)
        below = degree - 1.0
        upper = jnp.sqrt(
            jnp.maximum(4.0 * degree * degree - 1.0, 1.0)
            / jnp.maximum(degree * degree - square, 1.0)
        )
        lower = jnp.sqrt(
            jnp.maximum(below * below - square, 0.0)
            / jnp.maximum(4.0 * below * below - 1.0, 1.0)
        )
        rising = degree > order
        reached = degree >= order
        fresh = []
        for t in range(tiles):
            previous, current, scale = carry[3 * t : 3 * t + 3]
            value = upper * (cosines[t] * current - lower * previous)
            previous = jnp.where(rising, current, previous)
            current = jnp.where(rising, value, current)
            too_large = jnp.abs(current) > RESCALE
            factor = jnp.where(too_large, 1.0 / RESCALE, 1.0)
            previous = previous * factor
            current = current * factor
            scale = scale + jnp.where(too_large, RESCALE_LOG, 0.0)
            rows_ref[l, :, 128 * t : 128 * (t + 1)] = jnp.where(
                reached, current * jnp.exp(scale), 0.0
            )
            fresh += [previous, current, scale]
        return tuple(fresh)

    start = []
    for t in range(tiles):
        start += [zero, one, scales[t]]
    lax.fori_loop(0, L, advance, tuple(start), unroll=4)
    rows_ref[L:, :, :] = jnp.zeros((LPAD - L,) + rows_ref.shape[1:], F32)
    slots = slot_ref.shape[0]
    degrees = lax.broadcasted_iota(jnp.int32, (slots, LPAD), 1)
    pick = jnp.where((degrees == slot_ref[...]) & (degrees < L), 1.0, 0.0).astype(BF16)
    for j in range(GROUPS):
        table = rows_ref[:, j, :latitudes].astype(BF16)
        rows_out_ref[j] = jnp.dot(pick, table, preferred_element_type=F32).astype(BF16)
        table = rows_ref[:, j, latitudes:].astype(BF16)
        pairs_out_ref[j] = lax.dot_general(
            table, pick, (((0,), (1,)), ((), ())), preferred_element_type=F32
        ).astype(BF16)


def legendre_slots(at_rank, lat_count, slot_rows):
    slots = slot_rows.shape[0]
    latitudes = ROWS * lat_count
    cosine, logsine = latitude_rows(lat_count)
    return run(
        legendre_kernel,
        "legendre",
        [
            pltpu.VMEM((GROUPS, slots, latitudes), BF16),
            jax.ShapeDtypeStruct((GROUPS, latitudes, slots), BF16),
        ],
        [
            at_rank,
            jnp.asarray(cosine),
            jnp.asarray(logsine),
            jnp.asarray(order_norms(lat_count)),
            slot_rows[:, None],
        ],
        [pltpu.VMEM((LPAD, 8, 2 * latitudes), F32)],
    )


def analysis_kernel(
    counts_ref, rank_ref, field_ref, cotan_ref, field_in_ref, cotan_in_ref, table_ref,
    out_ref, rows_ref, fourier_ref, held_ref, sems,
):
    narrow = field_ref.shape[1]
    lat_count = out_ref.shape[0]
    width = 2 * ROWS * narrow
    loads = []
    block = 2 * lat_count * (GROUPS // 2)
    for half in range(2):
        at = pl.ds(half * block, block)
        loads.append(pltpu.make_async_copy(table_ref.at[at], fourier_ref.at[at], sems.at[half]))
        loads[-1].start()
    rank = rank_ref[0]
    odd = rank % 2
    first = counts_ref[rank - odd]
    for k in range(ROWS):
        own = k + odd * (ROWS - first)
        mine = (own >= 0) & ((odd == 1) | (k < first))
        theirs = jnp.where(odd == 1, k, k - first)
        for w, (here, there) in enumerate(((field_ref, field_in_ref), (cotan_ref, cotan_in_ref))):
            at = slice((2 * k + w) * narrow, (2 * k + w + 1) * narrow)

            @pl.when(mine)
            def _():
                rows_ref[at, :] = here[jnp.clip(own, 0, 2 * ROWS - 1)]

            @pl.when(jnp.logical_not(mine))
            def _():
                rows_ref[at, :] = there[jnp.clip(theirs, 0, ROWS - 1)]

    stores = []
    for half in range(2):
        loads[half].wait()
        modes = lax.dot_general(
            fourier_ref[half * block : (half + 1) * block, :],
            rows_ref[...],
            (((1,), (1,)), ((), ())),
            preferred_element_type=F32,
        ).astype(BF16)
        for i in range(GROUPS // 2):
            j = half * (GROUPS // 2) + i
            held_ref[:, :, j * width : (j + 1) * width] = modes[
                2 * lat_count * i : 2 * lat_count * (i + 1)
            ].reshape(lat_count, 2, width)
        lanes = pl.ds(half * (GROUPS // 2) * width, (GROUPS // 2) * width)
        stores.append(
            pltpu.make_async_copy(
                held_ref.at[:, :, lanes], out_ref.at[:, :, lanes], sems.at[2 + half]
            )
        )
        stores[-1].start()
    for store in stores:
        store.wait()


def forward_kernel(rank_ref, modes_ref, legendre_ref, out_ref):
    width = modes_ref.shape[2] // (GROUPS * ROWS)
    owners = out_ref.shape[0]
    slots = legendre_ref.shape[1]
    lane = lax.broadcasted_iota(jnp.int32, (slots, 2 * width), 1)
    cotangent = lane // (width // 2) % 2 == 1
    for j in range(GROUPS):
        slab = jnp.concatenate(
            [
                jnp.concatenate(
                    [
                        modes_ref[p, :, (j * ROWS + k) * width : (j * ROWS + k + 1) * width]
                        for p in range(2)
                    ],
                    axis=1,
                )
                for k in range(ROWS)
            ],
            axis=0,
        )
        coeffs = jnp.dot(legendre_ref[j], slab, preferred_element_type=F32)
        doubled = jnp.where(rank_ref[0] + j == 0, 1.0, 2.0)
        coeffs = jnp.where(cotangent, coeffs * doubled, coeffs)
        out_ref[:, :, 2 * j * width : 2 * (j + 1) * width] = coeffs.astype(BF16).reshape(
            owners, 2, 2 * width
        )


def side(coeffs_ref, s, w):
    chans = coeffs_ref.shape[1]
    narrow = coeffs_ref.shape[3] // (4 * GROUPS)
    return jnp.concatenate(
        [
            jnp.concatenate(
                [
                    coeffs_ref[s, y, :, (2 * jp + w) * narrow : (2 * jp + w + 1) * narrow]
                    for y in range(chans)
                ],
                axis=1,
            )
            for jp in range(2 * GROUPS)
        ],
        axis=0,
    )


def degree_kernel(coeffs_ref, stored_ref, back_ref, weights_ref, sems):
    chans, lat_count = coeffs_ref.shape[1:3]
    narrow = coeffs_ref.shape[3] // (4 * GROUPS)
    loads = [
        pltpu.make_async_copy(stored_ref.at[s], weights_ref.at[s], sems.at[s]) for s in range(2)
    ]
    for load in loads:
        load.start()
    for s in range(2):
        dcoeffs = side(coeffs_ref, s, 1)
        loads[s].wait()
        back = lax.dot_general(
            dcoeffs,
            weights_ref[s],
            (((1,), (1,)), ((), ())),
            preferred_element_type=F32,
        ).astype(BF16)
        for y in range(chans):
            back_ref[y * lat_count : (y + 1) * lat_count, s, :] = jnp.concatenate(
                [
                    back[jp * lat_count : (jp + 1) * lat_count, y * narrow : (y + 1) * narrow]
                    for jp in range(2 * GROUPS)
                ],
                axis=1,
            )


def gradient_kernel(coeffs_ref, grad_ref):
    for s in range(2):
        grad_ref[s] = lax.dot_general(
            side(coeffs_ref, s, 0),
            side(coeffs_ref, s, 1),
            (((0,), (0,)), ((), ())),
            preferred_element_type=F32,
        )


def backward_kernel(back_ref, stored_ref, out_ref, legendre_ref, sems):
    slots = legendre_ref.shape[2]
    loads = [
        pltpu.make_async_copy(stored_ref.at[j], legendre_ref.at[j], sems.at[j])
        for j in range(GROUPS)
    ]
    for load in loads:
        load.start()
    lat_count = out_ref.shape[0]
    span = back_ref.shape[2] // GROUPS
    half = ROWS // 2
    for j in range(GROUPS):
        held = back_ref[:, :, j * span : (j + 1) * span].reshape(slots, span)
        loads[j].wait()
        modes = jnp.dot(legendre_ref[j], held, preferred_element_type=F32).astype(BF16)
        for k in range(half):
            out_ref[:, :, (j * half + k) * span : (j * half + k + 1) * span] = modes[
                2 * lat_count * k : 2 * lat_count * (k + 1)
            ].reshape(lat_count, 2, span)


def synthesis_kernel(modes_ref, fourier_ref, out_ref):
    narrow = out_ref.shape[1]
    half = ROWS // 2
    modes = jnp.concatenate(
        [
            jnp.concatenate(
                [
                    modes_ref[k % 2, :, at : at + narrow]
                    for k in range(ROWS)
                    for at in [((j * half + k // 2) * 2 + p) * narrow]
                ],
                axis=1,
            )
            for j in range(GROUPS)
            for p in range(2)
        ],
        axis=0,
    )
    grad = lax.dot_general(
        modes, fourier_ref[...], (((0,), (0,)), ((), ())), preferred_element_type=F32
    ).astype(BF16)
    for k in range(ROWS):
        out_ref[k] = grad[k * narrow : (k + 1) * narrow, :]


def placing_kernel(counts_ref, rank_ref, mine_ref, theirs_ref, out_ref, empty_ref, sems):
    rank = rank_ref[0]
    odd = rank % 2
    first = counts_ref[rank - odd]
    start = odd * first
    count = jnp.where(odd == 1, 2 * ROWS - first, first)
    empty_ref[...] = jnp.zeros_like(empty_ref)
    copies = []
    for r in range(2 * ROWS):
        at = start + r
        live = r < count
        own = (at // ROWS) == odd
        target, sem = out_ref.at[r], sems.at[r]
        near = pltpu.make_async_copy(
            mine_ref.at[jnp.clip(at - odd * ROWS, 0, ROWS - 1)], target, sem
        )
        far = pltpu.make_async_copy(
            theirs_ref.at[jnp.clip(at - (1 - odd) * ROWS, 0, ROWS - 1)], target, sem
        )
        dead = pltpu.make_async_copy(empty_ref, target, sem)
        pl.when(live & own)(near.start)
        pl.when(live & jnp.logical_not(own))(far.start)
        pl.when(jnp.logical_not(live))(dead.start)
        copies.append(near)
    for copy in copies:
        copy.wait()


def on_device(field_in, cotangent, weights, row_counts, slot_degree):
    lat_count = lax.axis_size("lat")
    chan_count = lax.axis_size("chan")
    rank = lax.axis_index("lat")
    narrow = field_in.shape[1]
    held, full = weights.shape[:2]
    devices = lat_count * chan_count
    pairs = [(i, i ^ 1) for i in range(lat_count)]
    odd = rank % 2
    at_rank = jnp.reshape(rank, (1,)).astype(jnp.int32)
    table = fourier_rows(lat_count)
    by_part = jnp.asarray(table.reshape(-1, NLON))
    by_rank = jnp.asarray(table.transpose(0, 2, 1, 3).reshape(-1, NLON))
    everyone = ("chan", "lat")

    field_swap = lax.ppermute(
        lax.dynamic_slice_in_dim(field_in, (1 - odd) * ROWS, ROWS), "lat", pairs
    )
    cotan_swap = lax.ppermute(
        lax.dynamic_slice_in_dim(cotangent, (1 - odd) * ROWS, ROWS), "lat", pairs
    )
    width = 2 * ROWS * narrow
    modes = run(
        analysis_kernel,
        "analysis",
        [jax.ShapeDtypeStruct((lat_count, 2, GROUPS * width), BF16)],
        [row_counts, at_rank, field_in, cotangent, field_swap, cotan_swap, by_rank],
        [
            pltpu.VMEM((width, NLON), BF16),
            pltpu.VMEM(by_rank.shape, BF16),
            pltpu.VMEM((lat_count, 2, GROUPS * width), BF16),
            pltpu.SemaphoreType.DMA((4,)),
        ],
        far=(6,),
        home=pl.ANY,
    )
    modes = lax.all_to_all(modes, "lat", split_axis=0, concat_axis=0, tiled=True)
    modes = modes.transpose(1, 0, 2)
    slot_rows = slot_degree.reshape(lat_count, chan_count, held).transpose(1, 0, 2).reshape(-1)
    legendre, legendre_pairs = legendre_slots(at_rank, lat_count, slot_rows)
    coeffs = run(
        forward_kernel,
        "forward",
        [pltpu.VMEM((devices, held, 4 * GROUPS * narrow), BF16)],
        [at_rank, modes, legendre],
    )
    coeffs = lax.all_to_all(coeffs, everyone, split_axis=0, concat_axis=0, tiled=True)
    coeffs = coeffs.transpose(1, 0, 2).reshape(held, chan_count, lat_count, 4 * GROUPS * narrow)
    back = run(
        degree_kernel,
        "degree",
        [jax.ShapeDtypeStruct((devices, held, 2 * GROUPS * narrow), BF16)],
        [coeffs, weights],
        [pltpu.VMEM(weights.shape, BF16), pltpu.SemaphoreType.DMA((held,))],
        far=(1,),
    )
    back, coeffs = lax.optimization_barrier((back, coeffs))
    back = lax.all_to_all(back, everyone, split_axis=0, concat_axis=0, tiled=True)
    weight_grad = run(
        gradient_kernel, "gradient", [jax.ShapeDtypeStruct((held, full, full), F32)], [coeffs]
    )
    back, weight_grad = lax.optimization_barrier((back, weight_grad))
    modes_back = run(
        backward_kernel,
        "backward",
        [pltpu.VMEM((lat_count, 2, GROUPS * ROWS * narrow), BF16)],
        [back, legendre_pairs],
        [pltpu.VMEM(legendre_pairs.shape, BF16), pltpu.SemaphoreType.DMA((GROUPS,))],
        far=(1,),
    )
    modes_back = lax.all_to_all(modes_back, "lat", split_axis=0, concat_axis=0, tiled=True)
    grad = run(
        synthesis_kernel,
        "synthesis",
        [pltpu.VMEM((ROWS, narrow, NLON), BF16)],
        [modes_back.transpose(1, 0, 2), by_part],
    )
    grad_swap = lax.ppermute(grad, "lat", pairs)
    field_grad = run(
        placing_kernel,
        "placing",
        [jax.ShapeDtypeStruct(field_in.shape, BF16)],
        [row_counts, at_rank, grad, grad_swap],
        [pltpu.VMEM((narrow, NLON), BF16), pltpu.SemaphoreType.DMA((2 * ROWS,))],
        home=pl.ANY,
    )
    return field_grad, weight_grad


def solution(mesh):
    placed = (
        P("lat", "chan", None),
        P("lat", "chan", None),
        P(("lat", "chan"), None, None),
        P(),
        P(),
    )
    return jax.shard_map(
        on_device,
        mesh=mesh,
        in_specs=placed,
        out_specs=(P("lat", "chan", None), P(("lat", "chan"), None, None)),
        check_vma=False,
    )
```

```python
import math

import jax
import jax.numpy as jnp
import ml_dtypes
import numpy as np
from jax import lax
from jax.experimental import pallas as pl
from jax.experimental.pallas import tpu as pltpu
from jax.sharding import PartitionSpec as P

NLON = 720
L = 360
M = 360
LPAD = 384
ROWS = 6
GROUPS = 6
RESCALE = 2.0**40
RESCALE_LOG = 40.0 * math.log(2.0)
BF16 = jnp.bfloat16
F32 = jnp.float32
VMEM_BYTES = 30 * 1024 * 1024


def fourier_rows(lat_count):
    orders = np.arange(GROUPS * lat_count)
    turns = orders[:, None] * np.arange(NLON)[None, :] % NLON
    angles = turns * (2.0 * math.pi / NLON)
    live = (orders < M)[:, None] / math.sqrt(NLON)
    parts = np.stack([np.cos(angles) * live, -np.sin(angles) * live], axis=0)
    parts = parts.reshape(2, GROUPS, lat_count, NLON).transpose(1, 0, 2, 3)
    return parts.astype(ml_dtypes.bfloat16)


def order_norms(lat_count):
    orders = np.arange(8)[None, :] * lat_count + np.arange(lat_count)[:, None]
    logs = [
        0.5 * math.log((2.0 * m + 1.0) / (4.0 * math.pi))
        + 0.5 * math.lgamma(2.0 * m + 1.0)
        - m * math.log(2.0)
        - math.lgamma(m + 1.0)
        for m in orders.reshape(-1).tolist()
    ]
    latitudes = ROWS * lat_count
    total = np.array(logs).reshape(orders.shape) + 0.5 * math.log(2.0 * math.pi**2 / latitudes)
    return np.broadcast_to(total[:, :, None], total.shape + (128,)).astype(np.float32)


def latitude_rows(lat_count):
    grid = np.arange(lat_count)[None, :] * ROWS + np.arange(ROWS)[:, None]
    paired = grid.reshape(ROWS // 2, 2, lat_count).transpose(0, 2, 1)
    order = np.concatenate([grid.reshape(-1), paired.reshape(-1)])[None, :]
    theta = (order + 0.5) * (math.pi / (ROWS * lat_count))
    return np.cos(theta).astype(np.float32), np.log(np.sin(theta)).astype(np.float32)


def run(kernel, name, outs, args, scratch=(), far=(), home=pltpu.VMEM):
    specs, operands = [], []
    for at, arg in enumerate(args):
        if arg.dtype == jnp.int32 and arg.ndim == 1:
            specs.append(pl.BlockSpec(memory_space=pltpu.SMEM))
        elif at in far:
            specs.append(pl.BlockSpec(memory_space=pltpu.HBM))
            arg = pltpu.with_memory_space_constraint(arg, pltpu.HBM)
        else:
            specs.append(pl.BlockSpec(memory_space=pltpu.VMEM))
            arg = pltpu.with_memory_space_constraint(arg, pltpu.VMEM)
        operands.append(arg)
    results = pl.pallas_call(
        kernel,
        out_shape=tuple(outs),
        in_specs=specs,
        out_specs=tuple(pl.BlockSpec(memory_space=home) for _ in outs),
        scratch_shapes=list(scratch),
        compiler_params=pltpu.CompilerParams(vmem_limit_bytes=VMEM_BYTES),
        name=name,
    )(*operands)
    return results if len(outs) > 1 else results[0]


def legendre_kernel(
    rank_ref, cosine_ref, logsine_ref, norm_ref, slot_ref, rows_out_ref, pairs_out_ref, rows_ref
):
    rank = rank_ref[0]
    lat_count = norm_ref.shape[0]
    latitudes = rows_out_ref.shape[2]
    shape = (8, 128)
    groups = lax.broadcasted_iota(jnp.int32, shape, 0)
    order = (rank + groups * lat_count).astype(F32)
    square = order * order
    tiles = cosine_ref.shape[1] // 128
    cosines, scales = [], []
    for t in range(tiles):
        lanes = slice(128 * t, 128 * (t + 1))
        cosines.append(jnp.broadcast_to(cosine_ref[:, lanes], shape))
        logsine = jnp.broadcast_to(logsine_ref[:, lanes], shape)
        scales.append(norm_ref[rank] + order * logsine + 0.5 * logsine)
    zero = jnp.zeros(shape, F32)
    one = jnp.ones(shape, F32)

    def advance(l, carry):
        degree = l.astype(F32)
        below = degree - 1.0
        upper = jnp.sqrt(
            jnp.maximum(4.0 * degree * degree - 1.0, 1.0)
            / jnp.maximum(degree * degree - square, 1.0)
        )
        lower = jnp.sqrt(
            jnp.maximum(below * below - square, 0.0)
            / jnp.maximum(4.0 * below * below - 1.0, 1.0)
        )
        rising = degree > order
        reached = degree >= order
        fresh = []
        for t in range(tiles):
            previous, current, scale = carry[3 * t : 3 * t + 3]
            value = upper * (cosines[t] * current - lower * previous)
            previous = jnp.where(rising, current, previous)
            current = jnp.where(rising, value, current)
            too_large = jnp.abs(current) > RESCALE
            factor = jnp.where(too_large, 1.0 / RESCALE, 1.0)
            previous = previous * factor
            current = current * factor
            scale = scale + jnp.where(too_large, RESCALE_LOG, 0.0)
            rows_ref[l, :, 128 * t : 128 * (t + 1)] = jnp.where(
                reached, current * jnp.exp(scale), 0.0
            )
            fresh += [previous, current, scale]
        return tuple(fresh)

    start = []
    for t in range(tiles):
        start += [zero, one, scales[t]]
    lax.fori_loop(0, L, advance, tuple(start), unroll=4)
    rows_ref[L:, :, :] = jnp.zeros((LPAD - L,) + rows_ref.shape[1:], F32)
    slots = slot_ref.shape[0]
    degrees = lax.broadcasted_iota(jnp.int32, (slots, LPAD), 1)
    pick = jnp.where((degrees == slot_ref[...]) & (degrees < L), 1.0, 0.0).astype(BF16)
    for j in range(GROUPS):
        table = rows_ref[:, j, :latitudes].astype(BF16)
        rows_out_ref[j] = jnp.dot(pick, table, preferred_element_type=F32).astype(BF16)
        table = rows_ref[:, j, latitudes:].astype(BF16)
        pairs_out_ref[j] = lax.dot_general(
            table, pick, (((0,), (1,)), ((), ())), preferred_element_type=F32
        ).astype(BF16)


def legendre_slots(at_rank, lat_count, slot_rows):
    slots = slot_rows.shape[0]
    latitudes = ROWS * lat_count
    cosine, logsine = latitude_rows(lat_count)
    return run(
        legendre_kernel,
        "legendre",
        [
            pltpu.VMEM((GROUPS, slots, latitudes), BF16),
            pltpu.HBM((GROUPS, latitudes, slots), BF16),
        ],
        [
            at_rank,
            jnp.asarray(cosine),
            jnp.asarray(logsine),
            jnp.asarray(order_norms(lat_count)),
            slot_rows[:, None],
        ],
        [pltpu.VMEM((LPAD, 8, 2 * latitudes), F32)],
    )


def analysis_kernel(
    counts_ref, rank_ref, field_ref, cotan_ref, field_in_ref, cotan_in_ref, table_ref,
    out_ref, rows_ref, fourier_ref, held_ref, sems,
):
    narrow = field_ref.shape[1]
    lat_count = out_ref.shape[0]
    width = 2 * ROWS * narrow
    loads = []
    block = 2 * lat_count * (GROUPS // 2)
    for half in range(2):
        at = pl.ds(half * block, block)
        loads.append(pltpu.make_async_copy(table_ref.at[at], fourier_ref.at[at], sems.at[half]))
        loads[-1].start()
    rank = rank_ref[0]
    odd = rank % 2
    first = counts_ref[rank - odd]
    for k in range(ROWS):
        own = k + odd * (ROWS - first)
        mine = (own >= 0) & ((odd == 1) | (k < first))
        theirs = jnp.where(odd == 1, k, k - first)
        for w, (here, there) in enumerate(((field_ref, field_in_ref), (cotan_ref, cotan_in_ref))):
            at = slice((2 * k + w) * narrow, (2 * k + w + 1) * narrow)

            @pl.when(mine)
            def _():
                rows_ref[at, :] = here[jnp.clip(own, 0, 2 * ROWS - 1)]

            @pl.when(jnp.logical_not(mine))
            def _():
                rows_ref[at, :] = there[jnp.clip(theirs, 0, ROWS - 1)]

    stores = []
    for half in range(2):
        loads[half].wait()
        modes = lax.dot_general(
            fourier_ref[half * block : (half + 1) * block, :],
            rows_ref[...],
            (((1,), (1,)), ((), ())),
            preferred_element_type=F32,
        ).astype(BF16)
        for i in range(GROUPS // 2):
            j = half * (GROUPS // 2) + i
            held_ref[:, :, j * width : (j + 1) * width] = modes[
                2 * lat_count * i : 2 * lat_count * (i + 1)
            ].reshape(lat_count, 2, width)
        lanes = pl.ds(half * (GROUPS // 2) * width, (GROUPS // 2) * width)
        stores.append(
            pltpu.make_async_copy(
                held_ref.at[:, :, lanes], out_ref.at[:, :, lanes], sems.at[2 + half]
            )
        )
        stores[-1].start()
    for store in stores:
        store.wait()


def forward_kernel(rank_ref, modes_ref, legendre_ref, out_ref):
    width = modes_ref.shape[2] // (GROUPS * ROWS)
    owners = out_ref.shape[0]
    slots = legendre_ref.shape[1]
    lane = lax.broadcasted_iota(jnp.int32, (slots, 2 * width), 1)
    cotangent = lane // (width // 2) % 2 == 1
    for j in range(GROUPS):
        slab = jnp.concatenate(
            [
                jnp.concatenate(
                    [
                        modes_ref[p, :, (j * ROWS + k) * width : (j * ROWS + k + 1) * width]
                        for p in range(2)
                    ],
                    axis=1,
                )
                for k in range(ROWS)
            ],
            axis=0,
        )
        coeffs = jnp.dot(legendre_ref[j], slab, preferred_element_type=F32)
        doubled = jnp.where(rank_ref[0] + j == 0, 1.0, 2.0)
        coeffs = jnp.where(cotangent, coeffs * doubled, coeffs)
        out_ref[:, :, 2 * j * width : 2 * (j + 1) * width] = coeffs.astype(BF16).reshape(
            owners, 2, 2 * width
        )


def side(coeffs_ref, s, w):
    chans = coeffs_ref.shape[1]
    narrow = coeffs_ref.shape[3] // (4 * GROUPS)
    return jnp.concatenate(
        [
            jnp.concatenate(
                [
                    coeffs_ref[s, y, :, (2 * jp + w) * narrow : (2 * jp + w + 1) * narrow]
                    for y in range(chans)
                ],
                axis=1,
            )
            for jp in range(2 * GROUPS)
        ],
        axis=0,
    )


def degree_kernel(coeffs_ref, stored_ref, back_ref, weights_ref, sems):
    chans, lat_count = coeffs_ref.shape[1:3]
    narrow = coeffs_ref.shape[3] // (4 * GROUPS)
    loads = [
        pltpu.make_async_copy(stored_ref.at[s], weights_ref.at[s], sems.at[s]) for s in range(2)
    ]
    for load in loads:
        load.start()
    for s in range(2):
        dcoeffs = side(coeffs_ref, s, 1)
        loads[s].wait()
        back = lax.dot_general(
            dcoeffs,
            weights_ref[s],
            (((1,), (1,)), ((), ())),
            preferred_element_type=F32,
        ).astype(BF16)
        for y in range(chans):
            back_ref[y * lat_count : (y + 1) * lat_count, s, :] = jnp.concatenate(
                [
                    back[jp * lat_count : (jp + 1) * lat_count, y * narrow : (y + 1) * narrow]
                    for jp in range(2 * GROUPS)
                ],
                axis=1,
            )


def gradient_kernel(coeffs_ref, grad_ref):
    for s in range(2):
        grad_ref[s] = lax.dot_general(
            side(coeffs_ref, s, 0),
            side(coeffs_ref, s, 1),
            (((0,), (0,)), ((), ())),
            preferred_element_type=F32,
        )


def backward_kernel(back_ref, stored_ref, out_ref, legendre_ref, sems):
    slots = legendre_ref.shape[2]
    loads = [
        pltpu.make_async_copy(stored_ref.at[j], legendre_ref.at[j], sems.at[j])
        for j in range(GROUPS)
    ]
    for load in loads:
        load.start()
    lat_count = out_ref.shape[0]
    span = back_ref.shape[2] // GROUPS
    half = ROWS // 2
    for j in range(GROUPS):
        held = back_ref[:, :, j * span : (j + 1) * span].reshape(slots, span)
        loads[j].wait()
        modes = jnp.dot(legendre_ref[j], held, preferred_element_type=F32).astype(BF16)
        for k in range(half):
            out_ref[:, :, (j * half + k) * span : (j * half + k + 1) * span] = modes[
                2 * lat_count * k : 2 * lat_count * (k + 1)
            ].reshape(lat_count, 2, span)


def synthesis_kernel(modes_ref, fourier_ref, out_ref):
    narrow = out_ref.shape[1]
    half = ROWS // 2
    modes = jnp.concatenate(
        [
            jnp.concatenate(
                [
                    modes_ref[k % 2, :, at : at + narrow]
                    for k in range(ROWS)
                    for at in [((j * half + k // 2) * 2 + p) * narrow]
                ],
                axis=1,
            )
            for j in range(GROUPS)
            for p in range(2)
        ],
        axis=0,
    )
    grad = lax.dot_general(
        modes, fourier_ref[...], (((0,), (0,)), ((), ())), preferred_element_type=F32
    ).astype(BF16)
    for k in range(ROWS):
        out_ref[k] = grad[k * narrow : (k + 1) * narrow, :]


def placing_kernel(counts_ref, rank_ref, mine_ref, theirs_ref, out_ref, empty_ref, sems):
    rank = rank_ref[0]
    odd = rank % 2
    first = counts_ref[rank - odd]
    start = odd * first
    count = jnp.where(odd == 1, 2 * ROWS - first, first)
    empty_ref[...] = jnp.zeros_like(empty_ref)
    copies = []
    for r in range(2 * ROWS):
        at = start + r
        live = r < count
        own = (at // ROWS) == odd
        target, sem = out_ref.at[r], sems.at[r]
        near = pltpu.make_async_copy(
            mine_ref.at[jnp.clip(at - odd * ROWS, 0, ROWS - 1)], target, sem
        )
        far = pltpu.make_async_copy(
            theirs_ref.at[jnp.clip(at - (1 - odd) * ROWS, 0, ROWS - 1)], target, sem
        )
        dead = pltpu.make_async_copy(empty_ref, target, sem)
        pl.when(live & own)(near.start)
        pl.when(live & jnp.logical_not(own))(far.start)
        pl.when(jnp.logical_not(live))(dead.start)
        copies.append(near)
    for copy in copies:
        copy.wait()


def on_device(field_in, cotangent, weights, row_counts, slot_degree):
    lat_count = lax.axis_size("lat")
    chan_count = lax.axis_size("chan")
    rank = lax.axis_index("lat")
    narrow = field_in.shape[1]
    held, full = weights.shape[:2]
    devices = lat_count * chan_count
    pairs = [(i, i ^ 1) for i in range(lat_count)]
    odd = rank % 2
    at_rank = jnp.reshape(rank, (1,)).astype(jnp.int32)
    table = fourier_rows(lat_count)
    by_part = jnp.asarray(table.reshape(-1, NLON))
    by_rank = jnp.asarray(table.transpose(0, 2, 1, 3).reshape(-1, NLON))
    everyone = ("chan", "lat")

    field_swap = lax.ppermute(
        lax.dynamic_slice_in_dim(field_in, (1 - odd) * ROWS, ROWS), "lat", pairs
    )
    cotan_swap = lax.ppermute(
        lax.dynamic_slice_in_dim(cotangent, (1 - odd) * ROWS, ROWS), "lat", pairs
    )
    width = 2 * ROWS * narrow
    modes = run(
        analysis_kernel,
        "analysis",
        [pltpu.HBM((lat_count, 2, GROUPS * width), BF16)],
        [row_counts, at_rank, field_in, cotangent, field_swap, cotan_swap, by_rank],
        [
            pltpu.VMEM((width, NLON), BF16),
            pltpu.VMEM(by_rank.shape, BF16),
            pltpu.VMEM((lat_count, 2, GROUPS * width), BF16),
            pltpu.SemaphoreType.DMA((4,)),
        ],
        far=(6,),
        home=pltpu.HBM,
    )
    modes = lax.all_to_all(modes, "lat", split_axis=0, concat_axis=0, tiled=True)
    modes = modes.transpose(1, 0, 2)
    slot_rows = slot_degree.reshape(lat_count, chan_count, held).transpose(1, 0, 2).reshape(-1)
    legendre, legendre_pairs = legendre_slots(at_rank, lat_count, slot_rows)
    coeffs = run(
        forward_kernel,
        "forward",
        [pltpu.VMEM((devices, held, 4 * GROUPS * narrow), BF16)],
        [at_rank, modes, legendre],
    )
    coeffs = lax.all_to_all(coeffs, everyone, split_axis=0, concat_axis=0, tiled=True)
    coeffs = coeffs.transpose(1, 0, 2).reshape(held, chan_count, lat_count, 4 * GROUPS * narrow)
    back = run(
        degree_kernel,
        "degree",
        [pltpu.HBM((devices, held, 2 * GROUPS * narrow), BF16)],
        [coeffs, weights],
        [pltpu.VMEM(weights.shape, BF16), pltpu.SemaphoreType.DMA((held,))],
        far=(1,),
    )
    back, coeffs = lax.optimization_barrier((back, coeffs))
    back = lax.all_to_all(back, everyone, split_axis=0, concat_axis=0, tiled=True)
    weight_grad = run(
        gradient_kernel, "gradient", [jax.ShapeDtypeStruct((held, full, full), F32)], [coeffs]
    )
    back, weight_grad = lax.optimization_barrier((back, weight_grad))
    modes_back = run(
        backward_kernel,
        "backward",
        [pltpu.VMEM((lat_count, 2, GROUPS * ROWS * narrow), BF16)],
        [back, legendre_pairs],
        [pltpu.VMEM(legendre_pairs.shape, BF16), pltpu.SemaphoreType.DMA((GROUPS,))],
        far=(1,),
    )
    modes_back = lax.all_to_all(modes_back, "lat", split_axis=0, concat_axis=0, tiled=True)
    grad = run(
        synthesis_kernel,
        "synthesis",
        [pltpu.VMEM((ROWS, narrow, NLON), BF16)],
        [modes_back.transpose(1, 0, 2), by_part],
    )
    grad_swap = lax.ppermute(grad, "lat", pairs)
    field_grad = run(
        placing_kernel,
        "placing",
        [jax.ShapeDtypeStruct(field_in.shape, BF16)],
        [row_counts, at_rank, grad, grad_swap],
        [pltpu.VMEM((narrow, NLON), BF16), pltpu.SemaphoreType.DMA((2 * ROWS,))],
        home=pltpu.HBM,
    )
    return field_grad, weight_grad


def solution(mesh):
    placed = (
        P("lat", "chan", None),
        P("lat", "chan", None),
        P(("lat", "chan"), None, None),
        P(),
        P(),
    )
    return jax.shard_map(
        on_device,
        mesh=mesh,
        in_specs=placed,
        out_specs=(P("lat", "chan", None), P(("lat", "chan"), None, None)),
        check_vma=False,
    )
```

```python
import math

import jax
import jax.numpy as jnp
import ml_dtypes
import numpy as np
from jax import lax
from jax.experimental import pallas as pl
from jax.experimental.pallas import tpu as pltpu
from jax.sharding import PartitionSpec as P

NLON = 720
L = 360
M = 360
LPAD = 384
ROWS = 6
FULL = 5
UNITS = 2
BLOCKS = 3
GROUPS = FULL + UNITS
RESCALE = 2.0**40
RESCALE_LOG = 40.0 * math.log(2.0)
BF16 = jnp.bfloat16
F32 = jnp.float32
VMEM_BYTES = 30 * 1024 * 1024


def block_rows(units):
    lat_count = units[0].shape[0]
    last = M - FULL * lat_count
    parts = []
    for at in range(0, BLOCKS * last, last):
        ends = [(max(at, u * lat_count), min(at + last, (u + 1) * lat_count)) for u in range(UNITS)]
        pieces = [
            units[u][lo - u * lat_count : hi - u * lat_count]
            for u, (lo, hi) in enumerate(ends)
            if lo < hi
        ]
        parts.append(pieces[0] if len(pieces) == 1 else jnp.concatenate(pieces, axis=0))
    return parts


def unit_rows(blocks, lat_count, height=1):
    last = M - FULL * lat_count
    units = []
    for u in range(UNITS):
        pieces = []
        for b in range(BLOCKS):
            lo, hi = max(b * last, u * lat_count), min((b + 1) * last, (u + 1) * lat_count)
            if lo < hi:
                pieces.append(blocks[b][(lo - b * last) * height : (hi - b * last) * height])
        dead = (u + 1) * lat_count - max(BLOCKS * last, u * lat_count)
        if dead > 0:
            pieces.append(jnp.zeros((dead * height, blocks[0].shape[1]), blocks[0].dtype))
        units.append(jnp.concatenate(pieces, axis=0))
    return units


def fourier_rows(orders):
    turns = orders[:, None] * np.arange(NLON)[None, :] % NLON
    angles = turns * (2.0 * math.pi / NLON)
    parts = np.stack([np.cos(angles), -np.sin(angles)], axis=1) / math.sqrt(NLON)
    return parts.astype(ml_dtypes.bfloat16)


def fourier_tables(lat_count):
    first = fourier_rows(np.arange(FULL * lat_count)).reshape(FULL, lat_count, 2, NLON)
    last = fourier_rows(np.arange(FULL * lat_count, M))
    by_rank = np.concatenate([first.reshape(-1, NLON), last.reshape(-1, NLON)])
    by_part = np.concatenate(
        [first.transpose(0, 2, 1, 3).reshape(-1, NLON), last.transpose(1, 0, 2).reshape(-1, NLON)]
    )
    return by_rank, by_part


def order_tables(lat_count):
    rank = np.arange(lat_count)[:, None]
    unit = np.arange(UNITS)[None, :] * lat_count + rank
    last = M - FULL * lat_count
    units = np.where(unit < BLOCKS * last, FULL * lat_count + unit % last, 10**6)
    firsts = np.arange(FULL)[None, :] * lat_count + rank
    dead = np.full((lat_count, 8 - GROUPS), 10**6)
    orders = np.concatenate([firsts, units, dead], axis=1)
    logs = [
        0.5 * math.log((2.0 * m + 1.0) / (4.0 * math.pi))
        + 0.5 * math.lgamma(2.0 * m + 1.0)
        - m * math.log(2.0)
        - math.lgamma(m + 1.0)
        for m in np.minimum(orders, M).reshape(-1).tolist()
    ]
    latitudes = ROWS * lat_count
    norms = np.array(logs).reshape(orders.shape) + 0.5 * math.log(2.0 * math.pi**2 / latitudes)
    shape = orders.shape + (128,)
    return tuple(np.broadcast_to(t[:, :, None], shape).astype(np.float32) for t in (orders, norms))


def latitude_rows(lat_count):
    grid = np.arange(lat_count)[None, :] * ROWS + np.arange(ROWS)[:, None]
    paired = grid.reshape(ROWS // 2, 2, lat_count).transpose(0, 2, 1)
    order = np.concatenate([grid.reshape(-1), paired.reshape(-1)])[None, :]
    theta = (order + 0.5) * (math.pi / (ROWS * lat_count))
    return np.cos(theta).astype(np.float32), np.log(np.sin(theta)).astype(np.float32)


def run(kernel, name, outs, args, scratch=(), home=pltpu.VMEM):
    vmem = pl.BlockSpec(memory_space=pltpu.VMEM)
    scalar = pl.BlockSpec(memory_space=pltpu.SMEM)
    specs, operands = [], []
    for arg in args:
        small = arg.dtype == jnp.int32 and arg.ndim == 1
        specs.append(scalar if small else vmem)
        operands.append(arg if small else pltpu.with_memory_space_constraint(arg, pltpu.VMEM))
    results = pl.pallas_call(
        kernel,
        out_shape=tuple(outs),
        in_specs=specs,
        out_specs=tuple(pl.BlockSpec(memory_space=home) for _ in outs),
        scratch_shapes=list(scratch),
        compiler_params=pltpu.CompilerParams(vmem_limit_bytes=VMEM_BYTES),
        name=name,
    )(*operands)
    return results if len(outs) > 1 else results[0]


def legendre_kernel(
    rank_ref, cosine_ref, logsine_ref, order_ref, norm_ref, slot_ref,
    rows_out_ref, pairs_out_ref, rows_ref,
):
    rank = rank_ref[0]
    latitudes = rows_out_ref.shape[2]
    shape = (8, 128)
    order = order_ref[rank]
    square = order * order
    tiles = cosine_ref.shape[1] // 128
    cosines, scales = [], []
    for t in range(tiles):
        lanes = slice(128 * t, 128 * (t + 1))
        cosines.append(jnp.broadcast_to(cosine_ref[:, lanes], shape))
        logsine = jnp.broadcast_to(logsine_ref[:, lanes], shape)
        scales.append(norm_ref[rank] + order * logsine + 0.5 * logsine)
    zero = jnp.zeros(shape, F32)
    one = jnp.ones(shape, F32)

    def advance(l, carry):
        degree = l.astype(F32)
        below = degree - 1.0
        upper = jnp.sqrt(
            jnp.maximum(4.0 * degree * degree - 1.0, 1.0)
            / jnp.maximum(degree * degree - square, 1.0)
        )
        lower = jnp.sqrt(
            jnp.maximum(below * below - square, 0.0)
            / jnp.maximum(4.0 * below * below - 1.0, 1.0)
        )
        rising = degree > order
        reached = degree >= order
        fresh = []
        for t in range(tiles):
            previous, current, scale = carry[3 * t : 3 * t + 3]
            value = upper * (cosines[t] * current - lower * previous)
            previous = jnp.where(rising, current, previous)
            current = jnp.where(rising, value, current)
            too_large = jnp.abs(current) > RESCALE
            factor = jnp.where(too_large, 1.0 / RESCALE, 1.0)
            previous = previous * factor
            current = current * factor
            scale = scale + jnp.where(too_large, RESCALE_LOG, 0.0)
            rows_ref[l, :, 128 * t : 128 * (t + 1)] = jnp.where(
                reached, current * jnp.exp(scale), 0.0
            )
            fresh += [previous, current, scale]
        return tuple(fresh)

    start = []
    for t in range(tiles):
        start += [zero, one, scales[t]]
    lax.fori_loop(0, L, advance, tuple(start), unroll=4)
    rows_ref[L:, :, :] = jnp.zeros((LPAD - L,) + rows_ref.shape[1:], F32)
    slots = slot_ref.shape[0]
    degrees = lax.broadcasted_iota(jnp.int32, (slots, LPAD), 1)
    pick = jnp.where((degrees == slot_ref[...]) & (degrees < L), 1.0, 0.0).astype(BF16)
    for j in range(GROUPS):
        table = rows_ref[:, j, :latitudes].astype(BF16)
        rows_out_ref[j] = jnp.dot(pick, table, preferred_element_type=F32).astype(BF16)
        table = rows_ref[:, j, latitudes:].astype(BF16)
        pairs_out_ref[j] = lax.dot_general(
            table, pick, (((0,), (1,)), ((), ())), preferred_element_type=F32
        ).astype(BF16)


def legendre_slots(at_rank, lat_count, slot_rows):
    slots = slot_rows.shape[0]
    latitudes = ROWS * lat_count
    cosine, logsine = latitude_rows(lat_count)
    orders, norms = order_tables(lat_count)
    return run(
        legendre_kernel,
        "legendre",
        [pltpu.VMEM((GROUPS, slots, latitudes), BF16), pltpu.VMEM((GROUPS, latitudes, slots), BF16)],
        [
            at_rank,
            jnp.asarray(cosine),
            jnp.asarray(logsine),
            jnp.asarray(orders),
            jnp.asarray(norms),
            slot_rows[:, None],
        ],
        [pltpu.VMEM((LPAD, 8, 2 * latitudes), F32)],
    )


def analysis_kernel(
    counts_ref, rank_ref, field_ref, cotan_ref, field_in_ref, cotan_in_ref, fourier_ref,
    out_ref, rows_ref,
):
    narrow = field_ref.shape[1]
    lat_count = out_ref.shape[0]
    width = 2 * ROWS * narrow
    rank = rank_ref[0]
    odd = rank % 2
    first = counts_ref[rank - odd]
    for k in range(ROWS):
        own = k + odd * (ROWS - first)
        mine = (own >= 0) & ((odd == 1) | (k < first))
        theirs = jnp.where(odd == 1, k, k - first)
        for w, (here, there) in enumerate(((field_ref, field_in_ref), (cotan_ref, cotan_in_ref))):
            at = slice((2 * k + w) * narrow, (2 * k + w + 1) * narrow)

            @pl.when(mine)
            def _():
                rows_ref[at, :] = here[jnp.clip(own, 0, 2 * ROWS - 1)]

            @pl.when(jnp.logical_not(mine))
            def _():
                rows_ref[at, :] = there[jnp.clip(theirs, 0, ROWS - 1)]

    contract = (((1,), (1,)), ((), ()))
    full = 2 * lat_count * FULL
    modes = lax.dot_general(
        fourier_ref[:full, :], rows_ref[...], contract, preferred_element_type=F32
    ).astype(BF16)
    for j in range(FULL):
        out_ref[:, :, j * width : (j + 1) * width] = modes[
            2 * lat_count * j : 2 * lat_count * (j + 1)
        ].reshape(lat_count, 2, width)
    third = narrow // BLOCKS
    blocks = []
    for b in range(BLOCKS):
        rows = jnp.concatenate(
            [
                rows_ref[i * narrow + b * third : i * narrow + (b + 1) * third, :]
                for i in range(2 * ROWS)
            ],
            axis=0,
        )
        blocks.append(
            lax.dot_general(
                fourier_ref[full:, :], rows, contract, preferred_element_type=F32
            ).astype(BF16)
        )
    for u, unit in enumerate(unit_rows(blocks, lat_count, 2)):
        at = FULL * width + u * (width // BLOCKS)
        out_ref[:, :, at : at + width // BLOCKS] = unit.reshape(lat_count, 2, width // BLOCKS)


def forward_kernel(rank_ref, modes_ref, legendre_ref, out_ref):
    owners = out_ref.shape[0]
    slots = legendre_ref.shape[1]
    read = write = 0
    for j in range(GROUPS):
        width = modes_ref.shape[2] // (ROWS * (FULL * BLOCKS + UNITS)) * (BLOCKS if j < FULL else 1)
        slab = jnp.concatenate(
            [
                jnp.concatenate(
                    [
                        modes_ref[p, :, read + k * width : read + (k + 1) * width]
                        for p in range(2)
                    ],
                    axis=1,
                )
                for k in range(ROWS)
            ],
            axis=0,
        )
        coeffs = jnp.dot(legendre_ref[j], slab, preferred_element_type=F32)
        lane = lax.broadcasted_iota(jnp.int32, (slots, 2 * width), 1)
        cotangent = lane // (width // 2) % 2 == 1
        doubled = jnp.where(rank_ref[0] + j == 0, 1.0, 2.0)
        coeffs = jnp.where(cotangent, coeffs * doubled, coeffs)
        out_ref[:, :, write : write + 2 * width] = coeffs.astype(BF16).reshape(
            owners, 2, 2 * width
        )
        read += ROWS * width
        write += 2 * width


def side(coeffs_ref, s, w):
    chans = coeffs_ref.shape[1]
    third = coeffs_ref.shape[3] // (4 * (FULL * BLOCKS + UNITS))
    narrow = BLOCKS * third
    rows = [
        jnp.concatenate(
            [
                coeffs_ref[s, y, :, (2 * jp + w) * narrow : (2 * jp + w + 1) * narrow]
                for y in range(chans)
            ],
            axis=1,
        )
        for jp in range(2 * FULL)
    ]
    for p in range(2):
        at = 4 * FULL * narrow + (2 * p + w) * third
        pieces = []
        for y in range(chans):
            pieces += block_rows(
                [
                    coeffs_ref[s, y, :, at + u * 4 * third : at + u * 4 * third + third]
                    for u in range(UNITS)
                ]
            )
        rows.append(jnp.concatenate(pieces, axis=1))
    return jnp.concatenate(rows, axis=0)


def degree_kernel(coeffs_ref, weights_ref, back_ref):
    chans, lat_count = coeffs_ref.shape[1:3]
    third = coeffs_ref.shape[3] // (4 * (FULL * BLOCKS + UNITS))
    narrow = BLOCKS * third
    full = 2 * FULL * lat_count
    last = M - FULL * lat_count
    for s in range(2):
        back = lax.dot_general(
            side(coeffs_ref, s, 1),
            weights_ref[s],
            (((1,), (1,)), ((), ())),
            preferred_element_type=F32,
        ).astype(BF16)
        for y in range(chans):
            lanes = slice(y * narrow, (y + 1) * narrow)
            pieces = [back[jp * lat_count : (jp + 1) * lat_count, lanes] for jp in range(2 * FULL)]
            units = []
            for p in range(2):
                rows = slice(full + p * last, full + (p + 1) * last)
                units.append(
                    unit_rows(
                        [
                            back[rows, y * narrow + b * third : y * narrow + (b + 1) * third]
                            for b in range(BLOCKS)
                        ],
                        lat_count,
                    )
                )
            pieces += [units[p][u] for u in range(UNITS) for p in range(2)]
            back_ref[y * lat_count : (y + 1) * lat_count, s, :] = jnp.concatenate(pieces, axis=1)


def gradient_kernel(coeffs_ref, grad_ref):
    for s in range(2):
        grad_ref[s] = lax.dot_general(
            side(coeffs_ref, s, 0),
            side(coeffs_ref, s, 1),
            (((0,), (0,)), ((), ())),
            preferred_element_type=F32,
        )


def backward_kernel(back_ref, legendre_ref, out_ref):
    slots = legendre_ref.shape[2]
    lat_count = out_ref.shape[0]
    third = back_ref.shape[2] // (2 * (FULL * BLOCKS + UNITS))
    half = ROWS // 2
    read = write = 0
    for j in range(GROUPS):
        span = 2 * third * (BLOCKS if j < FULL else 1)
        held = back_ref[:, :, read : read + span].reshape(slots, span)
        modes = jnp.dot(legendre_ref[j], held, preferred_element_type=F32).astype(BF16)
        for k in range(half):
            out_ref[:, :, write + k * span : write + (k + 1) * span] = modes[
                2 * lat_count * k : 2 * lat_count * (k + 1)
            ].reshape(lat_count, 2, span)
        read += span
        write += half * span


def synthesis_kernel(modes_ref, fourier_ref, out_ref):
    narrow = out_ref.shape[1]
    third = narrow // BLOCKS
    half = ROWS // 2

    def piece(k, p, j):
        width = narrow if j < FULL else third
        start = (j if j < FULL else FULL) * half * 2 * narrow + max(j - FULL, 0) * half * 2 * third
        at = start + (2 * (k // 2) + p) * width
        return modes_ref[k % 2, :, at : at + width]

    rows = [
        jnp.concatenate([piece(k, p, j) for k in range(ROWS)], axis=1)
        for j in range(FULL)
        for p in range(2)
    ]
    for p in range(2):
        blocks = []
        for k in range(ROWS):
            blocks += block_rows([piece(k, p, FULL + u) for u in range(UNITS)])
        rows.append(jnp.concatenate(blocks, axis=1))
    grad = lax.dot_general(
        jnp.concatenate(rows, axis=0),
        fourier_ref[...],
        (((0,), (0,)), ((), ())),
        preferred_element_type=F32,
    ).astype(BF16)
    for k in range(ROWS):
        out_ref[k] = grad[k * narrow : (k + 1) * narrow, :]


def placing_kernel(counts_ref, rank_ref, mine_ref, theirs_ref, out_ref, empty_ref, sems):
    rank = rank_ref[0]
    odd = rank % 2
    first = counts_ref[rank - odd]
    start = odd * first
    count = jnp.where(odd == 1, 2 * ROWS - first, first)
    empty_ref[...] = jnp.zeros_like(empty_ref)
    copies = []
    for r in range(2 * ROWS):
        at = start + r
        live = r < count
        own = (at // ROWS) == odd
        target, sem = out_ref.at[r], sems.at[r]
        near = pltpu.make_async_copy(
            mine_ref.at[jnp.clip(at - odd * ROWS, 0, ROWS - 1)], target, sem
        )
        far = pltpu.make_async_copy(
            theirs_ref.at[jnp.clip(at - (1 - odd) * ROWS, 0, ROWS - 1)], target, sem
        )
        dead = pltpu.make_async_copy(empty_ref, target, sem)
        pl.when(live & own)(near.start)
        pl.when(live & jnp.logical_not(own))(far.start)
        pl.when(jnp.logical_not(live))(dead.start)
        copies.append(near)
    for copy in copies:
        copy.wait()


def on_device(field_in, cotangent, weights, row_counts, slot_degree):
    lat_count = lax.axis_size("lat")
    chan_count = lax.axis_size("chan")
    rank = lax.axis_index("lat")
    narrow = field_in.shape[1]
    held, full = weights.shape[:2]
    devices = lat_count * chan_count
    pairs = [(i, i ^ 1) for i in range(lat_count)]
    odd = rank % 2
    at_rank = jnp.reshape(rank, (1,)).astype(jnp.int32)
    by_rank, by_part = (jnp.asarray(table) for table in fourier_tables(lat_count))
    pieces = FULL * BLOCKS + UNITS
    third = narrow // BLOCKS
    everyone = ("chan", "lat")

    field_swap = lax.ppermute(
        lax.dynamic_slice_in_dim(field_in, (1 - odd) * ROWS, ROWS), "lat", pairs
    )
    cotan_swap = lax.ppermute(
        lax.dynamic_slice_in_dim(cotangent, (1 - odd) * ROWS, ROWS), "lat", pairs
    )
    width = 2 * ROWS * narrow
    modes = run(
        analysis_kernel,
        "analysis",
        [pltpu.VMEM((lat_count, 2, pieces * width // BLOCKS), BF16)],
        [row_counts, at_rank, field_in, cotangent, field_swap, cotan_swap, by_rank],
        [pltpu.VMEM((width, NLON), BF16)],
    )
    modes = lax.all_to_all(modes, "lat", split_axis=0, concat_axis=0, tiled=True)
    modes = modes.transpose(1, 0, 2)
    slot_rows = slot_degree.reshape(lat_count, chan_count, held).transpose(1, 0, 2).reshape(-1)
    legendre, legendre_pairs = legendre_slots(at_rank, lat_count, slot_rows)
    coeffs = run(
        forward_kernel,
        "forward",
        [pltpu.VMEM((devices, held, 4 * pieces * third), BF16)],
        [at_rank, modes, legendre],
    )
    coeffs = lax.all_to_all(coeffs, everyone, split_axis=0, concat_axis=0, tiled=True)
    coeffs = coeffs.transpose(1, 0, 2).reshape(held, chan_count, lat_count, 4 * pieces * third)
    back = run(
        degree_kernel,
        "degree",
        [pltpu.VMEM((devices, held, 2 * pieces * third), BF16)],
        [coeffs, weights],
    )
    back, coeffs = lax.optimization_barrier((back, coeffs))
    back = lax.all_to_all(back, everyone, split_axis=0, concat_axis=0, tiled=True)
    weight_grad = run(
        gradient_kernel, "gradient", [jax.ShapeDtypeStruct((held, full, full), F32)], [coeffs]
    )
    back, weight_grad = lax.optimization_barrier((back, weight_grad))
    modes_back = run(
        backward_kernel,
        "backward",
        [pltpu.VMEM((lat_count, 2, ROWS * pieces * third), BF16)],
        [back, legendre_pairs],
    )
    modes_back = lax.all_to_all(modes_back, "lat", split_axis=0, concat_axis=0, tiled=True)
    grad = run(
        synthesis_kernel,
        "synthesis",
        [pltpu.VMEM((ROWS, narrow, NLON), BF16)],
        [modes_back.transpose(1, 0, 2), by_part],
    )
    grad_swap = lax.ppermute(grad, "lat", pairs)
    field_grad = run(
        placing_kernel,
        "placing",
        [jax.ShapeDtypeStruct(field_in.shape, BF16)],
        [row_counts, at_rank, grad, grad_swap],
        [pltpu.VMEM((narrow, NLON), BF16), pltpu.SemaphoreType.DMA((2 * ROWS,))],
        pl.ANY,
    )
    return field_grad, weight_grad


def solution(mesh):
    placed = (
        P("lat", "chan", None),
        P("lat", "chan", None),
        P(("lat", "chan"), None, None),
        P(),
        P(),
    )
    return jax.shard_map(
        on_device,
        mesh=mesh,
        in_specs=placed,
        out_specs=(P("lat", "chan", None), P(("lat", "chan"), None, None)),
        check_vma=False,
    )
```

```python
import math

import jax
import jax.numpy as jnp
import ml_dtypes
import numpy as np
from jax import lax
from jax.experimental import pallas as pl
from jax.experimental.pallas import tpu as pltpu
from jax.sharding import PartitionSpec as P

NLON = 720
L = 360
M = 360
LPAD = 384
ROWS = 6
FULL = 5
UNITS = 2
BLOCKS = 3
GROUPS = FULL + UNITS
RESCALE = 2.0**40
RESCALE_LOG = 40.0 * math.log(2.0)
BF16 = jnp.bfloat16
F32 = jnp.float32
VMEM_BYTES = 30 * 1024 * 1024


def block_rows(units):
    lat_count = units[0].shape[0]
    last = M - FULL * lat_count
    parts = []
    for at in range(0, BLOCKS * last, last):
        ends = [(max(at, u * lat_count), min(at + last, (u + 1) * lat_count)) for u in range(UNITS)]
        pieces = [
            units[u][lo - u * lat_count : hi - u * lat_count]
            for u, (lo, hi) in enumerate(ends)
            if lo < hi
        ]
        parts.append(pieces[0] if len(pieces) == 1 else jnp.concatenate(pieces, axis=0))
    return parts


def unit_rows(blocks, lat_count, height=1):
    last = M - FULL * lat_count
    units = []
    for u in range(UNITS):
        pieces = []
        for b in range(BLOCKS):
            lo, hi = max(b * last, u * lat_count), min((b + 1) * last, (u + 1) * lat_count)
            if lo < hi:
                pieces.append(blocks[b][(lo - b * last) * height : (hi - b * last) * height])
        dead = (u + 1) * lat_count - max(BLOCKS * last, u * lat_count)
        if dead > 0:
            pieces.append(jnp.zeros((dead * height, blocks[0].shape[1]), blocks[0].dtype))
        units.append(jnp.concatenate(pieces, axis=0))
    return units


def fourier_rows(orders):
    turns = orders[:, None] * np.arange(NLON)[None, :] % NLON
    angles = turns * (2.0 * math.pi / NLON)
    parts = np.stack([np.cos(angles), -np.sin(angles)], axis=1) / math.sqrt(NLON)
    return parts.astype(ml_dtypes.bfloat16)


def fourier_tables(lat_count):
    first = fourier_rows(np.arange(FULL * lat_count)).reshape(FULL, lat_count, 2, NLON)
    last = fourier_rows(np.arange(FULL * lat_count, M))
    by_rank = np.concatenate([first.reshape(-1, NLON), last.reshape(-1, NLON)])
    by_part = np.concatenate(
        [first.transpose(0, 2, 1, 3).reshape(-1, NLON), last.transpose(1, 0, 2).reshape(-1, NLON)]
    )
    return by_rank, by_part


def order_tables(lat_count):
    rank = np.arange(lat_count)[:, None]
    unit = np.arange(UNITS)[None, :] * lat_count + rank
    last = M - FULL * lat_count
    units = np.where(unit < BLOCKS * last, FULL * lat_count + unit % last, 10**6)
    firsts = np.arange(FULL)[None, :] * lat_count + rank
    dead = np.full((lat_count, 8 - GROUPS), 10**6)
    orders = np.concatenate([firsts, units, dead], axis=1)
    logs = [
        0.5 * math.log((2.0 * m + 1.0) / (4.0 * math.pi))
        + 0.5 * math.lgamma(2.0 * m + 1.0)
        - m * math.log(2.0)
        - math.lgamma(m + 1.0)
        for m in np.minimum(orders, M).reshape(-1).tolist()
    ]
    latitudes = ROWS * lat_count
    norms = np.array(logs).reshape(orders.shape) + 0.5 * math.log(2.0 * math.pi**2 / latitudes)
    shape = orders.shape + (128,)
    return tuple(np.broadcast_to(t[:, :, None], shape).astype(np.float32) for t in (orders, norms))


def latitude_rows(lat_count):
    grid = np.arange(lat_count)[None, :] * ROWS + np.arange(ROWS)[:, None]
    paired = grid.reshape(ROWS // 2, 2, lat_count).transpose(0, 2, 1)
    order = np.concatenate([grid.reshape(-1), paired.reshape(-1)])[None, :]
    theta = (order + 0.5) * (math.pi / (ROWS * lat_count))
    return np.cos(theta).astype(np.float32), np.log(np.sin(theta)).astype(np.float32)


def run(kernel, name, outs, args, scratch=(), home=pltpu.VMEM, far=()):
    specs, operands = [], []
    for at, arg in enumerate(args):
        if arg.dtype == jnp.int32 and arg.ndim == 1:
            space = pltpu.SMEM
        else:
            space = pltpu.HBM if at in far else pltpu.VMEM
            arg = pltpu.with_memory_space_constraint(arg, space)
        specs.append(pl.BlockSpec(memory_space=space))
        operands.append(arg)
    results = pl.pallas_call(
        kernel,
        out_shape=tuple(outs),
        in_specs=specs,
        out_specs=tuple(pl.BlockSpec(memory_space=home) for _ in outs),
        scratch_shapes=list(scratch),
        compiler_params=pltpu.CompilerParams(vmem_limit_bytes=VMEM_BYTES),
        name=name,
    )(*operands)
    return results if len(outs) > 1 else results[0]


def loading_kernel(stored_ref, out_ref, sem):
    copy = pltpu.make_async_copy(stored_ref, out_ref, sem)
    copy.start()
    copy.wait()


def loaded(array, name):
    return run(
        loading_kernel,
        name,
        [pltpu.VMEM(array.shape, array.dtype)],
        [array],
        [pltpu.SemaphoreType.DMA],
        far=(0,),
    )


def legendre_kernel(
    rank_ref, cosine_ref, logsine_ref, order_ref, norm_ref, slot_ref,
    rows_out_ref, pairs_out_ref, rows_ref,
):
    rank = rank_ref[0]
    latitudes = rows_out_ref.shape[2]
    shape = (8, 128)
    order = order_ref[rank]
    square = order * order
    tiles = cosine_ref.shape[1] // 128
    cosines, scales = [], []
    for t in range(tiles):
        lanes = slice(128 * t, 128 * (t + 1))
        cosines.append(jnp.broadcast_to(cosine_ref[:, lanes], shape))
        logsine = jnp.broadcast_to(logsine_ref[:, lanes], shape)
        scales.append(norm_ref[rank] + order * logsine + 0.5 * logsine)
    zero = jnp.zeros(shape, F32)
    one = jnp.ones(shape, F32)

    def advance(l, carry):
        degree = l.astype(F32)
        below = degree - 1.0
        upper = jnp.sqrt(
            jnp.maximum(4.0 * degree * degree - 1.0, 1.0)
            / jnp.maximum(degree * degree - square, 1.0)
        )
        lower = jnp.sqrt(
            jnp.maximum(below * below - square, 0.0)
            / jnp.maximum(4.0 * below * below - 1.0, 1.0)
        )
        rising = degree > order
        reached = degree >= order
        fresh = []
        for t in range(tiles):
            previous, current, scale = carry[3 * t : 3 * t + 3]
            value = upper * (cosines[t] * current - lower * previous)
            previous = jnp.where(rising, current, previous)
            current = jnp.where(rising, value, current)
            too_large = jnp.abs(current) > RESCALE
            factor = jnp.where(too_large, 1.0 / RESCALE, 1.0)
            previous = previous * factor
            current = current * factor
            scale = scale + jnp.where(too_large, RESCALE_LOG, 0.0)
            rows_ref[l, :, 128 * t : 128 * (t + 1)] = jnp.where(
                reached, current * jnp.exp(scale), 0.0
            )
            fresh += [previous, current, scale]
        return tuple(fresh)

    start = []
    for t in range(tiles):
        start += [zero, one, scales[t]]
    lax.fori_loop(0, L, advance, tuple(start), unroll=4)
    rows_ref[L:, :, :] = jnp.zeros((LPAD - L,) + rows_ref.shape[1:], F32)
    slots = slot_ref.shape[0]
    degrees = lax.broadcasted_iota(jnp.int32, (slots, LPAD), 1)
    pick = jnp.where((degrees == slot_ref[...]) & (degrees < L), 1.0, 0.0).astype(BF16)
    for j in range(GROUPS):
        table = rows_ref[:, j, :latitudes].astype(BF16)
        rows_out_ref[j] = jnp.dot(pick, table, preferred_element_type=F32).astype(BF16)
        table = rows_ref[:, j, latitudes:].astype(BF16)
        pairs_out_ref[j] = lax.dot_general(
            table, pick, (((0,), (1,)), ((), ())), preferred_element_type=F32
        ).astype(BF16)


def legendre_slots(at_rank, lat_count, slot_rows):
    slots = slot_rows.shape[0]
    latitudes = ROWS * lat_count
    cosine, logsine = latitude_rows(lat_count)
    orders, norms = order_tables(lat_count)
    return run(
        legendre_kernel,
        "legendre",
        [pltpu.VMEM((GROUPS, slots, latitudes), BF16), pltpu.VMEM((GROUPS, latitudes, slots), BF16)],
        [
            at_rank,
            jnp.asarray(cosine),
            jnp.asarray(logsine),
            jnp.asarray(orders),
            jnp.asarray(norms),
            slot_rows[:, None],
        ],
        [pltpu.VMEM((LPAD, 8, 2 * latitudes), F32)],
    )


def analysis_kernel(
    counts_ref, rank_ref, field_ref, cotan_ref, field_in_ref, cotan_in_ref, fourier_ref,
    out_ref, rows_ref, held_ref, sems,
):
    narrow = field_ref.shape[1]
    lat_count = out_ref.shape[0]
    width = 2 * ROWS * narrow
    rank = rank_ref[0]
    odd = rank % 2
    first = counts_ref[rank - odd]
    for k in range(ROWS):
        own = k + odd * (ROWS - first)
        mine = (own >= 0) & ((odd == 1) | (k < first))
        theirs = jnp.where(odd == 1, k, k - first)
        for w, (here, there) in enumerate(((field_ref, field_in_ref), (cotan_ref, cotan_in_ref))):
            at = slice((2 * k + w) * narrow, (2 * k + w + 1) * narrow)

            @pl.when(mine)
            def _():
                rows_ref[at, :] = here[jnp.clip(own, 0, 2 * ROWS - 1)]

            @pl.when(jnp.logical_not(mine))
            def _():
                rows_ref[at, :] = there[jnp.clip(theirs, 0, ROWS - 1)]

    contract = (((1,), (1,)), ((), ()))
    full = 2 * lat_count * FULL
    stores = []

    def send(lo, hi):
        lanes = pl.ds(lo, hi - lo)
        store = pltpu.make_async_copy(
            held_ref.at[:, :, lanes], out_ref.at[:, :, lanes], sems.at[len(stores)]
        )
        store.start()
        stores.append(store)

    step = 2
    for j0 in range(0, FULL, step):
        j1 = min(j0 + step, FULL)
        modes = lax.dot_general(
            fourier_ref[2 * lat_count * j0 : 2 * lat_count * j1, :],
            rows_ref[...],
            contract,
            preferred_element_type=F32,
        ).astype(BF16)
        for j in range(j0, j1):
            held_ref[:, :, j * width : (j + 1) * width] = modes[
                2 * lat_count * (j - j0) : 2 * lat_count * (j - j0 + 1)
            ].reshape(lat_count, 2, width)
        if j1 < FULL:
            send(j0 * width, j1 * width)
    third = narrow // BLOCKS
    blocks = []
    for b in range(BLOCKS):
        rows = jnp.concatenate(
            [
                rows_ref[i * narrow + b * third : i * narrow + (b + 1) * third, :]
                for i in range(2 * ROWS)
            ],
            axis=0,
        )
        blocks.append(
            lax.dot_general(
                fourier_ref[full:, :], rows, contract, preferred_element_type=F32
            ).astype(BF16)
        )
    for u, unit in enumerate(unit_rows(blocks, lat_count, 2)):
        at = FULL * width + u * (width // BLOCKS)
        held_ref[:, :, at : at + width // BLOCKS] = unit.reshape(lat_count, 2, width // BLOCKS)
    send((FULL - 1) // step * step * width, out_ref.shape[2])
    for store in stores:
        store.wait()


def forward_kernel(rank_ref, modes_ref, legendre_ref, stored_ref, out_ref, weights_ref, sem):
    load = pltpu.make_async_copy(stored_ref, weights_ref, sem)
    load.start()
    owners = out_ref.shape[0]
    slots = legendre_ref.shape[1]
    read = write = 0
    for j in range(GROUPS):
        width = modes_ref.shape[2] // (ROWS * (FULL * BLOCKS + UNITS)) * (BLOCKS if j < FULL else 1)
        slab = jnp.concatenate(
            [
                jnp.concatenate(
                    [
                        modes_ref[p, :, read + k * width : read + (k + 1) * width]
                        for p in range(2)
                    ],
                    axis=1,
                )
                for k in range(ROWS)
            ],
            axis=0,
        )
        coeffs = jnp.dot(legendre_ref[j], slab, preferred_element_type=F32)
        lane = lax.broadcasted_iota(jnp.int32, (slots, 2 * width), 1)
        cotangent = lane // (width // 2) % 2 == 1
        doubled = jnp.where(rank_ref[0] + j == 0, 1.0, 2.0)
        coeffs = jnp.where(cotangent, coeffs * doubled, coeffs)
        out_ref[:, :, write : write + 2 * width] = coeffs.astype(BF16).reshape(
            owners, 2, 2 * width
        )
        read += ROWS * width
        write += 2 * width
    load.wait()


def side(coeffs_ref, s, w):
    chans = coeffs_ref.shape[1]
    third = coeffs_ref.shape[3] // (4 * (FULL * BLOCKS + UNITS))
    narrow = BLOCKS * third
    rows = [
        jnp.concatenate(
            [
                coeffs_ref[s, y, :, (2 * jp + w) * narrow : (2 * jp + w + 1) * narrow]
                for y in range(chans)
            ],
            axis=1,
        )
        for jp in range(2 * FULL)
    ]
    for p in range(2):
        at = 4 * FULL * narrow + (2 * p + w) * third
        pieces = []
        for y in range(chans):
            pieces += block_rows(
                [
                    coeffs_ref[s, y, :, at + u * 4 * third : at + u * 4 * third + third]
                    for u in range(UNITS)
                ]
            )
        rows.append(jnp.concatenate(pieces, axis=1))
    return jnp.concatenate(rows, axis=0)


def degree_kernel(coeffs_ref, weights_ref, back_ref):
    chans, lat_count = coeffs_ref.shape[1:3]
    third = coeffs_ref.shape[3] // (4 * (FULL * BLOCKS + UNITS))
    narrow = BLOCKS * third
    full = 2 * FULL * lat_count
    last = M - FULL * lat_count
    for s in range(2):
        back = lax.dot_general(
            side(coeffs_ref, s, 1),
            weights_ref[s],
            (((1,), (1,)), ((), ())),
            preferred_element_type=F32,
        ).astype(BF16)
        for y in range(chans):
            lanes = slice(y * narrow, (y + 1) * narrow)
            pieces = [back[jp * lat_count : (jp + 1) * lat_count, lanes] for jp in range(2 * FULL)]
            units = []
            for p in range(2):
                rows = slice(full + p * last, full + (p + 1) * last)
                units.append(
                    unit_rows(
                        [
                            back[rows, y * narrow + b * third : y * narrow + (b + 1) * third]
                            for b in range(BLOCKS)
                        ],
                        lat_count,
                    )
                )
            pieces += [units[p][u] for u in range(UNITS) for p in range(2)]
            back_ref[y * lat_count : (y + 1) * lat_count, s, :] = jnp.concatenate(pieces, axis=1)


def gradient_kernel(coeffs_ref, grad_ref):
    for s in range(2):
        grad_ref[s] = lax.dot_general(
            side(coeffs_ref, s, 0),
            side(coeffs_ref, s, 1),
            (((0,), (0,)), ((), ())),
            preferred_element_type=F32,
        )


def backward_kernel(back_ref, legendre_ref, out_ref):
    slots = legendre_ref.shape[2]
    lat_count = out_ref.shape[0]
    third = back_ref.shape[2] // (2 * (FULL * BLOCKS + UNITS))
    half = ROWS // 2
    read = write = 0
    for j in range(GROUPS):
        span = 2 * third * (BLOCKS if j < FULL else 1)
        held = back_ref[:, :, read : read + span].reshape(slots, span)
        modes = jnp.dot(legendre_ref[j], held, preferred_element_type=F32).astype(BF16)
        for k in range(half):
            out_ref[:, :, write + k * span : write + (k + 1) * span] = modes[
                2 * lat_count * k : 2 * lat_count * (k + 1)
            ].reshape(lat_count, 2, span)
        read += span
        write += half * span


def synthesis_kernel(modes_ref, fourier_ref, out_ref):
    narrow = out_ref.shape[1]
    third = narrow // BLOCKS
    half = ROWS // 2

    def piece(k, p, j):
        width = narrow if j < FULL else third
        start = (j if j < FULL else FULL) * half * 2 * narrow + max(j - FULL, 0) * half * 2 * third
        at = start + (2 * (k // 2) + p) * width
        return modes_ref[k % 2, :, at : at + width]

    rows = [
        jnp.concatenate([piece(k, p, j) for k in range(ROWS)], axis=1)
        for j in range(FULL)
        for p in range(2)
    ]
    for p in range(2):
        blocks = []
        for k in range(ROWS):
            blocks += block_rows([piece(k, p, FULL + u) for u in range(UNITS)])
        rows.append(jnp.concatenate(blocks, axis=1))
    grad = lax.dot_general(
        jnp.concatenate(rows, axis=0),
        fourier_ref[...],
        (((0,), (0,)), ((), ())),
        preferred_element_type=F32,
    ).astype(BF16)
    for k in range(ROWS):
        out_ref[k] = grad[k * narrow : (k + 1) * narrow, :]


def placing_kernel(counts_ref, rank_ref, mine_ref, theirs_ref, out_ref, empty_ref, sems):
    rank = rank_ref[0]
    odd = rank % 2
    first = counts_ref[rank - odd]
    start = odd * first
    count = jnp.where(odd == 1, 2 * ROWS - first, first)
    empty_ref[...] = jnp.zeros_like(empty_ref)
    copies = []
    for r in range(2 * ROWS):
        at = start + r
        live = r < count
        own = (at // ROWS) == odd
        target, sem = out_ref.at[r], sems.at[r]
        near = pltpu.make_async_copy(
            mine_ref.at[jnp.clip(at - odd * ROWS, 0, ROWS - 1)], target, sem
        )
        far = pltpu.make_async_copy(
            theirs_ref.at[jnp.clip(at - (1 - odd) * ROWS, 0, ROWS - 1)], target, sem
        )
        dead = pltpu.make_async_copy(empty_ref, target, sem)
        pl.when(live & own)(near.start)
        pl.when(live & jnp.logical_not(own))(far.start)
        pl.when(jnp.logical_not(live))(dead.start)
        copies.append(near)
    for copy in copies:
        copy.wait()


def on_device(field_in, cotangent, weights, row_counts, slot_degree):
    lat_count = lax.axis_size("lat")
    chan_count = lax.axis_size("chan")
    rank = lax.axis_index("lat")
    narrow = field_in.shape[1]
    held, full = weights.shape[:2]
    devices = lat_count * chan_count
    pairs = [(i, i ^ 1) for i in range(lat_count)]
    odd = rank % 2
    at_rank = jnp.reshape(rank, (1,)).astype(jnp.int32)
    by_rank, by_part = (jnp.asarray(table) for table in fourier_tables(lat_count))
    pieces = FULL * BLOCKS + UNITS
    third = narrow // BLOCKS
    everyone = ("chan", "lat")

    field_send = lax.dynamic_slice_in_dim(field_in, (1 - odd) * ROWS, ROWS)
    cotan_send = lax.dynamic_slice_in_dim(cotangent, (1 - odd) * ROWS, ROWS)
    field_send, by_rank = lax.optimization_barrier((field_send, by_rank))
    field_swap = lax.ppermute(field_send, "lat", pairs)
    cotan_swap = lax.ppermute(cotan_send, "lat", pairs)
    by_rank = loaded(by_rank, "fourier")
    width = 2 * ROWS * narrow
    modes = run(
        analysis_kernel,
        "analysis",
        [pltpu.HBM((lat_count, 2, pieces * width // BLOCKS), BF16)],
        [row_counts, at_rank, field_in, cotangent, field_swap, cotan_swap, by_rank],
        [
            pltpu.VMEM((width, NLON), BF16),
            pltpu.VMEM((lat_count, 2, pieces * width // BLOCKS), BF16),
            pltpu.SemaphoreType.DMA((GROUPS,)),
        ],
        home=pltpu.HBM,
    )
    modes = lax.all_to_all(modes, "lat", split_axis=0, concat_axis=0, tiled=True)
    modes = modes.transpose(1, 0, 2)
    slot_rows = slot_degree.reshape(lat_count, chan_count, held).transpose(1, 0, 2).reshape(-1)
    legendre, legendre_pairs = legendre_slots(at_rank, lat_count, slot_rows)
    coeffs, weights = run(
        forward_kernel,
        "forward",
        [
            pltpu.VMEM((devices, held, 4 * pieces * third), BF16),
            pltpu.VMEM(weights.shape, BF16),
        ],
        [at_rank, modes, legendre, weights],
        [pltpu.SemaphoreType.DMA],
        far=(3,),
    )
    coeffs = lax.all_to_all(coeffs, everyone, split_axis=0, concat_axis=0, tiled=True)
    coeffs = coeffs.transpose(1, 0, 2).reshape(held, chan_count, lat_count, 4 * pieces * third)
    back = run(
        degree_kernel,
        "degree",
        [pltpu.VMEM((devices, held, 2 * pieces * third), BF16)],
        [coeffs, weights],
    )
    back = lax.all_to_all(back, everyone, split_axis=0, concat_axis=0, tiled=True)
    modes_back = run(
        backward_kernel,
        "backward",
        [pltpu.VMEM((lat_count, 2, ROWS * pieces * third), BF16)],
        [back, legendre_pairs],
    )
    modes_back = lax.all_to_all(modes_back, "lat", split_axis=0, concat_axis=0, tiled=True)
    grad = run(
        synthesis_kernel,
        "synthesis",
        [pltpu.VMEM((ROWS, narrow, NLON), BF16)],
        [modes_back.transpose(1, 0, 2), by_part],
    )
    grad, coeffs = lax.optimization_barrier((grad, coeffs))
    grad_swap = lax.ppermute(grad, "lat", pairs)
    weight_grad = run(
        gradient_kernel, "gradient", [jax.ShapeDtypeStruct((held, full, full), F32)], [coeffs]
    )
    grad_swap, weight_grad = lax.optimization_barrier((grad_swap, weight_grad))
    field_grad = run(
        placing_kernel,
        "placing",
        [jax.ShapeDtypeStruct(field_in.shape, BF16)],
        [row_counts, at_rank, grad, grad_swap],
        [pltpu.VMEM((narrow, NLON), BF16), pltpu.SemaphoreType.DMA((2 * ROWS,))],
        pl.ANY,
    )
    return field_grad, weight_grad


def solution(mesh):
    placed = (
        P("lat", "chan", None),
        P("lat", "chan", None),
        P(("lat", "chan"), None, None),
        P(),
        P(),
    )
    return jax.shard_map(
        on_device,
        mesh=mesh,
        in_specs=placed,
        out_specs=(P("lat", "chan", None), P(("lat", "chan"), None, None)),
        check_vma=False,
    )
```

```python
import math

import jax
import jax.numpy as jnp
import ml_dtypes
import numpy as np
from jax import lax
from jax.experimental import pallas as pl
from jax.experimental.pallas import tpu as pltpu
from jax.sharding import PartitionSpec as P

NLON = 720
L = 360
M = 360
LPAD = 384
ROWS = 6
FULL = 5
UNITS = 2
BLOCKS = 3
GROUPS = FULL + UNITS
RESCALE = 2.0**40
RESCALE_LOG = 40.0 * math.log(2.0)
BF16 = jnp.bfloat16
F32 = jnp.float32
VMEM_BYTES = 30 * 1024 * 1024


def block_rows(units):
    lat_count = units[0].shape[0]
    last = M - FULL * lat_count
    parts = []
    for at in range(0, BLOCKS * last, last):
        ends = [(max(at, u * lat_count), min(at + last, (u + 1) * lat_count)) for u in range(UNITS)]
        pieces = [
            units[u][lo - u * lat_count : hi - u * lat_count]
            for u, (lo, hi) in enumerate(ends)
            if lo < hi
        ]
        parts.append(pieces[0] if len(pieces) == 1 else jnp.concatenate(pieces, axis=0))
    return parts


def unit_rows(blocks, lat_count, height=1):
    last = M - FULL * lat_count
    units = []
    for u in range(UNITS):
        pieces = []
        for b in range(BLOCKS):
            lo, hi = max(b * last, u * lat_count), min((b + 1) * last, (u + 1) * lat_count)
            if lo < hi:
                pieces.append(blocks[b][(lo - b * last) * height : (hi - b * last) * height])
        dead = (u + 1) * lat_count - max(BLOCKS * last, u * lat_count)
        if dead > 0:
            pieces.append(jnp.zeros((dead * height, blocks[0].shape[1]), blocks[0].dtype))
        units.append(jnp.concatenate(pieces, axis=0))
    return units


def fourier_rows(orders):
    turns = orders[:, None] * np.arange(NLON)[None, :] % NLON
    angles = turns * (2.0 * math.pi / NLON)
    parts = np.stack([np.cos(angles), -np.sin(angles)], axis=1) / math.sqrt(NLON)
    return parts.astype(ml_dtypes.bfloat16)


def fourier_tables(lat_count):
    first = fourier_rows(np.arange(FULL * lat_count)).reshape(FULL, lat_count, 2, NLON)
    last = fourier_rows(np.arange(FULL * lat_count, M))
    by_rank = np.concatenate([first.reshape(-1, NLON), last.reshape(-1, NLON)])
    by_part = np.concatenate(
        [first.transpose(0, 2, 1, 3).reshape(-1, NLON), last.transpose(1, 0, 2).reshape(-1, NLON)]
    )
    return by_rank, by_part


def order_tables(lat_count):
    rank = np.arange(lat_count)[:, None]
    unit = np.arange(UNITS)[None, :] * lat_count + rank
    last = M - FULL * lat_count
    units = np.where(unit < BLOCKS * last, FULL * lat_count + unit % last, 10**6)
    firsts = np.arange(FULL)[None, :] * lat_count + rank
    dead = np.full((lat_count, 8 - GROUPS), 10**6)
    orders = np.concatenate([firsts, units, dead], axis=1)
    logs = [
        0.5 * math.log((2.0 * m + 1.0) / (4.0 * math.pi))
        + 0.5 * math.lgamma(2.0 * m + 1.0)
        - m * math.log(2.0)
        - math.lgamma(m + 1.0)
        for m in np.minimum(orders, M).reshape(-1).tolist()
    ]
    latitudes = ROWS * lat_count
    norms = np.array(logs).reshape(orders.shape) + 0.5 * math.log(2.0 * math.pi**2 / latitudes)
    shape = orders.shape + (128,)
    return tuple(np.broadcast_to(t[:, :, None], shape).astype(np.float32) for t in (orders, norms))


def latitude_rows(lat_count):
    grid = np.arange(lat_count)[None, :] * ROWS + np.arange(ROWS)[:, None]
    paired = grid.reshape(ROWS // 2, 2, lat_count).transpose(0, 2, 1)
    order = np.concatenate([grid.reshape(-1), paired.reshape(-1)])[None, :]
    theta = (order + 0.5) * (math.pi / (ROWS * lat_count))
    return np.cos(theta).astype(np.float32), np.log(np.sin(theta)).astype(np.float32)


def run(kernel, name, outs, args, scratch=(), home=pltpu.VMEM, far=(), aliases={}):
    specs, operands = [], []
    for at, arg in enumerate(args):
        if arg.dtype == jnp.int32 and arg.ndim == 1:
            space = pltpu.SMEM
        else:
            space = pltpu.HBM if at in far else pltpu.VMEM
            arg = pltpu.with_memory_space_constraint(arg, space)
        specs.append(pl.BlockSpec(memory_space=space))
        operands.append(arg)
    results = pl.pallas_call(
        kernel,
        out_shape=tuple(outs),
        in_specs=specs,
        out_specs=tuple(pl.BlockSpec(memory_space=home) for _ in outs),
        scratch_shapes=list(scratch),
        input_output_aliases=aliases,
        compiler_params=pltpu.CompilerParams(vmem_limit_bytes=VMEM_BYTES),
        name=name,
    )(*operands)
    return results if len(outs) > 1 else results[0]


def loading_kernel(stored_ref, out_ref, sem):
    copy = pltpu.make_async_copy(stored_ref, out_ref, sem)
    copy.start()
    copy.wait()


def loaded(array, name):
    return run(
        loading_kernel,
        name,
        [pltpu.VMEM(array.shape, array.dtype)],
        [array],
        [pltpu.SemaphoreType.DMA],
        far=(0,),
    )


def legendre_kernel(
    rank_ref, cosine_ref, logsine_ref, order_ref, norm_ref, slot_ref,
    rows_out_ref, pairs_out_ref, rows_ref,
):
    rank = rank_ref[0]
    latitudes = rows_out_ref.shape[2]
    shape = (8, 128)
    order = order_ref[rank]
    square = order * order
    tiles = cosine_ref.shape[1] // 128
    cosines, scales = [], []
    for t in range(tiles):
        lanes = slice(128 * t, 128 * (t + 1))
        cosines.append(jnp.broadcast_to(cosine_ref[:, lanes], shape))
        logsine = jnp.broadcast_to(logsine_ref[:, lanes], shape)
        scales.append(norm_ref[rank] + order * logsine + 0.5 * logsine)
    zero = jnp.zeros(shape, F32)
    one = jnp.ones(shape, F32)

    def advance(l, carry):
        degree = l.astype(F32)
        below = degree - 1.0
        upper = jnp.sqrt(
            jnp.maximum(4.0 * degree * degree - 1.0, 1.0)
            / jnp.maximum(degree * degree - square, 1.0)
        )
        lower = jnp.sqrt(
            jnp.maximum(below * below - square, 0.0)
            / jnp.maximum(4.0 * below * below - 1.0, 1.0)
        )
        rising = degree > order
        reached = degree >= order
        fresh = []
        for t in range(tiles):
            previous, current, scale = carry[3 * t : 3 * t + 3]
            value = upper * (cosines[t] * current - lower * previous)
            previous = jnp.where(rising, current, previous)
            current = jnp.where(rising, value, current)
            too_large = jnp.abs(current) > RESCALE
            factor = jnp.where(too_large, 1.0 / RESCALE, 1.0)
            previous = previous * factor
            current = current * factor
            scale = scale + jnp.where(too_large, RESCALE_LOG, 0.0)
            rows_ref[l, :, 128 * t : 128 * (t + 1)] = jnp.where(
                reached, current * jnp.exp(scale), 0.0
            )
            fresh += [previous, current, scale]
        return tuple(fresh)

    start = []
    for t in range(tiles):
        start += [zero, one, scales[t]]
    lax.fori_loop(0, L, advance, tuple(start), unroll=4)
    rows_ref[L:, :, :] = jnp.zeros((LPAD - L,) + rows_ref.shape[1:], F32)
    slots = slot_ref.shape[0]
    degrees = lax.broadcasted_iota(jnp.int32, (slots, LPAD), 1)
    pick = jnp.where((degrees == slot_ref[...]) & (degrees < L), 1.0, 0.0).astype(BF16)
    for j in range(GROUPS):
        table = rows_ref[:, j, :latitudes].astype(BF16)
        rows_out_ref[j] = jnp.dot(pick, table, preferred_element_type=F32).astype(BF16)
        table = rows_ref[:, j, latitudes:].astype(BF16)
        pairs_out_ref[j] = lax.dot_general(
            table, pick, (((0,), (1,)), ((), ())), preferred_element_type=F32
        ).astype(BF16)


def legendre_slots(at_rank, lat_count, slot_rows):
    slots = slot_rows.shape[0]
    latitudes = ROWS * lat_count
    cosine, logsine = latitude_rows(lat_count)
    orders, norms = order_tables(lat_count)
    return run(
        legendre_kernel,
        "legendre",
        [pltpu.VMEM((GROUPS, slots, latitudes), BF16), pltpu.HBM((GROUPS, latitudes, slots), BF16)],
        [
            at_rank,
            jnp.asarray(cosine),
            jnp.asarray(logsine),
            jnp.asarray(orders),
            jnp.asarray(norms),
            slot_rows[:, None],
        ],
        [pltpu.VMEM((LPAD, 8, 2 * latitudes), F32)],
    )


def analysis_kernel(
    counts_ref, rank_ref, field_ref, cotan_ref, field_in_ref, cotan_in_ref, fourier_ref,
    out_ref, rows_ref, held_ref, sems,
):
    narrow = field_ref.shape[1]
    lat_count = out_ref.shape[0]
    width = 2 * ROWS * narrow
    rank = rank_ref[0]
    odd = rank % 2
    first = counts_ref[rank - odd]
    for k in range(ROWS):
        own = k + odd * (ROWS - first)
        mine = (own >= 0) & ((odd == 1) | (k < first))
        theirs = jnp.where(odd == 1, k, k - first)
        for w, (here, there) in enumerate(((field_ref, field_in_ref), (cotan_ref, cotan_in_ref))):
            at = slice((2 * k + w) * narrow, (2 * k + w + 1) * narrow)

            @pl.when(mine)
            def _():
                rows_ref[at, :] = here[jnp.clip(own, 0, 2 * ROWS - 1)]

            @pl.when(jnp.logical_not(mine))
            def _():
                rows_ref[at, :] = there[jnp.clip(theirs, 0, ROWS - 1)]

    contract = (((1,), (1,)), ((), ()))
    full = 2 * lat_count * FULL
    stores = []

    def send(lo, hi):
        lanes = pl.ds(lo, hi - lo)
        store = pltpu.make_async_copy(
            held_ref.at[:, :, lanes], out_ref.at[:, :, lanes], sems.at[len(stores)]
        )
        store.start()
        stores.append(store)

    third = narrow // BLOCKS
    blocks = []
    for b in range(BLOCKS):
        rows = jnp.concatenate(
            [
                rows_ref[i * narrow + b * third : i * narrow + (b + 1) * third, :]
                for i in range(2 * ROWS)
            ],
            axis=0,
        )
        blocks.append(
            lax.dot_general(
                fourier_ref[full:, :], rows, contract, preferred_element_type=F32
            ).astype(BF16)
        )
    for u, unit in enumerate(unit_rows(blocks, lat_count, 2)):
        at = FULL * width + u * (width // BLOCKS)
        held_ref[:, :, at : at + width // BLOCKS] = unit.reshape(lat_count, 2, width // BLOCKS)
    send(FULL * width, out_ref.shape[2])
    for j0, j1 in ((0, 2), (2, 4), (4, FULL)):
        modes = lax.dot_general(
            fourier_ref[2 * lat_count * j0 : 2 * lat_count * j1, :],
            rows_ref[...],
            contract,
            preferred_element_type=F32,
        ).astype(BF16)
        for j in range(j0, j1):
            held_ref[:, :, j * width : (j + 1) * width] = modes[
                2 * lat_count * (j - j0) : 2 * lat_count * (j - j0 + 1)
            ].reshape(lat_count, 2, width)
        send(j0 * width, j1 * width)
    for store in stores:
        store.wait()


def forward_kernel(
    rank_ref, modes_ref, legendre_ref, stored_ref, stored_pairs_ref,
    out_ref, weights_ref, pairs_ref, sems,
):
    loads = [
        pltpu.make_async_copy(stored_pairs_ref, pairs_ref, sems.at[0]),
        pltpu.make_async_copy(stored_ref, weights_ref, sems.at[1]),
    ]
    for load in loads:
        load.start()
    owners = out_ref.shape[0]
    slots = legendre_ref.shape[1]
    read = write = 0
    for j in range(GROUPS):
        width = modes_ref.shape[2] // (ROWS * (FULL * BLOCKS + UNITS)) * (BLOCKS if j < FULL else 1)
        slab = jnp.concatenate(
            [
                jnp.concatenate(
                    [
                        modes_ref[p, :, read + k * width : read + (k + 1) * width]
                        for p in range(2)
                    ],
                    axis=1,
                )
                for k in range(ROWS)
            ],
            axis=0,
        )
        coeffs = jnp.dot(legendre_ref[j], slab, preferred_element_type=F32)
        lane = lax.broadcasted_iota(jnp.int32, (slots, 2 * width), 1)
        cotangent = lane // (width // 2) % 2 == 1
        doubled = jnp.where(rank_ref[0] + j == 0, 1.0, 2.0)
        coeffs = jnp.where(cotangent, coeffs * doubled, coeffs)
        out_ref[:, :, write : write + 2 * width] = coeffs.astype(BF16).reshape(
            owners, 2, 2 * width
        )
        read += ROWS * width
        write += 2 * width
    for load in loads:
        load.wait()


def side(coeffs_ref, s, w):
    chans = coeffs_ref.shape[1]
    third = coeffs_ref.shape[3] // (4 * (FULL * BLOCKS + UNITS))
    narrow = BLOCKS * third
    rows = [
        jnp.concatenate(
            [
                coeffs_ref[s, y, :, (2 * jp + w) * narrow : (2 * jp + w + 1) * narrow]
                for y in range(chans)
            ],
            axis=1,
        )
        for jp in range(2 * FULL)
    ]
    for p in range(2):
        at = 4 * FULL * narrow + (2 * p + w) * third
        pieces = []
        for y in range(chans):
            pieces += block_rows(
                [
                    coeffs_ref[s, y, :, at + u * 4 * third : at + u * 4 * third + third]
                    for u in range(UNITS)
                ]
            )
        rows.append(jnp.concatenate(pieces, axis=1))
    return jnp.concatenate(rows, axis=0)


def degree_kernel(coeffs_ref, weights_ref, back_ref):
    chans, lat_count = coeffs_ref.shape[1:3]
    third = coeffs_ref.shape[3] // (4 * (FULL * BLOCKS + UNITS))
    narrow = BLOCKS * third
    full = 2 * FULL * lat_count
    last = M - FULL * lat_count
    for s in range(2):
        back = lax.dot_general(
            side(coeffs_ref, s, 1),
            weights_ref[s],
            (((1,), (1,)), ((), ())),
            preferred_element_type=F32,
        ).astype(BF16)
        for y in range(chans):
            lanes = slice(y * narrow, (y + 1) * narrow)
            pieces = [back[jp * lat_count : (jp + 1) * lat_count, lanes] for jp in range(2 * FULL)]
            units = []
            for p in range(2):
                rows = slice(full + p * last, full + (p + 1) * last)
                units.append(
                    unit_rows(
                        [
                            back[rows, y * narrow + b * third : y * narrow + (b + 1) * third]
                            for b in range(BLOCKS)
                        ],
                        lat_count,
                    )
                )
            pieces += [units[p][u] for u in range(UNITS) for p in range(2)]
            back_ref[y * lat_count : (y + 1) * lat_count, s, :] = jnp.concatenate(pieces, axis=1)


def backward_kernel(back_ref, legendre_ref, out_ref):
    slots = legendre_ref.shape[2]
    lat_count = out_ref.shape[0]
    third = back_ref.shape[2] // (2 * (FULL * BLOCKS + UNITS))
    half = ROWS // 2
    read = write = 0
    for j in range(GROUPS):
        span = 2 * third * (BLOCKS if j < FULL else 1)
        held = back_ref[:, :, read : read + span].reshape(slots, span)
        modes = jnp.dot(legendre_ref[j], held, preferred_element_type=F32).astype(BF16)
        for k in range(half):
            out_ref[:, :, write + k * span : write + (k + 1) * span] = modes[
                2 * lat_count * k : 2 * lat_count * (k + 1)
            ].reshape(lat_count, 2, span)
        read += span
        write += half * span


def synthesis_kernel(modes_ref, fourier_ref, out_ref):
    narrow = out_ref.shape[1]
    third = narrow // BLOCKS
    half = ROWS // 2

    def piece(k, p, j):
        width = narrow if j < FULL else third
        start = (j if j < FULL else FULL) * half * 2 * narrow + max(j - FULL, 0) * half * 2 * third
        at = start + (2 * (k // 2) + p) * width
        return modes_ref[k % 2, :, at : at + width]

    rows = [
        jnp.concatenate([piece(k, p, j) for k in range(ROWS)], axis=1)
        for j in range(FULL)
        for p in range(2)
    ]
    for p in range(2):
        blocks = []
        for k in range(ROWS):
            blocks += block_rows([piece(k, p, FULL + u) for u in range(UNITS)])
        rows.append(jnp.concatenate(blocks, axis=1))
    grad = lax.dot_general(
        jnp.concatenate(rows, axis=0),
        fourier_ref[...],
        (((0,), (0,)), ((), ())),
        preferred_element_type=F32,
    ).astype(BF16)
    for k in range(ROWS):
        out_ref[k] = grad[k * narrow : (k + 1) * narrow, :]


def held_rows(counts_ref, rank_ref):
    rank = rank_ref[0]
    odd = rank % 2
    first = counts_ref[rank - odd]
    count = jnp.where(odd == 1, 2 * ROWS - first, first)
    slots = []
    for r in range(2 * ROWS):
        at = odd * first + r
        slots.append((r < count, (at // ROWS) == odd, jnp.clip(at % ROWS, 0, ROWS - 1)))
    return slots


def gradient_kernel(
    counts_ref, rank_ref, coeffs_ref, mine_ref, grad_ref, out_ref, held_ref, empty_ref, sems, grad_sems
):
    empty_ref[...] = jnp.zeros_like(empty_ref)
    rows = []
    for r, (live, own, at) in enumerate(held_rows(counts_ref, rank_ref)):
        target, sem = out_ref.at[r], sems.at[r]
        near = pltpu.make_async_copy(mine_ref.at[at], target, sem)
        dead = pltpu.make_async_copy(empty_ref, target, sem)
        pl.when(live & own)(near.start)
        pl.when(jnp.logical_not(live))(dead.start)
        rows.append((jnp.logical_not(live) | own, near))
    stores = []
    for s in range(2):
        held_ref[s] = lax.dot_general(
            side(coeffs_ref, s, 0),
            side(coeffs_ref, s, 1),
            (((0,), (0,)), ((), ())),
            preferred_element_type=F32,
        )
        stores.append(pltpu.make_async_copy(held_ref.at[s], grad_ref.at[s], grad_sems.at[s]))
        stores[-1].start()
    for started, row in rows:
        pl.when(started)(row.wait)
    for store in stores:
        store.wait()


def placing_kernel(counts_ref, rank_ref, theirs_ref, placed_ref, out_ref, sems):
    rows = []
    for r, (live, own, at) in enumerate(held_rows(counts_ref, rank_ref)):
        wanted = live & jnp.logical_not(own)
        row = pltpu.make_async_copy(theirs_ref.at[at], out_ref.at[r], sems.at[r])
        pl.when(wanted)(row.start)
        rows.append((wanted, row))
    for wanted, row in rows:
        pl.when(wanted)(row.wait)


def on_device(field_in, cotangent, weights, row_counts, slot_degree):
    lat_count = lax.axis_size("lat")
    chan_count = lax.axis_size("chan")
    rank = lax.axis_index("lat")
    narrow = field_in.shape[1]
    held, full = weights.shape[:2]
    devices = lat_count * chan_count
    pairs = [(i, i ^ 1) for i in range(lat_count)]
    odd = rank % 2
    at_rank = jnp.reshape(rank, (1,)).astype(jnp.int32)
    by_rank, by_part = (jnp.asarray(table) for table in fourier_tables(lat_count))
    pieces = FULL * BLOCKS + UNITS
    third = narrow // BLOCKS
    everyone = ("chan", "lat")

    field_send = lax.dynamic_slice_in_dim(field_in, (1 - odd) * ROWS, ROWS)
    cotan_send = lax.dynamic_slice_in_dim(cotangent, (1 - odd) * ROWS, ROWS)
    field_send, by_rank = lax.optimization_barrier((field_send, by_rank))
    field_swap = lax.ppermute(field_send, "lat", pairs)
    cotan_swap = lax.ppermute(cotan_send, "lat", pairs)
    by_rank = loaded(by_rank, "fourier")
    width = 2 * ROWS * narrow
    modes = run(
        analysis_kernel,
        "analysis",
        [pltpu.HBM((lat_count, 2, pieces * width // BLOCKS), BF16)],
        [row_counts, at_rank, field_in, cotangent, field_swap, cotan_swap, by_rank],
        [
            pltpu.VMEM((width, NLON), BF16),
            pltpu.VMEM((lat_count, 2, pieces * width // BLOCKS), BF16),
            pltpu.SemaphoreType.DMA((GROUPS,)),
        ],
        home=pltpu.HBM,
    )
    modes = lax.all_to_all(modes, "lat", split_axis=0, concat_axis=0, tiled=True)
    modes = modes.transpose(1, 0, 2)
    slot_rows = slot_degree.reshape(lat_count, chan_count, held).transpose(1, 0, 2).reshape(-1)
    legendre, legendre_pairs = legendre_slots(at_rank, lat_count, slot_rows)
    coeffs, weights, legendre_pairs = run(
        forward_kernel,
        "forward",
        [
            pltpu.VMEM((devices, held, 4 * pieces * third), BF16),
            pltpu.VMEM(weights.shape, BF16),
            pltpu.VMEM(legendre_pairs.shape, BF16),
        ],
        [at_rank, modes, legendre, weights, legendre_pairs],
        [pltpu.SemaphoreType.DMA((2,))],
        far=(3, 4),
    )
    coeffs = lax.all_to_all(coeffs, everyone, split_axis=0, concat_axis=0, tiled=True)
    coeffs = coeffs.transpose(1, 0, 2).reshape(held, chan_count, lat_count, 4 * pieces * third)
    back = run(
        degree_kernel,
        "degree",
        [pltpu.VMEM((devices, held, 2 * pieces * third), BF16)],
        [coeffs, weights],
    )
    back = lax.all_to_all(back, everyone, split_axis=0, concat_axis=0, tiled=True)
    modes_back = run(
        backward_kernel,
        "backward",
        [pltpu.VMEM((lat_count, 2, ROWS * pieces * third), BF16)],
        [back, legendre_pairs],
    )
    modes_back = lax.all_to_all(modes_back, "lat", split_axis=0, concat_axis=0, tiled=True)
    grad = run(
        synthesis_kernel,
        "synthesis",
        [pltpu.VMEM((ROWS, narrow, NLON), BF16)],
        [modes_back.transpose(1, 0, 2), by_part],
    )
    grad, coeffs = lax.optimization_barrier((grad, coeffs))
    grad_swap = lax.ppermute(grad, "lat", pairs)
    weight_grad, placed = run(
        gradient_kernel,
        "gradient",
        [pltpu.HBM((held, full, full), F32), pltpu.HBM(field_in.shape, BF16)],
        [row_counts, at_rank, coeffs, grad],
        [
            pltpu.VMEM((held, full, full), F32),
            pltpu.VMEM((narrow, NLON), BF16),
            pltpu.SemaphoreType.DMA((2 * ROWS,)),
            pltpu.SemaphoreType.DMA((held,)),
        ],
        home=pltpu.HBM,
    )
    grad_swap, placed = lax.optimization_barrier((grad_swap, placed))
    field_grad = run(
        placing_kernel,
        "placing",
        [pltpu.HBM(field_in.shape, BF16)],
        [row_counts, at_rank, grad_swap, placed],
        [pltpu.SemaphoreType.DMA((2 * ROWS,))],
        home=pltpu.HBM,
        far=(3,),
        aliases={3: 0},
    )
    return field_grad, weight_grad


def solution(mesh):
    placed = (
        P("lat", "chan", None),
        P("lat", "chan", None),
        P(("lat", "chan"), None, None),
        P(),
        P(),
    )
    return jax.shard_map(
        on_device,
        mesh=mesh,
        in_specs=placed,
        out_specs=(P("lat", "chan", None), P(("lat", "chan"), None, None)),
        check_vma=False,
    )
```

```python
import math

import jax
import jax.numpy as jnp
import ml_dtypes
import numpy as np
from jax import lax
from jax.experimental import pallas as pl
from jax.experimental.pallas import tpu as pltpu
from jax.sharding import PartitionSpec as P

NLON = 720
L = 360
M = 360
LPAD = 384
ROWS = 6
FULL = 5
UNITS = 2
BLOCKS = 3
GROUPS = FULL + UNITS
RESCALE = 2.0**40
RESCALE_LOG = 40.0 * math.log(2.0)
BF16 = jnp.bfloat16
F32 = jnp.float32
VMEM_BYTES = 30 * 1024 * 1024


def block_rows(units):
    lat_count = units[0].shape[0]
    last = M - FULL * lat_count
    parts = []
    for at in range(0, BLOCKS * last, last):
        ends = [(max(at, u * lat_count), min(at + last, (u + 1) * lat_count)) for u in range(UNITS)]
        pieces = [
            units[u][lo - u * lat_count : hi - u * lat_count]
            for u, (lo, hi) in enumerate(ends)
            if lo < hi
        ]
        parts.append(pieces[0] if len(pieces) == 1 else jnp.concatenate(pieces, axis=0))
    return parts


def unit_rows(blocks, lat_count, height=1):
    last = M - FULL * lat_count
    units = []
    for u in range(UNITS):
        pieces = []
        for b in range(BLOCKS):
            lo, hi = max(b * last, u * lat_count), min((b + 1) * last, (u + 1) * lat_count)
            if lo < hi:
                pieces.append(blocks[b][(lo - b * last) * height : (hi - b * last) * height])
        dead = (u + 1) * lat_count - max(BLOCKS * last, u * lat_count)
        if dead > 0:
            pieces.append(jnp.zeros((dead * height, blocks[0].shape[1]), blocks[0].dtype))
        units.append(jnp.concatenate(pieces, axis=0))
    return units


def fourier_rows(orders):
    turns = orders[:, None] * np.arange(NLON)[None, :] % NLON
    angles = turns * (2.0 * math.pi / NLON)
    parts = np.stack([np.cos(angles), -np.sin(angles)], axis=1) / math.sqrt(NLON)
    return parts.astype(ml_dtypes.bfloat16)


def fourier_tables(lat_count):
    first = fourier_rows(np.arange(FULL * lat_count)).reshape(FULL, lat_count, 2, NLON)
    last = fourier_rows(np.arange(FULL * lat_count, M))
    by_rank = np.concatenate([first.reshape(-1, NLON), last.reshape(-1, NLON)])
    by_part = np.concatenate(
        [first.transpose(0, 2, 1, 3).reshape(-1, NLON), last.transpose(1, 0, 2).reshape(-1, NLON)]
    )
    return by_rank, by_part


def order_tables(lat_count):
    rank = np.arange(lat_count)[:, None]
    unit = np.arange(UNITS)[None, :] * lat_count + rank
    last = M - FULL * lat_count
    units = np.where(unit < BLOCKS * last, FULL * lat_count + unit % last, 10**6)
    firsts = np.arange(FULL)[None, :] * lat_count + rank
    dead = np.full((lat_count, 8 - GROUPS), 10**6)
    orders = np.concatenate([firsts, units, dead], axis=1)
    logs = [
        0.5 * math.log((2.0 * m + 1.0) / (4.0 * math.pi))
        + 0.5 * math.lgamma(2.0 * m + 1.0)
        - m * math.log(2.0)
        - math.lgamma(m + 1.0)
        for m in np.minimum(orders, M).reshape(-1).tolist()
    ]
    latitudes = ROWS * lat_count
    norms = np.array(logs).reshape(orders.shape) + 0.5 * math.log(2.0 * math.pi**2 / latitudes)
    shape = orders.shape + (128,)
    return tuple(np.broadcast_to(t[:, :, None], shape).astype(np.float32) for t in (orders, norms))


def latitude_rows(lat_count):
    grid = np.arange(lat_count)[None, :] * ROWS + np.arange(ROWS)[:, None]
    paired = grid.reshape(ROWS // 2, 2, lat_count).transpose(0, 2, 1)
    order = np.concatenate([grid.reshape(-1), paired.reshape(-1)])[None, :]
    theta = (order + 0.5) * (math.pi / (ROWS * lat_count))
    return np.cos(theta).astype(np.float32), np.log(np.sin(theta)).astype(np.float32)


def run(kernel, name, outs, args, scratch=(), far=(), aliases={}):
    specs, operands = [], []
    for at, arg in enumerate(args):
        if arg.dtype == jnp.int32 and arg.ndim == 1:
            space = pltpu.SMEM
        else:
            space = pltpu.HBM if at in far else pltpu.VMEM
            arg = pltpu.with_memory_space_constraint(arg, space)
        specs.append(pl.BlockSpec(memory_space=space))
        operands.append(arg)
    results = pl.pallas_call(
        kernel,
        out_shape=tuple(outs),
        in_specs=specs,
        out_specs=tuple(pl.BlockSpec(memory_space=out.memory_space) for out in outs),
        scratch_shapes=list(scratch),
        input_output_aliases=aliases,
        compiler_params=pltpu.CompilerParams(vmem_limit_bytes=VMEM_BYTES),
        name=name,
    )(*operands)
    return results if len(outs) > 1 else results[0]


def loading_kernel(stored_ref, out_ref, sem):
    copy = pltpu.make_async_copy(stored_ref, out_ref, sem)
    copy.start()
    copy.wait()


def slicing_kernel(rank_ref, stored_ref, out_ref, sem):
    start = (1 - rank_ref[0] % 2) * ROWS
    copy = pltpu.make_async_copy(stored_ref.at[pl.ds(start, ROWS)], out_ref, sem)
    copy.start()
    copy.wait()


def surplus(at_rank, array, name):
    return run(
        slicing_kernel,
        name,
        [pltpu.VMEM((ROWS,) + array.shape[1:], array.dtype)],
        [at_rank, array],
        [pltpu.SemaphoreType.DMA],
        far=(1,),
    )


def loaded(array, name):
    return run(
        loading_kernel,
        name,
        [pltpu.VMEM(array.shape, array.dtype)],
        [array],
        [pltpu.SemaphoreType.DMA],
        far=(0,),
    )


def held_rows(counts_ref, rank_ref):
    rank = rank_ref[0]
    odd = rank % 2
    first = counts_ref[rank - odd]
    count = jnp.where(odd == 1, 2 * ROWS - first, first)
    slots = []
    for r in range(2 * ROWS):
        at = odd * first + r
        slots.append((r < count, (at // ROWS) == odd, jnp.clip(at % ROWS, 0, ROWS - 1)))
    return slots


def legendre_kernel(
    counts_ref, rank_ref, cosine_ref, logsine_ref, order_ref, norm_ref, slot_ref,
    rows_out_ref, pairs_out_ref, placed_ref, rows_ref, table_ref, empty_ref, sems,
):
    empty_ref[...] = jnp.zeros_like(empty_ref)
    stores = []
    for r, (live, _, _) in enumerate(held_rows(counts_ref, rank_ref)):
        store = pltpu.make_async_copy(empty_ref, placed_ref.at[r], sems.at[r])
        pl.when(jnp.logical_not(live))(store.start)
        stores.append((jnp.logical_not(live), store))
    rank = rank_ref[0]
    latitudes = rows_out_ref.shape[2]
    shape = (8, 128)
    order = order_ref[rank]
    square = order * order
    tiles = cosine_ref.shape[1] // 128
    cosines, scales = [], []
    for t in range(tiles):
        lanes = slice(128 * t, 128 * (t + 1))
        cosines.append(jnp.broadcast_to(cosine_ref[:, lanes], shape))
        logsine = jnp.broadcast_to(logsine_ref[:, lanes], shape)
        scales.append(norm_ref[rank] + order * logsine + 0.5 * logsine)
    zero = jnp.zeros(shape, F32)
    one = jnp.ones(shape, F32)

    def advance(l, carry):
        degree = l.astype(F32)
        below = degree - 1.0
        upper = jnp.sqrt(
            jnp.maximum(4.0 * degree * degree - 1.0, 1.0)
            / jnp.maximum(degree * degree - square, 1.0)
        )
        lower = jnp.sqrt(
            jnp.maximum(below * below - square, 0.0)
            / jnp.maximum(4.0 * below * below - 1.0, 1.0)
        )
        rising = degree > order
        reached = degree >= order
        fresh = []
        for t in range(tiles):
            previous, current, scale = carry[3 * t : 3 * t + 3]
            value = upper * (cosines[t] * current - lower * previous)
            previous = jnp.where(rising, current, previous)
            current = jnp.where(rising, value, current)
            too_large = jnp.abs(current) > RESCALE
            factor = jnp.where(too_large, 1.0 / RESCALE, 1.0)
            previous = previous * factor
            current = current * factor
            scale = scale + jnp.where(too_large, RESCALE_LOG, 0.0)
            rows_ref[l, :, 128 * t : 128 * (t + 1)] = jnp.where(
                reached, current * jnp.exp(scale), 0.0
            )
            fresh += [previous, current, scale]
        return tuple(fresh)

    start = []
    for t in range(tiles):
        start += [zero, one, scales[t]]
    lax.fori_loop(0, L, advance, tuple(start), unroll=4)
    rows_ref[L:, :, :] = jnp.zeros((LPAD - L,) + rows_ref.shape[1:], F32)
    slots = slot_ref.shape[0]
    degrees = lax.broadcasted_iota(jnp.int32, (slots, LPAD), 1)
    pick = jnp.where((degrees == slot_ref[...]) & (degrees < L), 1.0, 0.0).astype(BF16)
    for j in range(GROUPS):
        table = rows_ref[:, j, :latitudes].astype(BF16)
        rows_out_ref[j] = jnp.dot(pick, table, preferred_element_type=F32).astype(BF16)
        table = rows_ref[:, j, latitudes:].astype(BF16)
        table_ref[j] = lax.dot_general(
            table, pick, (((0,), (1,)), ((), ())), preferred_element_type=F32
        ).astype(BF16)
        store = pltpu.make_async_copy(
            table_ref.at[j], pairs_out_ref.at[j], sems.at[2 * ROWS + j]
        )
        store.start()
        stores.append((True, store))
    for started, store in stores:
        pl.when(started)(store.wait)


def legendre_slots(row_counts, at_rank, lat_count, slot_rows, placed):
    slots = slot_rows.shape[0]
    latitudes = ROWS * lat_count
    cosine, logsine = latitude_rows(lat_count)
    orders, norms = order_tables(lat_count)
    return run(
        legendre_kernel,
        "legendre",
        [
            pltpu.VMEM((GROUPS, slots, latitudes), BF16),
            pltpu.HBM((GROUPS, latitudes, slots), BF16),
            pltpu.HBM(placed, BF16),
        ],
        [
            row_counts,
            at_rank,
            jnp.asarray(cosine),
            jnp.asarray(logsine),
            jnp.asarray(orders),
            jnp.asarray(norms),
            slot_rows[:, None],
        ],
        [
            pltpu.VMEM((LPAD, 8, 2 * latitudes), F32),
            pltpu.VMEM((GROUPS, latitudes, slots), BF16),
            pltpu.VMEM(placed[1:], BF16),
            pltpu.SemaphoreType.DMA((2 * ROWS + GROUPS,)),
        ],
    )


def analysis_kernel(
    counts_ref, rank_ref, field_ref, cotan_ref, field_in_ref, cotan_in_ref, fourier_ref,
    out_ref, rows_ref, held_ref, sems,
):
    narrow = field_ref.shape[1]
    lat_count = out_ref.shape[0]
    width = 2 * ROWS * narrow
    rank = rank_ref[0]
    odd = rank % 2
    first = counts_ref[rank - odd]
    for k in range(ROWS):
        own = k + odd * (ROWS - first)
        mine = (own >= 0) & ((odd == 1) | (k < first))
        theirs = jnp.where(odd == 1, k, k - first)
        for w, (here, there) in enumerate(((field_ref, field_in_ref), (cotan_ref, cotan_in_ref))):
            at = slice((2 * k + w) * narrow, (2 * k + w + 1) * narrow)

            @pl.when(mine)
            def _():
                rows_ref[at, :] = here[jnp.clip(own, 0, 2 * ROWS - 1)]

            @pl.when(jnp.logical_not(mine))
            def _():
                rows_ref[at, :] = there[jnp.clip(theirs, 0, ROWS - 1)]

    contract = (((1,), (1,)), ((), ()))
    full = 2 * lat_count * FULL
    stores = []

    def send(lo, hi):
        lanes = pl.ds(lo, hi - lo)
        store = pltpu.make_async_copy(
            held_ref.at[:, :, lanes], out_ref.at[:, :, lanes], sems.at[len(stores)]
        )
        store.start()
        stores.append(store)

    third = narrow // BLOCKS
    blocks = []
    for b in range(BLOCKS):
        rows = jnp.concatenate(
            [
                rows_ref[i * narrow + b * third : i * narrow + (b + 1) * third, :]
                for i in range(2 * ROWS)
            ],
            axis=0,
        )
        blocks.append(
            lax.dot_general(
                fourier_ref[full:, :], rows, contract, preferred_element_type=F32
            ).astype(BF16)
        )
    for u, unit in enumerate(unit_rows(blocks, lat_count, 2)):
        at = FULL * width + u * (width // BLOCKS)
        held_ref[:, :, at : at + width // BLOCKS] = unit.reshape(lat_count, 2, width // BLOCKS)
    send(FULL * width, out_ref.shape[2])
    for j0, j1 in ((0, 2), (2, 4), (4, FULL)):
        modes = lax.dot_general(
            fourier_ref[2 * lat_count * j0 : 2 * lat_count * j1, :],
            rows_ref[...],
            contract,
            preferred_element_type=F32,
        ).astype(BF16)
        for j in range(j0, j1):
            held_ref[:, :, j * width : (j + 1) * width] = modes[
                2 * lat_count * (j - j0) : 2 * lat_count * (j - j0 + 1)
            ].reshape(lat_count, 2, width)
        send(j0 * width, j1 * width)
    for store in stores:
        store.wait()


def forward_kernel(
    rank_ref, modes_ref, legendre_ref, stored_ref, stored_pairs_ref,
    out_ref, weights_ref, pairs_ref, sems,
):
    loads = [
        pltpu.make_async_copy(stored_pairs_ref, pairs_ref, sems.at[0]),
        pltpu.make_async_copy(stored_ref, weights_ref, sems.at[1]),
    ]
    for load in loads:
        load.start()
    owners = out_ref.shape[0]
    slots = legendre_ref.shape[1]
    read = write = 0
    for j in range(GROUPS):
        width = modes_ref.shape[2] // (ROWS * (FULL * BLOCKS + UNITS)) * (BLOCKS if j < FULL else 1)
        slab = jnp.concatenate(
            [
                jnp.concatenate(
                    [
                        modes_ref[p, :, read + k * width : read + (k + 1) * width]
                        for p in range(2)
                    ],
                    axis=1,
                )
                for k in range(ROWS)
            ],
            axis=0,
        )
        coeffs = jnp.dot(legendre_ref[j], slab, preferred_element_type=F32)
        lane = lax.broadcasted_iota(jnp.int32, (slots, 2 * width), 1)
        cotangent = lane // (width // 2) % 2 == 1
        doubled = jnp.where(rank_ref[0] + j == 0, 1.0, 2.0)
        coeffs = jnp.where(cotangent, coeffs * doubled, coeffs)
        out_ref[:, :, write : write + 2 * width] = coeffs.astype(BF16).reshape(
            owners, 2, 2 * width
        )
        read += ROWS * width
        write += 2 * width
    for load in loads:
        load.wait()


def side(coeffs_ref, s, w):
    chans = coeffs_ref.shape[1]
    third = coeffs_ref.shape[3] // (4 * (FULL * BLOCKS + UNITS))
    narrow = BLOCKS * third
    rows = [
        jnp.concatenate(
            [
                coeffs_ref[s, y, :, (2 * jp + w) * narrow : (2 * jp + w + 1) * narrow]
                for y in range(chans)
            ],
            axis=1,
        )
        for jp in range(2 * FULL)
    ]
    for p in range(2):
        at = 4 * FULL * narrow + (2 * p + w) * third
        pieces = []
        for y in range(chans):
            pieces += block_rows(
                [
                    coeffs_ref[s, y, :, at + u * 4 * third : at + u * 4 * third + third]
                    for u in range(UNITS)
                ]
            )
        rows.append(jnp.concatenate(pieces, axis=1))
    return jnp.concatenate(rows, axis=0)


def degree_kernel(coeffs_ref, weights_ref, back_ref):
    chans, lat_count = coeffs_ref.shape[1:3]
    third = coeffs_ref.shape[3] // (4 * (FULL * BLOCKS + UNITS))
    narrow = BLOCKS * third
    full = 2 * FULL * lat_count
    last = M - FULL * lat_count
    for s in range(2):
        back = lax.dot_general(
            side(coeffs_ref, s, 1),
            weights_ref[s],
            (((1,), (1,)), ((), ())),
            preferred_element_type=F32,
        ).astype(BF16)
        for y in range(chans):
            lanes = slice(y * narrow, (y + 1) * narrow)
            pieces = [back[jp * lat_count : (jp + 1) * lat_count, lanes] for jp in range(2 * FULL)]
            units = []
            for p in range(2):
                rows = slice(full + p * last, full + (p + 1) * last)
                units.append(
                    unit_rows(
                        [
                            back[rows, y * narrow + b * third : y * narrow + (b + 1) * third]
                            for b in range(BLOCKS)
                        ],
                        lat_count,
                    )
                )
            pieces += [units[p][u] for u in range(UNITS) for p in range(2)]
            back_ref[y * lat_count : (y + 1) * lat_count, s, :] = jnp.concatenate(pieces, axis=1)


def backward_kernel(back_ref, legendre_ref, out_ref):
    slots = legendre_ref.shape[2]
    lat_count = out_ref.shape[0]
    third = back_ref.shape[2] // (2 * (FULL * BLOCKS + UNITS))
    half = ROWS // 2
    read = write = 0
    for j in range(GROUPS):
        span = 2 * third * (BLOCKS if j < FULL else 1)
        held = back_ref[:, :, read : read + span].reshape(slots, span)
        modes = jnp.dot(legendre_ref[j], held, preferred_element_type=F32).astype(BF16)
        for k in range(half):
            out_ref[:, :, write + k * span : write + (k + 1) * span] = modes[
                2 * lat_count * k : 2 * lat_count * (k + 1)
            ].reshape(lat_count, 2, span)
        read += span
        write += half * span


def synthesis_kernel(modes_ref, fourier_ref, out_ref):
    narrow = out_ref.shape[1]
    third = narrow // BLOCKS
    half = ROWS // 2

    def piece(k, p, j):
        width = narrow if j < FULL else third
        start = (j if j < FULL else FULL) * half * 2 * narrow + max(j - FULL, 0) * half * 2 * third
        at = start + (2 * (k // 2) + p) * width
        return modes_ref[k % 2, :, at : at + width]

    rows = [
        jnp.concatenate([piece(k, p, j) for k in range(ROWS)], axis=1)
        for j in range(FULL)
        for p in range(2)
    ]
    for p in range(2):
        blocks = []
        for k in range(ROWS):
            blocks += block_rows([piece(k, p, FULL + u) for u in range(UNITS)])
        rows.append(jnp.concatenate(blocks, axis=1))
    grad = lax.dot_general(
        jnp.concatenate(rows, axis=0),
        fourier_ref[...],
        (((0,), (0,)), ((), ())),
        preferred_element_type=F32,
    ).astype(BF16)
    for k in range(ROWS):
        out_ref[k] = grad[k * narrow : (k + 1) * narrow, :]


def gradient_kernel(
    counts_ref, rank_ref, coeffs_ref, mine_ref, placed_ref, grad_ref, out_ref, held_ref, sems, grad_sems
):
    rows = []
    for r, (live, own, at) in enumerate(held_rows(counts_ref, rank_ref)):
        row = pltpu.make_async_copy(mine_ref.at[at], out_ref.at[r], sems.at[r])
        pl.when(live & own)(row.start)
        rows.append((live & own, row))
    stores = []
    for s in range(2):
        held_ref[s] = lax.dot_general(
            side(coeffs_ref, s, 0),
            side(coeffs_ref, s, 1),
            (((0,), (0,)), ((), ())),
            preferred_element_type=F32,
        )
        stores.append(pltpu.make_async_copy(held_ref.at[s], grad_ref.at[s], grad_sems.at[s]))
        stores[-1].start()
    for started, row in rows:
        pl.when(started)(row.wait)
    for store in stores:
        store.wait()


def placing_kernel(counts_ref, rank_ref, theirs_ref, placed_ref, out_ref, sems):
    rows = []
    for r, (live, own, at) in enumerate(held_rows(counts_ref, rank_ref)):
        wanted = live & jnp.logical_not(own)
        row = pltpu.make_async_copy(theirs_ref.at[at], out_ref.at[r], sems.at[r])
        pl.when(wanted)(row.start)
        rows.append((wanted, row))
    for wanted, row in rows:
        pl.when(wanted)(row.wait)


def on_device(field_in, cotangent, weights, row_counts, slot_degree):
    lat_count = lax.axis_size("lat")
    chan_count = lax.axis_size("chan")
    rank = lax.axis_index("lat")
    narrow = field_in.shape[1]
    held, full = weights.shape[:2]
    devices = lat_count * chan_count
    pairs = [(i, i ^ 1) for i in range(lat_count)]
    at_rank = jnp.reshape(rank, (1,)).astype(jnp.int32)
    by_rank, by_part = (jnp.asarray(table) for table in fourier_tables(lat_count))
    pieces = FULL * BLOCKS + UNITS
    third = narrow // BLOCKS
    everyone = ("chan", "lat")

    cotan_send = surplus(at_rank, cotangent, "cotangent_rows")
    field_send = surplus(at_rank, field_in, "field_rows")
    field_send, by_rank = lax.optimization_barrier((field_send, by_rank))
    field_swap = lax.ppermute(field_send, "lat", pairs)
    cotan_swap = lax.ppermute(cotan_send, "lat", pairs)
    by_rank = loaded(by_rank, "fourier")
    width = 2 * ROWS * narrow
    modes = run(
        analysis_kernel,
        "analysis",
        [pltpu.HBM((lat_count, 2, pieces * width // BLOCKS), BF16)],
        [row_counts, at_rank, field_in, cotangent, field_swap, cotan_swap, by_rank],
        [
            pltpu.VMEM((width, NLON), BF16),
            pltpu.VMEM((lat_count, 2, pieces * width // BLOCKS), BF16),
            pltpu.SemaphoreType.DMA((GROUPS,)),
        ],
    )
    modes = lax.all_to_all(modes, "lat", split_axis=0, concat_axis=0, tiled=True)
    modes = modes.transpose(1, 0, 2)
    slot_rows = slot_degree.reshape(lat_count, chan_count, held).transpose(1, 0, 2).reshape(-1)
    legendre, legendre_pairs, placed = legendre_slots(
        row_counts, at_rank, lat_count, slot_rows, field_in.shape
    )
    coeffs, weights, legendre_pairs = run(
        forward_kernel,
        "forward",
        [
            pltpu.VMEM((devices, held, 4 * pieces * third), BF16),
            pltpu.VMEM(weights.shape, BF16),
            pltpu.VMEM(legendre_pairs.shape, BF16),
        ],
        [at_rank, modes, legendre, weights, legendre_pairs],
        [pltpu.SemaphoreType.DMA((2,))],
        far=(3, 4),
    )
    coeffs = lax.all_to_all(coeffs, everyone, split_axis=0, concat_axis=0, tiled=True)
    coeffs = coeffs.transpose(1, 0, 2).reshape(held, chan_count, lat_count, 4 * pieces * third)
    back = run(
        degree_kernel,
        "degree",
        [pltpu.VMEM((devices, held, 2 * pieces * third), BF16)],
        [coeffs, weights],
    )
    back = lax.all_to_all(back, everyone, split_axis=0, concat_axis=0, tiled=True)
    modes_back = run(
        backward_kernel,
        "backward",
        [pltpu.VMEM((lat_count, 2, ROWS * pieces * third), BF16)],
        [back, legendre_pairs],
    )
    modes_back = lax.all_to_all(modes_back, "lat", split_axis=0, concat_axis=0, tiled=True)
    grad = run(
        synthesis_kernel,
        "synthesis",
        [pltpu.VMEM((ROWS, narrow, NLON), BF16)],
        [modes_back.transpose(1, 0, 2), by_part],
    )
    grad, coeffs = lax.optimization_barrier((grad, coeffs))
    grad_swap = lax.ppermute(grad, "lat", pairs)
    weight_grad, placed = run(
        gradient_kernel,
        "gradient",
        [pltpu.HBM((held, full, full), F32), pltpu.HBM(field_in.shape, BF16)],
        [row_counts, at_rank, coeffs, grad, placed],
        [
            pltpu.VMEM((held, full, full), F32),
            pltpu.SemaphoreType.DMA((2 * ROWS,)),
            pltpu.SemaphoreType.DMA((held,)),
        ],
        far=(4,),
        aliases={4: 1},
    )
    grad_swap, placed = lax.optimization_barrier((grad_swap, placed))
    field_grad = run(
        placing_kernel,
        "placing",
        [pltpu.HBM(field_in.shape, BF16)],
        [row_counts, at_rank, grad_swap, placed],
        [pltpu.SemaphoreType.DMA((2 * ROWS,))],
        far=(3,),
        aliases={3: 0},
    )
    return field_grad, weight_grad


def solution(mesh):
    placed = (
        P("lat", "chan", None),
        P("lat", "chan", None),
        P(("lat", "chan"), None, None),
        P(),
        P(),
    )
    return jax.shard_map(
        on_device,
        mesh=mesh,
        in_specs=placed,
        out_specs=(P("lat", "chan", None), P(("lat", "chan"), None, None)),
        check_vma=False,
    )
```

```python
import math

import jax
import jax.numpy as jnp
import ml_dtypes
import numpy as np
from jax import lax
from jax.experimental import pallas as pl
from jax.experimental.pallas import tpu as pltpu
from jax.sharding import PartitionSpec as P

NLON = 720
L = 360
M = 360
LPAD = 384
ROWS = 6
FULL = 5
UNITS = 2
BLOCKS = 3
GROUPS = FULL + UNITS
RESCALE = 2.0**40
RESCALE_LOG = 40.0 * math.log(2.0)
BF16 = jnp.bfloat16
F32 = jnp.float32
VMEM_BYTES = 30 * 1024 * 1024


def block_rows(units):
    lat_count = units[0].shape[0]
    last = M - FULL * lat_count
    parts = []
    for at in range(0, BLOCKS * last, last):
        ends = [(max(at, u * lat_count), min(at + last, (u + 1) * lat_count)) for u in range(UNITS)]
        pieces = [
            units[u][lo - u * lat_count : hi - u * lat_count]
            for u, (lo, hi) in enumerate(ends)
            if lo < hi
        ]
        parts.append(pieces[0] if len(pieces) == 1 else jnp.concatenate(pieces, axis=0))
    return parts


def unit_rows(blocks, lat_count, height=1):
    last = M - FULL * lat_count
    units = []
    for u in range(UNITS):
        pieces = []
        for b in range(BLOCKS):
            lo, hi = max(b * last, u * lat_count), min((b + 1) * last, (u + 1) * lat_count)
            if lo < hi:
                pieces.append(blocks[b][(lo - b * last) * height : (hi - b * last) * height])
        dead = (u + 1) * lat_count - max(BLOCKS * last, u * lat_count)
        if dead > 0:
            pieces.append(jnp.zeros((dead * height, blocks[0].shape[1]), blocks[0].dtype))
        units.append(jnp.concatenate(pieces, axis=0))
    return units


def fourier_rows(orders):
    turns = orders[:, None] * np.arange(NLON)[None, :] % NLON
    angles = turns * (2.0 * math.pi / NLON)
    parts = np.stack([np.cos(angles), -np.sin(angles)], axis=1) / math.sqrt(NLON)
    return parts.astype(ml_dtypes.bfloat16)


def fourier_tables(lat_count):
    first = fourier_rows(np.arange(FULL * lat_count)).reshape(FULL, lat_count, 2, NLON)
    last = fourier_rows(np.arange(FULL * lat_count, M))
    by_rank = np.concatenate([first.reshape(-1, NLON), last.reshape(-1, NLON)])
    by_part = np.concatenate(
        [first.transpose(0, 2, 1, 3).reshape(-1, NLON), last.transpose(1, 0, 2).reshape(-1, NLON)]
    )
    return by_rank, by_part


def order_tables(lat_count):
    rank = np.arange(lat_count)[:, None]
    unit = np.arange(UNITS)[None, :] * lat_count + rank
    last = M - FULL * lat_count
    units = np.where(unit < BLOCKS * last, FULL * lat_count + unit % last, 10**6)
    firsts = np.arange(FULL)[None, :] * lat_count + rank
    dead = np.full((lat_count, 8 - GROUPS), 10**6)
    orders = np.concatenate([firsts, units, dead], axis=1)
    logs = [
        0.5 * math.log((2.0 * m + 1.0) / (4.0 * math.pi))
        + 0.5 * math.lgamma(2.0 * m + 1.0)
        - m * math.log(2.0)
        - math.lgamma(m + 1.0)
        for m in np.minimum(orders, M).reshape(-1).tolist()
    ]
    latitudes = ROWS * lat_count
    norms = np.array(logs).reshape(orders.shape) + 0.5 * math.log(2.0 * math.pi**2 / latitudes)
    shape = orders.shape + (128,)
    return tuple(np.broadcast_to(t[:, :, None], shape).astype(np.float32) for t in (orders, norms))


def latitude_rows(lat_count):
    grid = np.arange(lat_count)[None, :] * ROWS + np.arange(ROWS)[:, None]
    paired = grid.reshape(ROWS // 2, 2, lat_count).transpose(0, 2, 1)
    order = np.concatenate([grid.reshape(-1), paired.reshape(-1)])[None, :]
    theta = (order + 0.5) * (math.pi / (ROWS * lat_count))
    return np.cos(theta).astype(np.float32), np.log(np.sin(theta)).astype(np.float32)


def run(kernel, name, outs, args, scratch=(), far=(), aliases={}):
    specs, operands = [], []
    for at, arg in enumerate(args):
        if arg.dtype == jnp.int32 and arg.ndim == 1:
            space = pltpu.SMEM
        else:
            space = pltpu.HBM if at in far else pltpu.VMEM
            arg = pltpu.with_memory_space_constraint(arg, space)
        specs.append(pl.BlockSpec(memory_space=space))
        operands.append(arg)
    results = pl.pallas_call(
        kernel,
        out_shape=tuple(outs),
        in_specs=specs,
        out_specs=tuple(pl.BlockSpec(memory_space=out.memory_space) for out in outs),
        scratch_shapes=list(scratch),
        input_output_aliases=aliases,
        compiler_params=pltpu.CompilerParams(vmem_limit_bytes=VMEM_BYTES),
        name=name,
    )(*operands)
    return results if len(outs) > 1 else results[0]


def loading_kernel(stored_ref, out_ref, sem):
    copy = pltpu.make_async_copy(stored_ref, out_ref, sem)
    copy.start()
    copy.wait()


def loaded(array, name):
    return run(
        loading_kernel,
        name,
        [pltpu.VMEM(array.shape, array.dtype)],
        [array],
        [pltpu.SemaphoreType.DMA],
        far=(0,),
    )


def held_rows(counts_ref, rank_ref):
    rank = rank_ref[0]
    odd = rank % 2
    first = counts_ref[rank - odd]
    count = jnp.where(odd == 1, 2 * ROWS - first, first)
    slots = []
    for r in range(2 * ROWS):
        at = odd * first + r
        slots.append((r < count, (at // ROWS) == odd, jnp.clip(at % ROWS, 0, ROWS - 1)))
    return slots


def legendre_kernel(
    counts_ref, rank_ref, cosine_ref, logsine_ref, order_ref, norm_ref, slot_ref,
    rows_out_ref, pairs_out_ref, placed_ref, rows_ref, table_ref, empty_ref, sems,
):
    empty_ref[...] = jnp.zeros_like(empty_ref)
    stores = []
    for r, (live, _, _) in enumerate(held_rows(counts_ref, rank_ref)):
        store = pltpu.make_async_copy(empty_ref, placed_ref.at[r], sems.at[r])
        pl.when(jnp.logical_not(live))(store.start)
        stores.append((jnp.logical_not(live), store))
    rank = rank_ref[0]
    latitudes = rows_out_ref.shape[2]
    shape = (8, 128)
    order = order_ref[rank]
    square = order * order
    tiles = cosine_ref.shape[1] // 128
    cosines, scales = [], []
    for t in range(tiles):
        lanes = slice(128 * t, 128 * (t + 1))
        cosines.append(jnp.broadcast_to(cosine_ref[:, lanes], shape))
        logsine = jnp.broadcast_to(logsine_ref[:, lanes], shape)
        scales.append(norm_ref[rank] + order * logsine + 0.5 * logsine)
    zero = jnp.zeros(shape, F32)
    one = jnp.ones(shape, F32)

    def advance(l, carry):
        degree = l.astype(F32)
        below = degree - 1.0
        upper = jnp.sqrt(
            jnp.maximum(4.0 * degree * degree - 1.0, 1.0)
            / jnp.maximum(degree * degree - square, 1.0)
        )
        lower = jnp.sqrt(
            jnp.maximum(below * below - square, 0.0)
            / jnp.maximum(4.0 * below * below - 1.0, 1.0)
        )
        rising = degree > order
        reached = degree >= order
        fresh = []
        for t in range(tiles):
            previous, current, scale = carry[3 * t : 3 * t + 3]
            value = upper * (cosines[t] * current - lower * previous)
            previous = jnp.where(rising, current, previous)
            current = jnp.where(rising, value, current)
            too_large = jnp.abs(current) > RESCALE
            factor = jnp.where(too_large, 1.0 / RESCALE, 1.0)
            previous = previous * factor
            current = current * factor
            scale = scale + jnp.where(too_large, RESCALE_LOG, 0.0)
            rows_ref[l, :, 128 * t : 128 * (t + 1)] = jnp.where(
                reached, current * jnp.exp(scale), 0.0
            )
            fresh += [previous, current, scale]
        return tuple(fresh)

    start = []
    for t in range(tiles):
        start += [zero, one, scales[t]]
    lax.fori_loop(0, L, advance, tuple(start), unroll=4)
    rows_ref[L:, :, :] = jnp.zeros((LPAD - L,) + rows_ref.shape[1:], F32)
    slots = slot_ref.shape[0]
    degrees = lax.broadcasted_iota(jnp.int32, (slots, LPAD), 1)
    pick = jnp.where((degrees == slot_ref[...]) & (degrees < L), 1.0, 0.0).astype(BF16)
    for j in range(GROUPS):
        table = rows_ref[:, j, :latitudes].astype(BF16)
        rows_out_ref[j] = jnp.dot(pick, table, preferred_element_type=F32).astype(BF16)
        table = rows_ref[:, j, latitudes:].astype(BF16)
        table_ref[j] = lax.dot_general(
            table, pick, (((0,), (1,)), ((), ())), preferred_element_type=F32
        ).astype(BF16)
        store = pltpu.make_async_copy(
            table_ref.at[j], pairs_out_ref.at[j], sems.at[2 * ROWS + j]
        )
        store.start()
        stores.append((True, store))
    for started, store in stores:
        pl.when(started)(store.wait)


def legendre_slots(row_counts, at_rank, lat_count, slot_rows, placed):
    slots = slot_rows.shape[0]
    latitudes = ROWS * lat_count
    cosine, logsine = latitude_rows(lat_count)
    orders, norms = order_tables(lat_count)
    return run(
        legendre_kernel,
        "legendre",
        [
            pltpu.VMEM((GROUPS, slots, latitudes), BF16),
            pltpu.HBM((GROUPS, latitudes, slots), BF16),
            pltpu.HBM(placed, BF16),
        ],
        [
            row_counts,
            at_rank,
            jnp.asarray(cosine),
            jnp.asarray(logsine),
            jnp.asarray(orders),
            jnp.asarray(norms),
            slot_rows[:, None],
        ],
        [
            pltpu.VMEM((LPAD, 8, 2 * latitudes), F32),
            pltpu.VMEM((GROUPS, latitudes, slots), BF16),
            pltpu.VMEM(placed[1:], BF16),
            pltpu.SemaphoreType.DMA((2 * ROWS + GROUPS,)),
        ],
    )


def analysis_kernel(
    counts_ref, rank_ref, field_ref, cotan_ref, field_in_ref, cotan_in_ref, fourier_ref,
    out_ref, rows_ref, held_ref, sems,
):
    narrow = field_ref.shape[1]
    lat_count = out_ref.shape[0]
    width = 2 * ROWS * narrow
    rank = rank_ref[0]
    odd = rank % 2
    first = counts_ref[rank - odd]
    for k in range(ROWS):
        own = k + odd * (ROWS - first)
        mine = (own >= 0) & ((odd == 1) | (k < first))
        theirs = jnp.where(odd == 1, k, k - first)
        for w, (here, there) in enumerate(((field_ref, field_in_ref), (cotan_ref, cotan_in_ref))):
            at = slice((2 * k + w) * narrow, (2 * k + w + 1) * narrow)

            @pl.when(mine)
            def _():
                rows_ref[at, :] = here[jnp.clip(own, 0, 2 * ROWS - 1)]

            @pl.when(jnp.logical_not(mine))
            def _():
                rows_ref[at, :] = there[jnp.clip(theirs, 0, ROWS - 1)]

    contract = (((1,), (1,)), ((), ()))
    full = 2 * lat_count * FULL
    stores = []

    def send(lo, hi):
        lanes = pl.ds(lo, hi - lo)
        store = pltpu.make_async_copy(
            held_ref.at[:, :, lanes], out_ref.at[:, :, lanes], sems.at[len(stores)]
        )
        store.start()
        stores.append(store)

    third = narrow // BLOCKS
    blocks = []
    for b in range(BLOCKS):
        rows = jnp.concatenate(
            [
                rows_ref[i * narrow + b * third : i * narrow + (b + 1) * third, :]
                for i in range(2 * ROWS)
            ],
            axis=0,
        )
        blocks.append(
            lax.dot_general(
                fourier_ref[full:, :], rows, contract, preferred_element_type=F32
            ).astype(BF16)
        )
    for u, unit in enumerate(unit_rows(blocks, lat_count, 2)):
        at = FULL * width + u * (width // BLOCKS)
        held_ref[:, :, at : at + width // BLOCKS] = unit.reshape(lat_count, 2, width // BLOCKS)
    send(FULL * width, out_ref.shape[2])
    for j0, j1 in ((0, 2), (2, 4), (4, FULL)):
        modes = lax.dot_general(
            fourier_ref[2 * lat_count * j0 : 2 * lat_count * j1, :],
            rows_ref[...],
            contract,
            preferred_element_type=F32,
        ).astype(BF16)
        for j in range(j0, j1):
            held_ref[:, :, j * width : (j + 1) * width] = modes[
                2 * lat_count * (j - j0) : 2 * lat_count * (j - j0 + 1)
            ].reshape(lat_count, 2, width)
        send(j0 * width, j1 * width)
    for store in stores:
        store.wait()


def forward_kernel(
    rank_ref, modes_ref, legendre_ref, stored_ref, stored_pairs_ref,
    out_ref, weights_ref, pairs_ref, sems,
):
    loads = [
        pltpu.make_async_copy(stored_pairs_ref, pairs_ref, sems.at[0]),
        pltpu.make_async_copy(stored_ref, weights_ref, sems.at[1]),
    ]
    for load in loads:
        load.start()
    owners = out_ref.shape[0]
    slots = legendre_ref.shape[1]
    read = write = 0
    for j in range(GROUPS):
        width = modes_ref.shape[2] // (ROWS * (FULL * BLOCKS + UNITS)) * (BLOCKS if j < FULL else 1)
        slab = jnp.concatenate(
            [
                jnp.concatenate(
                    [
                        modes_ref[p, :, read + k * width : read + (k + 1) * width]
                        for p in range(2)
                    ],
                    axis=1,
                )
                for k in range(ROWS)
            ],
            axis=0,
        )
        coeffs = jnp.dot(legendre_ref[j], slab, preferred_element_type=F32)
        lane = lax.broadcasted_iota(jnp.int32, (slots, 2 * width), 1)
        cotangent = lane // (width // 2) % 2 == 1
        doubled = jnp.where(rank_ref[0] + j == 0, 1.0, 2.0)
        coeffs = jnp.where(cotangent, coeffs * doubled, coeffs)
        out_ref[:, :, write : write + 2 * width] = coeffs.astype(BF16).reshape(
            owners, 2, 2 * width
        )
        read += ROWS * width
        write += 2 * width
    for load in loads:
        load.wait()


def side(coeffs_ref, s, w):
    chans = coeffs_ref.shape[1]
    third = coeffs_ref.shape[3] // (4 * (FULL * BLOCKS + UNITS))
    narrow = BLOCKS * third
    rows = [
        jnp.concatenate(
            [
                coeffs_ref[s, y, :, (2 * jp + w) * narrow : (2 * jp + w + 1) * narrow]
                for y in range(chans)
            ],
            axis=1,
        )
        for jp in range(2 * FULL)
    ]
    for p in range(2):
        at = 4 * FULL * narrow + (2 * p + w) * third
        pieces = []
        for y in range(chans):
            pieces += block_rows(
                [
                    coeffs_ref[s, y, :, at + u * 4 * third : at + u * 4 * third + third]
                    for u in range(UNITS)
                ]
            )
        rows.append(jnp.concatenate(pieces, axis=1))
    return jnp.concatenate(rows, axis=0)


def degree_kernel(coeffs_ref, weights_ref, back_ref):
    chans, lat_count = coeffs_ref.shape[1:3]
    third = coeffs_ref.shape[3] // (4 * (FULL * BLOCKS + UNITS))
    narrow = BLOCKS * third
    full = 2 * FULL * lat_count
    last = M - FULL * lat_count
    for s in range(2):
        back = lax.dot_general(
            side(coeffs_ref, s, 1),
            weights_ref[s],
            (((1,), (1,)), ((), ())),
            preferred_element_type=F32,
        ).astype(BF16)
        for y in range(chans):
            lanes = slice(y * narrow, (y + 1) * narrow)
            pieces = [back[jp * lat_count : (jp + 1) * lat_count, lanes] for jp in range(2 * FULL)]
            units = []
            for p in range(2):
                rows = slice(full + p * last, full + (p + 1) * last)
                units.append(
                    unit_rows(
                        [
                            back[rows, y * narrow + b * third : y * narrow + (b + 1) * third]
                            for b in range(BLOCKS)
                        ],
                        lat_count,
                    )
                )
            pieces += [units[p][u] for u in range(UNITS) for p in range(2)]
            back_ref[y * lat_count : (y + 1) * lat_count, s, :] = jnp.concatenate(pieces, axis=1)


def backward_kernel(back_ref, legendre_ref, out_ref):
    slots = legendre_ref.shape[2]
    lat_count = out_ref.shape[0]
    third = back_ref.shape[2] // (2 * (FULL * BLOCKS + UNITS))
    half = ROWS // 2
    read = write = 0
    for j in range(GROUPS):
        span = 2 * third * (BLOCKS if j < FULL else 1)
        held = back_ref[:, :, read : read + span].reshape(slots, span)
        modes = jnp.dot(legendre_ref[j], held, preferred_element_type=F32).astype(BF16)
        for k in range(half):
            out_ref[:, :, write + k * span : write + (k + 1) * span] = modes[
                2 * lat_count * k : 2 * lat_count * (k + 1)
            ].reshape(lat_count, 2, span)
        read += span
        write += half * span


def synthesis_kernel(modes_ref, fourier_ref, out_ref):
    narrow = out_ref.shape[1]
    third = narrow // BLOCKS
    half = ROWS // 2

    def piece(k, p, j):
        width = narrow if j < FULL else third
        start = (j if j < FULL else FULL) * half * 2 * narrow + max(j - FULL, 0) * half * 2 * third
        at = start + (2 * (k // 2) + p) * width
        return modes_ref[k % 2, :, at : at + width]

    rows = [
        jnp.concatenate([piece(k, p, j) for k in range(ROWS)], axis=1)
        for j in range(FULL)
        for p in range(2)
    ]
    for p in range(2):
        blocks = []
        for k in range(ROWS):
            blocks += block_rows([piece(k, p, FULL + u) for u in range(UNITS)])
        rows.append(jnp.concatenate(blocks, axis=1))
    grad = lax.dot_general(
        jnp.concatenate(rows, axis=0),
        fourier_ref[...],
        (((0,), (0,)), ((), ())),
        preferred_element_type=F32,
    ).astype(BF16)
    for k in range(ROWS):
        out_ref[k] = grad[k * narrow : (k + 1) * narrow, :]


def finish(slot, near, counts_ref, rank_ref, coeffs_ref, rows_ref, grad_ref, out_ref, held_ref, sems):
    copies = []
    for r, (live, own, at) in enumerate(held_rows(counts_ref, rank_ref)):
        wanted = live & (own if near else jnp.logical_not(own))
        copy = pltpu.make_async_copy(rows_ref.at[at], out_ref.at[r], sems.at[r])
        pl.when(wanted)(copy.start)
        copies.append((wanted, copy))
    coeffs = side(coeffs_ref, slot, 0)
    dcoeffs = side(coeffs_ref, slot, 1)
    full = held_ref.shape[0]
    stores = []
    for i, (lo, hi) in enumerate(((0, 256), (256, full))):
        held_ref[lo:hi, :] = lax.dot_general(
            coeffs[:, lo:hi], dcoeffs, (((0,), (0,)), ((), ())), preferred_element_type=F32
        )
        part = pl.ds(lo, hi - lo)
        stores.append(
            pltpu.make_async_copy(
                held_ref.at[part], grad_ref.at[slot, part], sems.at[2 * ROWS + i]
            )
        )
        stores[-1].start()
    for wanted, copy in copies:
        pl.when(wanted)(copy.wait)
    for store in stores:
        store.wait()


def first_kernel(counts_ref, rank_ref, coeffs_ref, rows_ref, _, grad_ref, out_ref, held_ref, sems):
    finish(0, True, counts_ref, rank_ref, coeffs_ref, rows_ref, grad_ref, out_ref, held_ref, sems)


def second_kernel(counts_ref, rank_ref, coeffs_ref, rows_ref, _, __, grad_ref, out_ref, held_ref, sems):
    finish(1, False, counts_ref, rank_ref, coeffs_ref, rows_ref, grad_ref, out_ref, held_ref, sems)


def on_device(field_in, cotangent, weights, row_counts, slot_degree):
    lat_count = lax.axis_size("lat")
    chan_count = lax.axis_size("chan")
    rank = lax.axis_index("lat")
    narrow = field_in.shape[1]
    held, full = weights.shape[:2]
    devices = lat_count * chan_count
    pairs = [(i, i ^ 1) for i in range(lat_count)]
    odd = rank % 2
    at_rank = jnp.reshape(rank, (1,)).astype(jnp.int32)
    by_rank, by_part = (jnp.asarray(table) for table in fourier_tables(lat_count))
    pieces = FULL * BLOCKS + UNITS
    third = narrow // BLOCKS
    everyone = ("chan", "lat")

    field_send = lax.dynamic_slice_in_dim(field_in, (1 - odd) * ROWS, ROWS)
    cotan_send = lax.dynamic_slice_in_dim(cotangent, (1 - odd) * ROWS, ROWS)
    field_send, by_rank = lax.optimization_barrier((field_send, by_rank))
    field_swap = lax.ppermute(field_send, "lat", pairs)
    cotan_swap = lax.ppermute(cotan_send, "lat", pairs)
    by_rank = loaded(by_rank, "fourier")
    width = 2 * ROWS * narrow
    modes = run(
        analysis_kernel,
        "analysis",
        [pltpu.HBM((lat_count, 2, pieces * width // BLOCKS), BF16)],
        [row_counts, at_rank, field_in, cotangent, field_swap, cotan_swap, by_rank],
        [
            pltpu.VMEM((width, NLON), BF16),
            pltpu.VMEM((lat_count, 2, pieces * width // BLOCKS), BF16),
            pltpu.SemaphoreType.DMA((GROUPS,)),
        ],
    )
    modes = lax.all_to_all(modes, "lat", split_axis=0, concat_axis=0, tiled=True)
    modes = modes.transpose(1, 0, 2)
    slot_rows = slot_degree.reshape(lat_count, chan_count, held).transpose(1, 0, 2).reshape(-1)
    legendre, legendre_pairs, placed = legendre_slots(
        row_counts, at_rank, lat_count, slot_rows, field_in.shape
    )
    coeffs, weights, legendre_pairs = run(
        forward_kernel,
        "forward",
        [
            pltpu.VMEM((devices, held, 4 * pieces * third), BF16),
            pltpu.VMEM(weights.shape, BF16),
            pltpu.VMEM(legendre_pairs.shape, BF16),
        ],
        [at_rank, modes, legendre, weights, legendre_pairs],
        [pltpu.SemaphoreType.DMA((2,))],
        far=(3, 4),
    )
    coeffs = lax.all_to_all(coeffs, everyone, split_axis=0, concat_axis=0, tiled=True)
    coeffs = coeffs.transpose(1, 0, 2).reshape(held, chan_count, lat_count, 4 * pieces * third)
    back = run(
        degree_kernel,
        "degree",
        [pltpu.VMEM((devices, held, 2 * pieces * third), BF16)],
        [coeffs, weights],
    )
    back = lax.all_to_all(back, everyone, split_axis=0, concat_axis=0, tiled=True)
    modes_back = run(
        backward_kernel,
        "backward",
        [pltpu.VMEM((lat_count, 2, ROWS * pieces * third), BF16)],
        [back, legendre_pairs],
    )
    modes_back = lax.all_to_all(modes_back, "lat", split_axis=0, concat_axis=0, tiled=True)
    grad = run(
        synthesis_kernel,
        "synthesis",
        [pltpu.VMEM((ROWS, narrow, NLON), BF16)],
        [modes_back.transpose(1, 0, 2), by_part],
    )
    grad, coeffs = lax.optimization_barrier((grad, coeffs))
    grad_swap = lax.ppermute(grad, "lat", pairs)
    outs = [pltpu.HBM((held, full, full), F32), pltpu.HBM(field_in.shape, BF16)]
    scratch = [pltpu.VMEM((full, full), F32), pltpu.SemaphoreType.DMA((2 * ROWS + 2,))]
    weight_grad, placed = run(
        first_kernel,
        "first_slot",
        outs,
        [row_counts, at_rank, coeffs, grad, placed],
        scratch,
        far=(4,),
        aliases={4: 1},
    )
    grad_swap, placed = lax.optimization_barrier((grad_swap, placed))
    weight_grad, field_grad = run(
        second_kernel,
        "second_slot",
        outs,
        [row_counts, at_rank, coeffs, grad_swap, weight_grad, placed],
        scratch,
        far=(4, 5),
        aliases={4: 0, 5: 1},
    )
    return field_grad, weight_grad


def solution(mesh):
    placed = (
        P("lat", "chan", None),
        P("lat", "chan", None),
        P(("lat", "chan"), None, None),
        P(),
        P(),
    )
    return jax.shard_map(
        on_device,
        mesh=mesh,
        in_specs=placed,
        out_specs=(P("lat", "chan", None), P(("lat", "chan"), None, None)),
        check_vma=False,
    )
```

```python
import math

import jax
import jax.numpy as jnp
import ml_dtypes
import numpy as np
from jax import lax
from jax.experimental import pallas as pl
from jax.experimental.pallas import tpu as pltpu
from jax.sharding import PartitionSpec as P

NLON = 720
L = 360
M = 360
LPAD = 384
ROWS = 6
FULL = 5
UNITS = 2
BLOCKS = 3
GROUPS = FULL + UNITS
RESCALE = 2.0**40
RESCALE_LOG = 40.0 * math.log(2.0)
BF16 = jnp.bfloat16
F32 = jnp.float32
VMEM_BYTES = 30 * 1024 * 1024


def block_rows(units):
    lat_count = units[0].shape[0]
    last = M - FULL * lat_count
    parts = []
    for at in range(0, BLOCKS * last, last):
        ends = [(max(at, u * lat_count), min(at + last, (u + 1) * lat_count)) for u in range(UNITS)]
        pieces = [
            units[u][lo - u * lat_count : hi - u * lat_count]
            for u, (lo, hi) in enumerate(ends)
            if lo < hi
        ]
        parts.append(pieces[0] if len(pieces) == 1 else jnp.concatenate(pieces, axis=0))
    return parts


def unit_rows(blocks, lat_count, height=1):
    last = M - FULL * lat_count
    units = []
    for u in range(UNITS):
        pieces = []
        for b in range(BLOCKS):
            lo, hi = max(b * last, u * lat_count), min((b + 1) * last, (u + 1) * lat_count)
            if lo < hi:
                pieces.append(blocks[b][(lo - b * last) * height : (hi - b * last) * height])
        dead = (u + 1) * lat_count - max(BLOCKS * last, u * lat_count)
        if dead > 0:
            pieces.append(jnp.zeros((dead * height, blocks[0].shape[1]), blocks[0].dtype))
        units.append(jnp.concatenate(pieces, axis=0))
    return units


def fourier_rows(orders):
    turns = orders[:, None] * np.arange(NLON)[None, :] % NLON
    angles = turns * (2.0 * math.pi / NLON)
    parts = np.stack([np.cos(angles), -np.sin(angles)], axis=1) / math.sqrt(NLON)
    return parts.astype(ml_dtypes.bfloat16)


def fourier_tables(lat_count):
    first = fourier_rows(np.arange(FULL * lat_count)).reshape(FULL, lat_count, 2, NLON)
    last = fourier_rows(np.arange(FULL * lat_count, M))
    by_rank = np.concatenate([first.reshape(-1, NLON), last.reshape(-1, NLON)])
    by_part = np.concatenate(
        [first.transpose(0, 2, 1, 3).reshape(-1, NLON), last.transpose(1, 0, 2).reshape(-1, NLON)]
    )
    return by_rank, by_part


def order_tables(lat_count):
    rank = np.arange(lat_count)[:, None]
    unit = np.arange(UNITS)[None, :] * lat_count + rank
    last = M - FULL * lat_count
    units = np.where(unit < BLOCKS * last, FULL * lat_count + unit % last, 10**6)
    firsts = np.arange(FULL)[None, :] * lat_count + rank
    dead = np.full((lat_count, 8 - GROUPS), 10**6)
    orders = np.concatenate([firsts, units, dead], axis=1)
    logs = [
        0.5 * math.log((2.0 * m + 1.0) / (4.0 * math.pi))
        + 0.5 * math.lgamma(2.0 * m + 1.0)
        - m * math.log(2.0)
        - math.lgamma(m + 1.0)
        for m in np.minimum(orders, M).reshape(-1).tolist()
    ]
    latitudes = ROWS * lat_count
    norms = np.array(logs).reshape(orders.shape) + 0.5 * math.log(2.0 * math.pi**2 / latitudes)
    shape = orders.shape + (128,)
    return tuple(np.broadcast_to(t[:, :, None], shape).astype(np.float32) for t in (orders, norms))


def latitude_rows(lat_count):
    grid = np.arange(lat_count)[None, :] * ROWS + np.arange(ROWS)[:, None]
    paired = grid.reshape(ROWS // 2, 2, lat_count).transpose(0, 2, 1)
    order = np.concatenate([grid.reshape(-1), paired.reshape(-1)])[None, :]
    theta = (order + 0.5) * (math.pi / (ROWS * lat_count))
    return np.cos(theta).astype(np.float32), np.log(np.sin(theta)).astype(np.float32)


def run(kernel, name, outs, args, scratch=(), far=(), aliases={}):
    specs, operands = [], []
    for at, arg in enumerate(args):
        if arg.dtype == jnp.int32 and arg.ndim == 1:
            space = pltpu.SMEM
        else:
            space = pltpu.HBM if at in far else pltpu.VMEM
            arg = pltpu.with_memory_space_constraint(arg, space)
        specs.append(pl.BlockSpec(memory_space=space))
        operands.append(arg)
    results = pl.pallas_call(
        kernel,
        out_shape=tuple(outs),
        in_specs=specs,
        out_specs=tuple(pl.BlockSpec(memory_space=out.memory_space) for out in outs),
        scratch_shapes=list(scratch),
        input_output_aliases=aliases,
        compiler_params=pltpu.CompilerParams(vmem_limit_bytes=VMEM_BYTES),
        name=name,
    )(*operands)
    return results if len(outs) > 1 else results[0]


def loading_kernel(stored_ref, out_ref, sem):
    copy = pltpu.make_async_copy(stored_ref, out_ref, sem)
    copy.start()
    copy.wait()


def loaded(array, name):
    return run(
        loading_kernel,
        name,
        [pltpu.VMEM(array.shape, array.dtype)],
        [array],
        [pltpu.SemaphoreType.DMA],
        far=(0,),
    )


def held_rows(counts_ref, rank_ref):
    rank = rank_ref[0]
    odd = rank % 2
    first = counts_ref[rank - odd]
    count = jnp.where(odd == 1, 2 * ROWS - first, first)
    slots = []
    for r in range(2 * ROWS):
        at = odd * first + r
        slots.append((r < count, (at // ROWS) == odd, jnp.clip(at % ROWS, 0, ROWS - 1)))
    return slots


def legendre_kernel(
    counts_ref, rank_ref, cosine_ref, logsine_ref, order_ref, norm_ref, slot_ref,
    rows_out_ref, pairs_out_ref, placed_ref, rows_ref, table_ref, empty_ref, sems,
):
    empty_ref[...] = jnp.zeros_like(empty_ref)
    stores = []
    for r, (live, _, _) in enumerate(held_rows(counts_ref, rank_ref)):
        store = pltpu.make_async_copy(empty_ref, placed_ref.at[r], sems.at[r])
        pl.when(jnp.logical_not(live))(store.start)
        stores.append((jnp.logical_not(live), store))
    rank = rank_ref[0]
    latitudes = rows_out_ref.shape[2]
    shape = (8, 128)
    order = order_ref[rank]
    square = order * order
    tiles = cosine_ref.shape[1] // 128
    cosines, scales = [], []
    for t in range(tiles):
        lanes = slice(128 * t, 128 * (t + 1))
        cosines.append(jnp.broadcast_to(cosine_ref[:, lanes], shape))
        logsine = jnp.broadcast_to(logsine_ref[:, lanes], shape)
        scales.append(norm_ref[rank] + order * logsine + 0.5 * logsine)
    zero = jnp.zeros(shape, F32)
    one = jnp.ones(shape, F32)

    def advance(l, carry):
        degree = l.astype(F32)
        below = degree - 1.0
        upper = jnp.sqrt(
            jnp.maximum(4.0 * degree * degree - 1.0, 1.0)
            / jnp.maximum(degree * degree - square, 1.0)
        )
        lower = jnp.sqrt(
            jnp.maximum(below * below - square, 0.0)
            / jnp.maximum(4.0 * below * below - 1.0, 1.0)
        )
        rising = degree > order
        reached = degree >= order
        fresh = []
        for t in range(tiles):
            previous, current, scale = carry[3 * t : 3 * t + 3]
            value = upper * (cosines[t] * current - lower * previous)
            previous = jnp.where(rising, current, previous)
            current = jnp.where(rising, value, current)
            too_large = jnp.abs(current) > RESCALE
            factor = jnp.where(too_large, 1.0 / RESCALE, 1.0)
            previous = previous * factor
            current = current * factor
            scale = scale + jnp.where(too_large, RESCALE_LOG, 0.0)
            rows_ref[l, :, 128 * t : 128 * (t + 1)] = jnp.where(
                reached, current * jnp.exp(scale), 0.0
            )
            fresh += [previous, current, scale]
        return tuple(fresh)

    start = []
    for t in range(tiles):
        start += [zero, one, scales[t]]
    lax.fori_loop(0, L, advance, tuple(start), unroll=4)
    rows_ref[L:, :, :] = jnp.zeros((LPAD - L,) + rows_ref.shape[1:], F32)
    slots = slot_ref.shape[0]
    degrees = lax.broadcasted_iota(jnp.int32, (slots, LPAD), 1)
    pick = jnp.where((degrees == slot_ref[...]) & (degrees < L), 1.0, 0.0).astype(BF16)
    for j in range(GROUPS):
        table = rows_ref[:, j, :latitudes].astype(BF16)
        rows_out_ref[j] = jnp.dot(pick, table, preferred_element_type=F32).astype(BF16)
        table = rows_ref[:, j, latitudes:].astype(BF16)
        table_ref[j] = lax.dot_general(
            table, pick, (((0,), (1,)), ((), ())), preferred_element_type=F32
        ).astype(BF16)
        store = pltpu.make_async_copy(
            table_ref.at[j], pairs_out_ref.at[j], sems.at[2 * ROWS + j]
        )
        store.start()
        stores.append((True, store))
    for started, store in stores:
        pl.when(started)(store.wait)


def legendre_slots(row_counts, at_rank, lat_count, slot_rows, placed):
    slots = slot_rows.shape[0]
    latitudes = ROWS * lat_count
    cosine, logsine = latitude_rows(lat_count)
    orders, norms = order_tables(lat_count)
    return run(
        legendre_kernel,
        "legendre",
        [
            pltpu.VMEM((GROUPS, slots, latitudes), BF16),
            pltpu.HBM((GROUPS, latitudes, slots), BF16),
            pltpu.HBM(placed, BF16),
        ],
        [
            row_counts,
            at_rank,
            jnp.asarray(cosine),
            jnp.asarray(logsine),
            jnp.asarray(orders),
            jnp.asarray(norms),
            slot_rows[:, None],
        ],
        [
            pltpu.VMEM((LPAD, 8, 2 * latitudes), F32),
            pltpu.VMEM((GROUPS, latitudes, slots), BF16),
            pltpu.VMEM(placed[1:], BF16),
            pltpu.SemaphoreType.DMA((2 * ROWS + GROUPS,)),
        ],
    )


def analysis_kernel(
    counts_ref, rank_ref, field_ref, cotan_ref, field_in_ref, cotan_in_ref, fourier_ref,
    out_ref, rows_ref, held_ref, sems,
):
    narrow = field_ref.shape[1]
    lat_count = out_ref.shape[0]
    width = 2 * ROWS * narrow
    rank = rank_ref[0]
    odd = rank % 2
    first = counts_ref[rank - odd]
    for k in range(ROWS):
        own = k + odd * (ROWS - first)
        mine = (own >= 0) & ((odd == 1) | (k < first))
        theirs = jnp.where(odd == 1, k, k - first)
        for w, (here, there) in enumerate(((field_ref, field_in_ref), (cotan_ref, cotan_in_ref))):
            at = slice((2 * k + w) * narrow, (2 * k + w + 1) * narrow)

            @pl.when(mine)
            def _():
                rows_ref[at, :] = here[jnp.clip(own, 0, 2 * ROWS - 1)]

            @pl.when(jnp.logical_not(mine))
            def _():
                rows_ref[at, :] = there[jnp.clip(theirs, 0, ROWS - 1)]

    contract = (((1,), (1,)), ((), ()))
    full = 2 * lat_count * FULL
    stores = []

    def send(lo, hi):
        lanes = pl.ds(lo, hi - lo)
        store = pltpu.make_async_copy(
            held_ref.at[:, :, lanes], out_ref.at[:, :, lanes], sems.at[len(stores)]
        )
        store.start()
        stores.append(store)

    third = narrow // BLOCKS
    blocks = []
    for b in range(BLOCKS):
        rows = jnp.concatenate(
            [
                rows_ref[i * narrow + b * third : i * narrow + (b + 1) * third, :]
                for i in range(2 * ROWS)
            ],
            axis=0,
        )
        blocks.append(
            lax.dot_general(
                fourier_ref[full:, :], rows, contract, preferred_element_type=F32
            ).astype(BF16)
        )
    for u, unit in enumerate(unit_rows(blocks, lat_count, 2)):
        at = FULL * width + u * (width // BLOCKS)
        held_ref[:, :, at : at + width // BLOCKS] = unit.reshape(lat_count, 2, width // BLOCKS)
    send(FULL * width, out_ref.shape[2])
    for j0, j1 in ((0, 2), (2, 4), (4, FULL)):
        modes = lax.dot_general(
            fourier_ref[2 * lat_count * j0 : 2 * lat_count * j1, :],
            rows_ref[...],
            contract,
            preferred_element_type=F32,
        ).astype(BF16)
        for j in range(j0, j1):
            held_ref[:, :, j * width : (j + 1) * width] = modes[
                2 * lat_count * (j - j0) : 2 * lat_count * (j - j0 + 1)
            ].reshape(lat_count, 2, width)
        send(j0 * width, j1 * width)
    for store in stores:
        store.wait()


def forward_kernel(
    rank_ref, modes_ref, legendre_ref, stored_ref, stored_pairs_ref,
    out_ref, weights_ref, pairs_ref, sems,
):
    loads = [
        pltpu.make_async_copy(stored_pairs_ref, pairs_ref, sems.at[0]),
        pltpu.make_async_copy(stored_ref, weights_ref, sems.at[1]),
    ]
    for load in loads:
        load.start()
    owners = out_ref.shape[0]
    slots = legendre_ref.shape[1]
    read = write = 0
    for j in range(GROUPS):
        width = modes_ref.shape[2] // (ROWS * (FULL * BLOCKS + UNITS)) * (BLOCKS if j < FULL else 1)
        slab = jnp.concatenate(
            [
                jnp.concatenate(
                    [
                        modes_ref[p, :, read + k * width : read + (k + 1) * width]
                        for p in range(2)
                    ],
                    axis=1,
                )
                for k in range(ROWS)
            ],
            axis=0,
        )
        coeffs = jnp.dot(legendre_ref[j], slab, preferred_element_type=F32)
        lane = lax.broadcasted_iota(jnp.int32, (slots, 2 * width), 1)
        cotangent = lane // (width // 2) % 2 == 1
        doubled = jnp.where(rank_ref[0] + j == 0, 1.0, 2.0)
        coeffs = jnp.where(cotangent, coeffs * doubled, coeffs)
        out_ref[:, :, write : write + 2 * width] = coeffs.astype(BF16).reshape(
            owners, 2, 2 * width
        )
        read += ROWS * width
        write += 2 * width
    for load in loads:
        load.wait()


def side(coeffs_ref, s, w):
    chans = coeffs_ref.shape[1]
    third = coeffs_ref.shape[3] // (4 * (FULL * BLOCKS + UNITS))
    narrow = BLOCKS * third
    rows = [
        jnp.concatenate(
            [
                coeffs_ref[s, y, :, (2 * jp + w) * narrow : (2 * jp + w + 1) * narrow]
                for y in range(chans)
            ],
            axis=1,
        )
        for jp in range(2 * FULL)
    ]
    for p in range(2):
        at = 4 * FULL * narrow + (2 * p + w) * third
        pieces = []
        for y in range(chans):
            pieces += block_rows(
                [
                    coeffs_ref[s, y, :, at + u * 4 * third : at + u * 4 * third + third]
                    for u in range(UNITS)
                ]
            )
        rows.append(jnp.concatenate(pieces, axis=1))
    return jnp.concatenate(rows, axis=0)


def degree_kernel(coeffs_ref, weights_ref, back_ref):
    chans, lat_count = coeffs_ref.shape[1:3]
    third = coeffs_ref.shape[3] // (4 * (FULL * BLOCKS + UNITS))
    narrow = BLOCKS * third
    full = 2 * FULL * lat_count
    last = M - FULL * lat_count
    for s in range(2):
        back = lax.dot_general(
            side(coeffs_ref, s, 1),
            weights_ref[s],
            (((1,), (1,)), ((), ())),
            preferred_element_type=F32,
        ).astype(BF16)
        for y in range(chans):
            lanes = slice(y * narrow, (y + 1) * narrow)
            pieces = [back[jp * lat_count : (jp + 1) * lat_count, lanes] for jp in range(2 * FULL)]
            units = []
            for p in range(2):
                rows = slice(full + p * last, full + (p + 1) * last)
                units.append(
                    unit_rows(
                        [
                            back[rows, y * narrow + b * third : y * narrow + (b + 1) * third]
                            for b in range(BLOCKS)
                        ],
                        lat_count,
                    )
                )
            pieces += [units[p][u] for u in range(UNITS) for p in range(2)]
            back_ref[y * lat_count : (y + 1) * lat_count, s, :] = jnp.concatenate(pieces, axis=1)


def backward_kernel(back_ref, legendre_ref, out_ref):
    slots = legendre_ref.shape[2]
    lat_count = out_ref.shape[0]
    third = back_ref.shape[2] // (2 * (FULL * BLOCKS + UNITS))
    half = ROWS // 2
    read = write = 0
    for j in range(GROUPS):
        span = 2 * third * (BLOCKS if j < FULL else 1)
        held = back_ref[:, :, read : read + span].reshape(slots, span)
        modes = jnp.dot(legendre_ref[j], held, preferred_element_type=F32).astype(BF16)
        for k in range(half):
            out_ref[:, :, write + k * span : write + (k + 1) * span] = modes[
                2 * lat_count * k : 2 * lat_count * (k + 1)
            ].reshape(lat_count, 2, span)
        read += span
        write += half * span


def synthesis_kernel(modes_ref, fourier_ref, out_ref):
    narrow = out_ref.shape[1]
    third = narrow // BLOCKS
    half = ROWS // 2

    def piece(k, p, j):
        width = narrow if j < FULL else third
        start = (j if j < FULL else FULL) * half * 2 * narrow + max(j - FULL, 0) * half * 2 * third
        at = start + (2 * (k // 2) + p) * width
        return modes_ref[k % 2, :, at : at + width]

    rows = [
        jnp.concatenate([piece(k, p, j) for k in range(ROWS)], axis=1)
        for j in range(FULL)
        for p in range(2)
    ]
    for p in range(2):
        blocks = []
        for k in range(ROWS):
            blocks += block_rows([piece(k, p, FULL + u) for u in range(UNITS)])
        rows.append(jnp.concatenate(blocks, axis=1))
    grad = lax.dot_general(
        jnp.concatenate(rows, axis=0),
        fourier_ref[...],
        (((0,), (0,)), ((), ())),
        preferred_element_type=F32,
    ).astype(BF16)
    for k in range(ROWS):
        out_ref[k] = grad[k * narrow : (k + 1) * narrow, :]


def place(near, counts_ref, rank_ref, rows_ref, out_ref, sems):
    copies = []
    for r, (live, own, at) in enumerate(held_rows(counts_ref, rank_ref)):
        wanted = live & (own if near else jnp.logical_not(own))
        copy = pltpu.make_async_copy(rows_ref.at[at], out_ref.at[r], sems.at[r])
        pl.when(wanted)(copy.start)
        copies.append((wanted, copy))
    return copies


def gradient_kernel(
    counts_ref, rank_ref, coeffs_ref, mine_ref, _, grad_ref, out_ref, held_ref, sems, grad_sems
):
    copies = place(True, counts_ref, rank_ref, mine_ref, out_ref, sems)
    full = held_ref.shape[1]
    stores = []
    for s in range(2):
        coeffs = side(coeffs_ref, s, 0)
        dcoeffs = side(coeffs_ref, s, 1)
        for lo, hi in ((0, 256), (256, full)):
            held_ref[s, lo:hi, :] = lax.dot_general(
                coeffs[:, lo:hi], dcoeffs, (((0,), (0,)), ((), ())), preferred_element_type=F32
            )
            part = pl.ds(lo, hi - lo)
            stores.append(
                pltpu.make_async_copy(
                    held_ref.at[s, part], grad_ref.at[s, part], grad_sems.at[len(stores)]
                )
            )
            stores[-1].start()
    for wanted, copy in copies:
        pl.when(wanted)(copy.wait)
    for store in stores:
        store.wait()


def placing_kernel(counts_ref, rank_ref, theirs_ref, _, out_ref, sems):
    for wanted, copy in place(False, counts_ref, rank_ref, theirs_ref, out_ref, sems):
        pl.when(wanted)(copy.wait)


def on_device(field_in, cotangent, weights, row_counts, slot_degree):
    lat_count = lax.axis_size("lat")
    chan_count = lax.axis_size("chan")
    rank = lax.axis_index("lat")
    narrow = field_in.shape[1]
    held, full = weights.shape[:2]
    devices = lat_count * chan_count
    pairs = [(i, i ^ 1) for i in range(lat_count)]
    odd = rank % 2
    at_rank = jnp.reshape(rank, (1,)).astype(jnp.int32)
    by_rank, by_part = (jnp.asarray(table) for table in fourier_tables(lat_count))
    pieces = FULL * BLOCKS + UNITS
    third = narrow // BLOCKS
    everyone = ("chan", "lat")

    field_send = lax.dynamic_slice_in_dim(field_in, (1 - odd) * ROWS, ROWS)
    cotan_send = lax.dynamic_slice_in_dim(cotangent, (1 - odd) * ROWS, ROWS)
    field_send, by_rank = lax.optimization_barrier((field_send, by_rank))
    field_swap = lax.ppermute(field_send, "lat", pairs)
    cotan_swap = lax.ppermute(cotan_send, "lat", pairs)
    by_rank = loaded(by_rank, "fourier")
    width = 2 * ROWS * narrow
    modes = run(
        analysis_kernel,
        "analysis",
        [pltpu.HBM((lat_count, 2, pieces * width // BLOCKS), BF16)],
        [row_counts, at_rank, field_in, cotangent, field_swap, cotan_swap, by_rank],
        [
            pltpu.VMEM((width, NLON), BF16),
            pltpu.VMEM((lat_count, 2, pieces * width // BLOCKS), BF16),
            pltpu.SemaphoreType.DMA((GROUPS,)),
        ],
    )
    modes = lax.all_to_all(modes, "lat", split_axis=0, concat_axis=0, tiled=True)
    modes = modes.transpose(1, 0, 2)
    slot_rows = slot_degree.reshape(lat_count, chan_count, held).transpose(1, 0, 2).reshape(-1)
    legendre, legendre_pairs, placed = legendre_slots(
        row_counts, at_rank, lat_count, slot_rows, field_in.shape
    )
    coeffs, weights, legendre_pairs = run(
        forward_kernel,
        "forward",
        [
            pltpu.VMEM((devices, held, 4 * pieces * third), BF16),
            pltpu.VMEM(weights.shape, BF16),
            pltpu.VMEM(legendre_pairs.shape, BF16),
        ],
        [at_rank, modes, legendre, weights, legendre_pairs],
        [pltpu.SemaphoreType.DMA((2,))],
        far=(3, 4),
    )
    coeffs = lax.all_to_all(coeffs, everyone, split_axis=0, concat_axis=0, tiled=True)
    coeffs = coeffs.transpose(1, 0, 2).reshape(held, chan_count, lat_count, 4 * pieces * third)
    back = run(
        degree_kernel,
        "degree",
        [pltpu.VMEM((devices, held, 2 * pieces * third), BF16)],
        [coeffs, weights],
    )
    back = lax.all_to_all(back, everyone, split_axis=0, concat_axis=0, tiled=True)
    modes_back = run(
        backward_kernel,
        "backward",
        [pltpu.VMEM((lat_count, 2, ROWS * pieces * third), BF16)],
        [back, legendre_pairs],
    )
    modes_back = lax.all_to_all(modes_back, "lat", split_axis=0, concat_axis=0, tiled=True)
    grad = run(
        synthesis_kernel,
        "synthesis",
        [pltpu.VMEM((ROWS, narrow, NLON), BF16)],
        [modes_back.transpose(1, 0, 2), by_part],
    )
    grad, coeffs = lax.optimization_barrier((grad, coeffs))
    grad_swap = lax.ppermute(grad, "lat", pairs)
    weight_grad, placed = run(
        gradient_kernel,
        "gradient",
        [pltpu.HBM((held, full, full), F32), pltpu.HBM(field_in.shape, BF16)],
        [row_counts, at_rank, coeffs, grad, placed],
        [
            pltpu.VMEM((held, full, full), F32),
            pltpu.SemaphoreType.DMA((2 * ROWS,)),
            pltpu.SemaphoreType.DMA((2 * held,)),
        ],
        far=(4,),
        aliases={4: 1},
    )
    grad_swap, placed = lax.optimization_barrier((grad_swap, placed))
    field_grad = run(
        placing_kernel,
        "placing",
        [pltpu.HBM(field_in.shape, BF16)],
        [row_counts, at_rank, grad_swap, placed],
        [pltpu.SemaphoreType.DMA((2 * ROWS,))],
        far=(3,),
        aliases={3: 0},
    )
    return field_grad, weight_grad


def solution(mesh):
    placed = (
        P("lat", "chan", None),
        P("lat", "chan", None),
        P(("lat", "chan"), None, None),
        P(),
        P(),
    )
    return jax.shard_map(
        on_device,
        mesh=mesh,
        in_specs=placed,
        out_specs=(P("lat", "chan", None), P(("lat", "chan"), None, None)),
        check_vma=False,
    )
```

```python
import math

import jax
import jax.numpy as jnp
import ml_dtypes
import numpy as np
from jax import lax
from jax.experimental import pallas as pl
from jax.experimental.pallas import tpu as pltpu
from jax.sharding import PartitionSpec as P

NLON = 720
L = 360
M = 360
LPAD = 384
ROWS = 6
FULL = 5
UNITS = 2
BLOCKS = 3
GROUPS = FULL + UNITS
RESCALE = 2.0**40
RESCALE_LOG = 40.0 * math.log(2.0)
BF16 = jnp.bfloat16
F32 = jnp.float32
VMEM_BYTES = 30 * 1024 * 1024


def block_rows(units):
    lat_count = units[0].shape[0]
    last = M - FULL * lat_count
    parts = []
    for at in range(0, BLOCKS * last, last):
        ends = [(max(at, u * lat_count), min(at + last, (u + 1) * lat_count)) for u in range(UNITS)]
        pieces = [
            units[u][lo - u * lat_count : hi - u * lat_count]
            for u, (lo, hi) in enumerate(ends)
            if lo < hi
        ]
        parts.append(pieces[0] if len(pieces) == 1 else jnp.concatenate(pieces, axis=0))
    return parts


def unit_rows(blocks, lat_count, height=1):
    last = M - FULL * lat_count
    units = []
    for u in range(UNITS):
        pieces = []
        for b in range(BLOCKS):
            lo, hi = max(b * last, u * lat_count), min((b + 1) * last, (u + 1) * lat_count)
            if lo < hi:
                pieces.append(blocks[b][(lo - b * last) * height : (hi - b * last) * height])
        dead = (u + 1) * lat_count - max(BLOCKS * last, u * lat_count)
        if dead > 0:
            pieces.append(jnp.zeros((dead * height, blocks[0].shape[1]), blocks[0].dtype))
        units.append(jnp.concatenate(pieces, axis=0))
    return units


def fourier_rows(orders):
    turns = orders[:, None] * np.arange(NLON)[None, :] % NLON
    angles = turns * (2.0 * math.pi / NLON)
    parts = np.stack([np.cos(angles), -np.sin(angles)], axis=1) / math.sqrt(NLON)
    return parts.astype(ml_dtypes.bfloat16)


def fourier_tables(lat_count):
    first = fourier_rows(np.arange(FULL * lat_count)).reshape(FULL, lat_count, 2, NLON)
    last = fourier_rows(np.arange(FULL * lat_count, M))
    by_rank = np.concatenate([first.reshape(-1, NLON), last.reshape(-1, NLON)])
    by_part = np.concatenate(
        [first.transpose(0, 2, 1, 3).reshape(-1, NLON), last.transpose(1, 0, 2).reshape(-1, NLON)]
    )
    return by_rank, by_part


def order_tables(lat_count):
    rank = np.arange(lat_count)[:, None]
    unit = np.arange(UNITS)[None, :] * lat_count + rank
    last = M - FULL * lat_count
    units = np.where(unit < BLOCKS * last, FULL * lat_count + unit % last, 10**6)
    firsts = np.arange(FULL)[None, :] * lat_count + rank
    dead = np.full((lat_count, 8 - GROUPS), 10**6)
    orders = np.concatenate([firsts, units, dead], axis=1)
    logs = [
        0.5 * math.log((2.0 * m + 1.0) / (4.0 * math.pi))
        + 0.5 * math.lgamma(2.0 * m + 1.0)
        - m * math.log(2.0)
        - math.lgamma(m + 1.0)
        for m in np.minimum(orders, M).reshape(-1).tolist()
    ]
    latitudes = ROWS * lat_count
    norms = np.array(logs).reshape(orders.shape) + 0.5 * math.log(2.0 * math.pi**2 / latitudes)
    shape = orders.shape + (128,)
    return tuple(np.broadcast_to(t[:, :, None], shape).astype(np.float32) for t in (orders, norms))


def latitude_rows(lat_count):
    grid = np.arange(lat_count)[None, :] * ROWS + np.arange(ROWS)[:, None]
    paired = grid.reshape(ROWS // 2, 2, lat_count).transpose(0, 2, 1)
    order = np.concatenate([grid.reshape(-1), paired.reshape(-1)])[None, :]
    theta = (order + 0.5) * (math.pi / (ROWS * lat_count))
    return np.cos(theta).astype(np.float32), np.log(np.sin(theta)).astype(np.float32)


def run(kernel, name, outs, args, scratch=(), home=pltpu.VMEM, far=(), aliases={}):
    specs, operands = [], []
    for at, arg in enumerate(args):
        if arg.dtype == jnp.int32 and arg.ndim == 1:
            space = pltpu.SMEM
        else:
            space = pltpu.HBM if at in far else pltpu.VMEM
            arg = pltpu.with_memory_space_constraint(arg, space)
        specs.append(pl.BlockSpec(memory_space=space))
        operands.append(arg)
    results = pl.pallas_call(
        kernel,
        out_shape=tuple(outs),
        in_specs=specs,
        out_specs=tuple(pl.BlockSpec(memory_space=home) for _ in outs),
        scratch_shapes=list(scratch),
        input_output_aliases=aliases,
        compiler_params=pltpu.CompilerParams(vmem_limit_bytes=VMEM_BYTES),
        name=name,
    )(*operands)
    return results if len(outs) > 1 else results[0]


def loading_kernel(stored_ref, out_ref, sem):
    copy = pltpu.make_async_copy(stored_ref, out_ref, sem)
    copy.start()
    copy.wait()


def loaded(array, name):
    return run(
        loading_kernel,
        name,
        [pltpu.VMEM(array.shape, array.dtype)],
        [array],
        [pltpu.SemaphoreType.DMA],
        far=(0,),
    )


def legendre_kernel(
    rank_ref, cosine_ref, logsine_ref, order_ref, norm_ref, slot_ref,
    rows_out_ref, pairs_out_ref, rows_ref,
):
    rank = rank_ref[0]
    latitudes = rows_out_ref.shape[2]
    shape = (8, 128)
    order = order_ref[rank]
    square = order * order
    tiles = cosine_ref.shape[1] // 128
    cosines, scales = [], []
    for t in range(tiles):
        lanes = slice(128 * t, 128 * (t + 1))
        cosines.append(jnp.broadcast_to(cosine_ref[:, lanes], shape))
        logsine = jnp.broadcast_to(logsine_ref[:, lanes], shape)
        scales.append(norm_ref[rank] + order * logsine + 0.5 * logsine)
    zero = jnp.zeros(shape, F32)
    one = jnp.ones(shape, F32)

    def advance(l, carry):
        degree = l.astype(F32)
        below = degree - 1.0
        upper = jnp.sqrt(
            jnp.maximum(4.0 * degree * degree - 1.0, 1.0)
            / jnp.maximum(degree * degree - square, 1.0)
        )
        lower = jnp.sqrt(
            jnp.maximum(below * below - square, 0.0)
            / jnp.maximum(4.0 * below * below - 1.0, 1.0)
        )
        rising = degree > order
        reached = degree >= order
        fresh = []
        for t in range(tiles):
            previous, current, scale = carry[3 * t : 3 * t + 3]
            value = upper * (cosines[t] * current - lower * previous)
            previous = jnp.where(rising, current, previous)
            current = jnp.where(rising, value, current)
            too_large = jnp.abs(current) > RESCALE
            factor = jnp.where(too_large, 1.0 / RESCALE, 1.0)
            previous = previous * factor
            current = current * factor
            scale = scale + jnp.where(too_large, RESCALE_LOG, 0.0)
            rows_ref[l, :, 128 * t : 128 * (t + 1)] = jnp.where(
                reached, current * jnp.exp(scale), 0.0
            )
            fresh += [previous, current, scale]
        return tuple(fresh)

    start = []
    for t in range(tiles):
        start += [zero, one, scales[t]]
    lax.fori_loop(0, L, advance, tuple(start), unroll=4)
    rows_ref[L:, :, :] = jnp.zeros((LPAD - L,) + rows_ref.shape[1:], F32)
    slots = slot_ref.shape[0]
    degrees = lax.broadcasted_iota(jnp.int32, (slots, LPAD), 1)
    pick = jnp.where((degrees == slot_ref[...]) & (degrees < L), 1.0, 0.0).astype(BF16)
    for j in range(GROUPS):
        table = rows_ref[:, j, :latitudes].astype(BF16)
        rows_out_ref[j] = jnp.dot(pick, table, preferred_element_type=F32).astype(BF16)
        table = rows_ref[:, j, latitudes:].astype(BF16)
        pairs_out_ref[j] = lax.dot_general(
            table, pick, (((0,), (1,)), ((), ())), preferred_element_type=F32
        ).astype(BF16)


def legendre_slots(at_rank, lat_count, slot_rows):
    slots = slot_rows.shape[0]
    latitudes = ROWS * lat_count
    cosine, logsine = latitude_rows(lat_count)
    orders, norms = order_tables(lat_count)
    return run(
        legendre_kernel,
        "legendre",
        [pltpu.VMEM((GROUPS, slots, latitudes), BF16), pltpu.HBM((GROUPS, latitudes, slots), BF16)],
        [
            at_rank,
            jnp.asarray(cosine),
            jnp.asarray(logsine),
            jnp.asarray(orders),
            jnp.asarray(norms),
            slot_rows[:, None],
        ],
        [pltpu.VMEM((LPAD, 8, 2 * latitudes), F32)],
    )


def analysis_kernel(
    counts_ref, rank_ref, field_ref, cotan_ref, field_in_ref, cotan_in_ref, fourier_ref,
    out_ref, rows_ref, held_ref, sems,
):
    narrow = field_ref.shape[1]
    lat_count = out_ref.shape[0]
    width = 2 * ROWS * narrow
    rank = rank_ref[0]
    odd = rank % 2
    first = counts_ref[rank - odd]
    for k in range(ROWS):
        own = k + odd * (ROWS - first)
        mine = (own >= 0) & ((odd == 1) | (k < first))
        theirs = jnp.where(odd == 1, k, k - first)
        for w, (here, there) in enumerate(((field_ref, field_in_ref), (cotan_ref, cotan_in_ref))):
            at = slice((2 * k + w) * narrow, (2 * k + w + 1) * narrow)

            @pl.when(mine)
            def _():
                rows_ref[at, :] = here[jnp.clip(own, 0, 2 * ROWS - 1)]

            @pl.when(jnp.logical_not(mine))
            def _():
                rows_ref[at, :] = there[jnp.clip(theirs, 0, ROWS - 1)]

    contract = (((1,), (1,)), ((), ()))
    full = 2 * lat_count * FULL
    stores = []

    def send(lo, hi):
        lanes = pl.ds(lo, hi - lo)
        store = pltpu.make_async_copy(
            held_ref.at[:, :, lanes], out_ref.at[:, :, lanes], sems.at[len(stores)]
        )
        store.start()
        stores.append(store)

    third = narrow // BLOCKS
    blocks = []
    for b in range(BLOCKS):
        rows = jnp.concatenate(
            [
                rows_ref[i * narrow + b * third : i * narrow + (b + 1) * third, :]
                for i in range(2 * ROWS)
            ],
            axis=0,
        )
        blocks.append(
            lax.dot_general(
                fourier_ref[full:, :], rows, contract, preferred_element_type=F32
            ).astype(BF16)
        )
    for u, unit in enumerate(unit_rows(blocks, lat_count, 2)):
        at = FULL * width + u * (width // BLOCKS)
        held_ref[:, :, at : at + width // BLOCKS] = unit.reshape(lat_count, 2, width // BLOCKS)
    send(FULL * width, out_ref.shape[2])
    for j0, j1 in ((0, 2), (2, 4), (4, FULL)):
        modes = lax.dot_general(
            fourier_ref[2 * lat_count * j0 : 2 * lat_count * j1, :],
            rows_ref[...],
            contract,
            preferred_element_type=F32,
        ).astype(BF16)
        for j in range(j0, j1):
            held_ref[:, :, j * width : (j + 1) * width] = modes[
                2 * lat_count * (j - j0) : 2 * lat_count * (j - j0 + 1)
            ].reshape(lat_count, 2, width)
        send(j0 * width, j1 * width)
    for store in stores:
        store.wait()


def forward_kernel(
    rank_ref, modes_ref, legendre_ref, stored_ref, stored_pairs_ref,
    out_ref, weights_ref, pairs_ref, sems,
):
    loads = [
        pltpu.make_async_copy(stored_pairs_ref, pairs_ref, sems.at[0]),
        pltpu.make_async_copy(stored_ref, weights_ref, sems.at[1]),
    ]
    for load in loads:
        load.start()
    owners = out_ref.shape[0]
    slots = legendre_ref.shape[1]
    read = write = 0
    for j in range(GROUPS):
        width = modes_ref.shape[2] // (ROWS * (FULL * BLOCKS + UNITS)) * (BLOCKS if j < FULL else 1)
        slab = jnp.concatenate(
            [
                jnp.concatenate(
                    [
                        modes_ref[p, :, read + k * width : read + (k + 1) * width]
                        for p in range(2)
                    ],
                    axis=1,
                )
                for k in range(ROWS)
            ],
            axis=0,
        )
        coeffs = jnp.dot(legendre_ref[j], slab, preferred_element_type=F32)
        lane = lax.broadcasted_iota(jnp.int32, (slots, 2 * width), 1)
        cotangent = lane // (width // 2) % 2 == 1
        doubled = jnp.where(rank_ref[0] + j == 0, 1.0, 2.0)
        coeffs = jnp.where(cotangent, coeffs * doubled, coeffs)
        out_ref[:, :, write : write + 2 * width] = coeffs.astype(BF16).reshape(
            owners, 2, 2 * width
        )
        read += ROWS * width
        write += 2 * width
    for load in loads:
        load.wait()


def side(coeffs_ref, s, w):
    chans = coeffs_ref.shape[1]
    third = coeffs_ref.shape[3] // (4 * (FULL * BLOCKS + UNITS))
    narrow = BLOCKS * third
    rows = [
        jnp.concatenate(
            [
                coeffs_ref[s, y, :, (2 * jp + w) * narrow : (2 * jp + w + 1) * narrow]
                for y in range(chans)
            ],
            axis=1,
        )
        for jp in range(2 * FULL)
    ]
    for p in range(2):
        at = 4 * FULL * narrow + (2 * p + w) * third
        pieces = []
        for y in range(chans):
            pieces += block_rows(
                [
                    coeffs_ref[s, y, :, at + u * 4 * third : at + u * 4 * third + third]
                    for u in range(UNITS)
                ]
            )
        rows.append(jnp.concatenate(pieces, axis=1))
    return jnp.concatenate(rows, axis=0)


def degree_kernel(coeffs_ref, weights_ref, stored_ref, back_ref, table_ref, sem):
    load = pltpu.make_async_copy(stored_ref, table_ref, sem)
    load.start()
    chans, lat_count = coeffs_ref.shape[1:3]
    third = coeffs_ref.shape[3] // (4 * (FULL * BLOCKS + UNITS))
    narrow = BLOCKS * third
    full = 2 * FULL * lat_count
    last = M - FULL * lat_count
    for s in range(2):
        back = lax.dot_general(
            side(coeffs_ref, s, 1),
            weights_ref[s],
            (((1,), (1,)), ((), ())),
            preferred_element_type=F32,
        ).astype(BF16)
        for y in range(chans):
            lanes = slice(y * narrow, (y + 1) * narrow)
            pieces = [back[jp * lat_count : (jp + 1) * lat_count, lanes] for jp in range(2 * FULL)]
            units = []
            for p in range(2):
                rows = slice(full + p * last, full + (p + 1) * last)
                units.append(
                    unit_rows(
                        [
                            back[rows, y * narrow + b * third : y * narrow + (b + 1) * third]
                            for b in range(BLOCKS)
                        ],
                        lat_count,
                    )
                )
            pieces += [units[p][u] for u in range(UNITS) for p in range(2)]
            back_ref[y * lat_count : (y + 1) * lat_count, s, :] = jnp.concatenate(pieces, axis=1)
    load.wait()


def backward_kernel(back_ref, legendre_ref, out_ref):
    slots = legendre_ref.shape[2]
    lat_count = out_ref.shape[0]
    third = back_ref.shape[2] // (2 * (FULL * BLOCKS + UNITS))
    half = ROWS // 2
    read = write = 0
    for j in range(GROUPS):
        span = 2 * third * (BLOCKS if j < FULL else 1)
        held = back_ref[:, :, read : read + span].reshape(slots, span)
        modes = jnp.dot(legendre_ref[j], held, preferred_element_type=F32).astype(BF16)
        for k in range(half):
            out_ref[:, :, write + k * span : write + (k + 1) * span] = modes[
                2 * lat_count * k : 2 * lat_count * (k + 1)
            ].reshape(lat_count, 2, span)
        read += span
        write += half * span


def synthesis_kernel(modes_ref, fourier_ref, out_ref):
    narrow = out_ref.shape[1]
    third = narrow // BLOCKS
    half = ROWS // 2

    def piece(k, p, j):
        width = narrow if j < FULL else third
        start = (j if j < FULL else FULL) * half * 2 * narrow + max(j - FULL, 0) * half * 2 * third
        at = start + (2 * (k // 2) + p) * width
        return modes_ref[k % 2, :, at : at + width]

    rows = [
        jnp.concatenate([piece(k, p, j) for k in range(ROWS)], axis=1)
        for j in range(FULL)
        for p in range(2)
    ]
    for p in range(2):
        blocks = []
        for k in range(ROWS):
            blocks += block_rows([piece(k, p, FULL + u) for u in range(UNITS)])
        rows.append(jnp.concatenate(blocks, axis=1))
    grad = lax.dot_general(
        jnp.concatenate(rows, axis=0),
        fourier_ref[...],
        (((0,), (0,)), ((), ())),
        preferred_element_type=F32,
    ).astype(BF16)
    for k in range(ROWS):
        out_ref[k] = grad[k * narrow : (k + 1) * narrow, :]


def held_rows(counts_ref, rank_ref):
    rank = rank_ref[0]
    odd = rank % 2
    first = counts_ref[rank - odd]
    count = jnp.where(odd == 1, 2 * ROWS - first, first)
    slots = []
    for r in range(2 * ROWS):
        at = odd * first + r
        slots.append((r < count, (at // ROWS) == odd, jnp.clip(at % ROWS, 0, ROWS - 1)))
    return slots


def gradient_kernel(coeffs_ref, grad_ref, held_ref, sems):
    stores = []
    for s in range(2):
        held_ref[s] = lax.dot_general(
            side(coeffs_ref, s, 0),
            side(coeffs_ref, s, 1),
            (((0,), (0,)), ((), ())),
            preferred_element_type=F32,
        )
        stores.append(pltpu.make_async_copy(held_ref.at[s], grad_ref.at[s], sems.at[s]))
        stores[-1].start()
    for store in stores:
        store.wait()


def own_kernel(counts_ref, rank_ref, mine_ref, out_ref, empty_ref, sems):
    empty_ref[...] = jnp.zeros_like(empty_ref)
    rows = []
    for r, (live, own, at) in enumerate(held_rows(counts_ref, rank_ref)):
        target, sem = out_ref.at[r], sems.at[r]
        near = pltpu.make_async_copy(mine_ref.at[at], target, sem)
        dead = pltpu.make_async_copy(empty_ref, target, sem)
        pl.when(live & own)(near.start)
        pl.when(jnp.logical_not(live))(dead.start)
        rows.append((jnp.logical_not(live) | own, near))
    for started, row in rows:
        pl.when(started)(row.wait)


def placing_kernel(counts_ref, rank_ref, theirs_ref, placed_ref, out_ref, sems):
    rows = []
    for r, (live, own, at) in enumerate(held_rows(counts_ref, rank_ref)):
        wanted = live & jnp.logical_not(own)
        row = pltpu.make_async_copy(theirs_ref.at[at], out_ref.at[r], sems.at[r])
        pl.when(wanted)(row.start)
        rows.append((wanted, row))
    for wanted, row in rows:
        pl.when(wanted)(row.wait)


def on_device(field_in, cotangent, weights, row_counts, slot_degree):
    lat_count = lax.axis_size("lat")
    chan_count = lax.axis_size("chan")
    rank = lax.axis_index("lat")
    narrow = field_in.shape[1]
    held, full = weights.shape[:2]
    devices = lat_count * chan_count
    pairs = [(i, i ^ 1) for i in range(lat_count)]
    odd = rank % 2
    at_rank = jnp.reshape(rank, (1,)).astype(jnp.int32)
    by_rank, by_part = (jnp.asarray(table) for table in fourier_tables(lat_count))
    pieces = FULL * BLOCKS + UNITS
    third = narrow // BLOCKS
    everyone = ("chan", "lat")

    field_send = lax.dynamic_slice_in_dim(field_in, (1 - odd) * ROWS, ROWS)
    cotan_send = lax.dynamic_slice_in_dim(cotangent, (1 - odd) * ROWS, ROWS)
    field_send, by_rank = lax.optimization_barrier((field_send, by_rank))
    field_swap = lax.ppermute(field_send, "lat", pairs)
    cotan_swap = lax.ppermute(cotan_send, "lat", pairs)
    by_rank = loaded(by_rank, "fourier")
    width = 2 * ROWS * narrow
    modes = run(
        analysis_kernel,
        "analysis",
        [pltpu.HBM((lat_count, 2, pieces * width // BLOCKS), BF16)],
        [row_counts, at_rank, field_in, cotangent, field_swap, cotan_swap, by_rank],
        [
            pltpu.VMEM((width, NLON), BF16),
            pltpu.VMEM((lat_count, 2, pieces * width // BLOCKS), BF16),
            pltpu.SemaphoreType.DMA((GROUPS,)),
        ],
        home=pltpu.HBM,
    )
    modes = lax.all_to_all(modes, "lat", split_axis=0, concat_axis=0, tiled=True)
    modes = modes.transpose(1, 0, 2)
    slot_rows = slot_degree.reshape(lat_count, chan_count, held).transpose(1, 0, 2).reshape(-1)
    legendre, legendre_pairs = legendre_slots(at_rank, lat_count, slot_rows)
    coeffs, weights, legendre_pairs = run(
        forward_kernel,
        "forward",
        [
            pltpu.VMEM((devices, held, 4 * pieces * third), BF16),
            pltpu.VMEM(weights.shape, BF16),
            pltpu.VMEM(legendre_pairs.shape, BF16),
        ],
        [at_rank, modes, legendre, weights, legendre_pairs],
        [pltpu.SemaphoreType.DMA((2,))],
        far=(3, 4),
    )
    coeffs = lax.all_to_all(coeffs, everyone, split_axis=0, concat_axis=0, tiled=True)
    coeffs = coeffs.transpose(1, 0, 2).reshape(held, chan_count, lat_count, 4 * pieces * third)
    back, by_part = run(
        degree_kernel,
        "degree",
        [
            pltpu.VMEM((devices, held, 2 * pieces * third), BF16),
            pltpu.VMEM(by_part.shape, BF16),
        ],
        [coeffs, weights, by_part],
        [pltpu.SemaphoreType.DMA],
        far=(2,),
    )
    back = lax.all_to_all(back, everyone, split_axis=0, concat_axis=0, tiled=True)
    modes_back = run(
        backward_kernel,
        "backward",
        [pltpu.VMEM((lat_count, 2, ROWS * pieces * third), BF16)],
        [back, legendre_pairs],
    )
    modes_back, coeffs = lax.optimization_barrier((modes_back, coeffs))
    modes_back = lax.all_to_all(modes_back, "lat", split_axis=0, concat_axis=0, tiled=True)
    weight_grad = run(
        gradient_kernel,
        "gradient",
        [pltpu.HBM((held, full, full), F32)],
        [coeffs],
        [pltpu.VMEM((held, full, full), F32), pltpu.SemaphoreType.DMA((held,))],
        home=pltpu.HBM,
    )
    modes_back, weight_grad = lax.optimization_barrier((modes_back, weight_grad))
    grad = run(
        synthesis_kernel,
        "synthesis",
        [pltpu.VMEM((ROWS, narrow, NLON), BF16)],
        [modes_back.transpose(1, 0, 2), by_part],
    )
    grad_swap = lax.ppermute(grad, "lat", pairs)
    placed = run(
        own_kernel,
        "own",
        [pltpu.HBM(field_in.shape, BF16)],
        [row_counts, at_rank, grad],
        [pltpu.VMEM((narrow, NLON), BF16), pltpu.SemaphoreType.DMA((2 * ROWS,))],
        home=pltpu.HBM,
    )
    grad_swap, placed = lax.optimization_barrier((grad_swap, placed))
    field_grad = run(
        placing_kernel,
        "placing",
        [pltpu.HBM(field_in.shape, BF16)],
        [row_counts, at_rank, grad_swap, placed],
        [pltpu.SemaphoreType.DMA((2 * ROWS,))],
        home=pltpu.HBM,
        far=(3,),
        aliases={3: 0},
    )
    return field_grad, weight_grad


def solution(mesh):
    placed = (
        P("lat", "chan", None),
        P("lat", "chan", None),
        P(("lat", "chan"), None, None),
        P(),
        P(),
    )
    return jax.shard_map(
        on_device,
        mesh=mesh,
        in_specs=placed,
        out_specs=(P("lat", "chan", None), P(("lat", "chan"), None, None)),
        check_vma=False,
    )
```

```python
import math

import jax
import jax.numpy as jnp
import ml_dtypes
import numpy as np
from jax import lax
from jax.experimental import pallas as pl
from jax.experimental.pallas import tpu as pltpu
from jax.sharding import PartitionSpec as P

NLON = 720
L = 360
M = 360
LPAD = 384
ROWS = 6
FULL = 5
UNITS = 2
BLOCKS = 3
GROUPS = FULL + UNITS
RESCALE = 2.0**40
RESCALE_LOG = 40.0 * math.log(2.0)
BF16 = jnp.bfloat16
F32 = jnp.float32
VMEM_BYTES = 30 * 1024 * 1024


def block_rows(units):
    lat_count = units[0].shape[0]
    last = M - FULL * lat_count
    parts = []
    for at in range(0, BLOCKS * last, last):
        ends = [(max(at, u * lat_count), min(at + last, (u + 1) * lat_count)) for u in range(UNITS)]
        pieces = [
            units[u][lo - u * lat_count : hi - u * lat_count]
            for u, (lo, hi) in enumerate(ends)
            if lo < hi
        ]
        parts.append(pieces[0] if len(pieces) == 1 else jnp.concatenate(pieces, axis=0))
    return parts


def unit_rows(blocks, lat_count, height=1):
    last = M - FULL * lat_count
    units = []
    for u in range(UNITS):
        pieces = []
        for b in range(BLOCKS):
            lo, hi = max(b * last, u * lat_count), min((b + 1) * last, (u + 1) * lat_count)
            if lo < hi:
                pieces.append(blocks[b][(lo - b * last) * height : (hi - b * last) * height])
        dead = (u + 1) * lat_count - max(BLOCKS * last, u * lat_count)
        if dead > 0:
            pieces.append(jnp.zeros((dead * height, blocks[0].shape[1]), blocks[0].dtype))
        units.append(jnp.concatenate(pieces, axis=0))
    return units


def fourier_rows(orders):
    turns = orders[:, None] * np.arange(NLON)[None, :] % NLON
    angles = turns * (2.0 * math.pi / NLON)
    parts = np.stack([np.cos(angles), -np.sin(angles)], axis=1) / math.sqrt(NLON)
    return parts.astype(ml_dtypes.bfloat16)


def fourier_tables(lat_count):
    first = fourier_rows(np.arange(FULL * lat_count)).reshape(FULL, lat_count, 2, NLON)
    last = fourier_rows(np.arange(FULL * lat_count, M))
    by_rank = np.concatenate([first.reshape(-1, NLON), last.reshape(-1, NLON)])
    by_part = np.concatenate(
        [first.transpose(0, 2, 1, 3).reshape(-1, NLON), last.transpose(1, 0, 2).reshape(-1, NLON)]
    )
    return by_rank, by_part


def order_tables(lat_count):
    rank = np.arange(lat_count)[:, None]
    unit = np.arange(UNITS)[None, :] * lat_count + rank
    last = M - FULL * lat_count
    units = np.where(unit < BLOCKS * last, FULL * lat_count + unit % last, 10**6)
    firsts = np.arange(FULL)[None, :] * lat_count + rank
    dead = np.full((lat_count, 8 - GROUPS), 10**6)
    orders = np.concatenate([firsts, units, dead], axis=1)
    logs = [
        0.5 * math.log((2.0 * m + 1.0) / (4.0 * math.pi))
        + 0.5 * math.lgamma(2.0 * m + 1.0)
        - m * math.log(2.0)
        - math.lgamma(m + 1.0)
        for m in np.minimum(orders, M).reshape(-1).tolist()
    ]
    latitudes = ROWS * lat_count
    norms = np.array(logs).reshape(orders.shape) + 0.5 * math.log(2.0 * math.pi**2 / latitudes)
    shape = orders.shape + (128,)
    return tuple(np.broadcast_to(t[:, :, None], shape).astype(np.float32) for t in (orders, norms))


def latitude_rows(lat_count):
    grid = np.arange(lat_count)[None, :] * ROWS + np.arange(ROWS)[:, None]
    paired = grid.reshape(ROWS // 2, 2, lat_count).transpose(0, 2, 1)
    order = np.concatenate([grid.reshape(-1), paired.reshape(-1)])[None, :]
    theta = (order + 0.5) * (math.pi / (ROWS * lat_count))
    return np.cos(theta).astype(np.float32), np.log(np.sin(theta)).astype(np.float32)


def run(kernel, name, outs, args, scratch=(), home=pltpu.VMEM, far=(), aliases={}):
    specs, operands = [], []
    for at, arg in enumerate(args):
        if arg.dtype == jnp.int32 and arg.ndim == 1:
            space = pltpu.SMEM
        else:
            space = pltpu.HBM if at in far else pltpu.VMEM
            arg = pltpu.with_memory_space_constraint(arg, space)
        specs.append(pl.BlockSpec(memory_space=space))
        operands.append(arg)
    results = pl.pallas_call(
        kernel,
        out_shape=tuple(outs),
        in_specs=specs,
        out_specs=tuple(pl.BlockSpec(memory_space=home) for _ in outs),
        scratch_shapes=list(scratch),
        input_output_aliases=aliases,
        compiler_params=pltpu.CompilerParams(vmem_limit_bytes=VMEM_BYTES),
        name=name,
    )(*operands)
    return results if len(outs) > 1 else results[0]


def loading_kernel(stored_ref, out_ref, sem):
    copy = pltpu.make_async_copy(stored_ref, out_ref, sem)
    copy.start()
    copy.wait()


def loaded(array, name):
    return run(
        loading_kernel,
        name,
        [pltpu.VMEM(array.shape, array.dtype)],
        [array],
        [pltpu.SemaphoreType.DMA],
        far=(0,),
    )


def legendre_kernel(
    rank_ref, cosine_ref, logsine_ref, order_ref, norm_ref, slot_ref,
    rows_out_ref, pairs_out_ref, rows_ref,
):
    rank = rank_ref[0]
    latitudes = rows_out_ref.shape[2]
    shape = (8, 128)
    order = order_ref[rank]
    square = order * order
    tiles = cosine_ref.shape[1] // 128
    cosines, scales = [], []
    for t in range(tiles):
        lanes = slice(128 * t, 128 * (t + 1))
        cosines.append(jnp.broadcast_to(cosine_ref[:, lanes], shape))
        logsine = jnp.broadcast_to(logsine_ref[:, lanes], shape)
        scales.append(norm_ref[rank] + order * logsine + 0.5 * logsine)
    zero = jnp.zeros(shape, F32)
    one = jnp.ones(shape, F32)

    def advance(l, carry):
        degree = l.astype(F32)
        below = degree - 1.0
        upper = jnp.sqrt(
            jnp.maximum(4.0 * degree * degree - 1.0, 1.0)
            / jnp.maximum(degree * degree - square, 1.0)
        )
        lower = jnp.sqrt(
            jnp.maximum(below * below - square, 0.0)
            / jnp.maximum(4.0 * below * below - 1.0, 1.0)
        )
        rising = degree > order
        reached = degree >= order
        fresh = []
        for t in range(tiles):
            previous, current, scale = carry[3 * t : 3 * t + 3]
            value = upper * (cosines[t] * current - lower * previous)
            previous = jnp.where(rising, current, previous)
            current = jnp.where(rising, value, current)
            too_large = jnp.abs(current) > RESCALE
            factor = jnp.where(too_large, 1.0 / RESCALE, 1.0)
            previous = previous * factor
            current = current * factor
            scale = scale + jnp.where(too_large, RESCALE_LOG, 0.0)
            rows_ref[l, :, 128 * t : 128 * (t + 1)] = jnp.where(
                reached, current * jnp.exp(scale), 0.0
            )
            fresh += [previous, current, scale]
        return tuple(fresh)

    start = []
    for t in range(tiles):
        start += [zero, one, scales[t]]
    lax.fori_loop(0, L, advance, tuple(start), unroll=4)
    rows_ref[L:, :, :] = jnp.zeros((LPAD - L,) + rows_ref.shape[1:], F32)
    slots = slot_ref.shape[0]
    degrees = lax.broadcasted_iota(jnp.int32, (slots, LPAD), 1)
    pick = jnp.where((degrees == slot_ref[...]) & (degrees < L), 1.0, 0.0).astype(BF16)
    for j in range(GROUPS):
        table = rows_ref[:, j, :latitudes].astype(BF16)
        rows_out_ref[j] = jnp.dot(pick, table, preferred_element_type=F32).astype(BF16)
        table = rows_ref[:, j, latitudes:].astype(BF16)
        pairs_out_ref[j] = lax.dot_general(
            table, pick, (((0,), (1,)), ((), ())), preferred_element_type=F32
        ).astype(BF16)


def legendre_slots(at_rank, lat_count, slot_rows):
    slots = slot_rows.shape[0]
    latitudes = ROWS * lat_count
    cosine, logsine = latitude_rows(lat_count)
    orders, norms = order_tables(lat_count)
    return run(
        legendre_kernel,
        "legendre",
        [pltpu.VMEM((GROUPS, slots, latitudes), BF16), pltpu.HBM((GROUPS, latitudes, slots), BF16)],
        [
            at_rank,
            jnp.asarray(cosine),
            jnp.asarray(logsine),
            jnp.asarray(orders),
            jnp.asarray(norms),
            slot_rows[:, None],
        ],
        [pltpu.VMEM((LPAD, 8, 2 * latitudes), F32)],
    )


def analysis_kernel(
    counts_ref, rank_ref, field_ref, cotan_ref, field_in_ref, cotan_in_ref, fourier_ref,
    out_ref, rows_ref, held_ref, sems,
):
    narrow = field_ref.shape[1]
    lat_count = out_ref.shape[0]
    width = 2 * ROWS * narrow
    rank = rank_ref[0]
    odd = rank % 2
    first = counts_ref[rank - odd]
    for k in range(ROWS):
        own = k + odd * (ROWS - first)
        mine = (own >= 0) & ((odd == 1) | (k < first))
        theirs = jnp.where(odd == 1, k, k - first)
        for w, (here, there) in enumerate(((field_ref, field_in_ref), (cotan_ref, cotan_in_ref))):
            at = slice((2 * k + w) * narrow, (2 * k + w + 1) * narrow)

            @pl.when(mine)
            def _():
                rows_ref[at, :] = here[jnp.clip(own, 0, 2 * ROWS - 1)]

            @pl.when(jnp.logical_not(mine))
            def _():
                rows_ref[at, :] = there[jnp.clip(theirs, 0, ROWS - 1)]

    contract = (((1,), (1,)), ((), ()))
    full = 2 * lat_count * FULL
    stores = []

    def send(lo, hi):
        lanes = pl.ds(lo, hi - lo)
        store = pltpu.make_async_copy(
            held_ref.at[:, :, lanes], out_ref.at[:, :, lanes], sems.at[len(stores)]
        )
        store.start()
        stores.append(store)

    third = narrow // BLOCKS
    blocks = []
    for b in range(BLOCKS):
        rows = jnp.concatenate(
            [
                rows_ref[i * narrow + b * third : i * narrow + (b + 1) * third, :]
                for i in range(2 * ROWS)
            ],
            axis=0,
        )
        blocks.append(
            lax.dot_general(
                fourier_ref[full:, :], rows, contract, preferred_element_type=F32
            ).astype(BF16)
        )
    for u, unit in enumerate(unit_rows(blocks, lat_count, 2)):
        at = FULL * width + u * (width // BLOCKS)
        held_ref[:, :, at : at + width // BLOCKS] = unit.reshape(lat_count, 2, width // BLOCKS)
    send(FULL * width, out_ref.shape[2])
    for j0, j1 in ((0, 2), (2, 4), (4, FULL)):
        modes = lax.dot_general(
            fourier_ref[2 * lat_count * j0 : 2 * lat_count * j1, :],
            rows_ref[...],
            contract,
            preferred_element_type=F32,
        ).astype(BF16)
        for j in range(j0, j1):
            held_ref[:, :, j * width : (j + 1) * width] = modes[
                2 * lat_count * (j - j0) : 2 * lat_count * (j - j0 + 1)
            ].reshape(lat_count, 2, width)
        send(j0 * width, j1 * width)
    for store in stores:
        store.wait()


def forward_kernel(
    rank_ref, modes_ref, legendre_ref, stored_ref, stored_pairs_ref,
    out_ref, weights_ref, pairs_ref, sems,
):
    loads = [
        pltpu.make_async_copy(stored_pairs_ref, pairs_ref, sems.at[0]),
        pltpu.make_async_copy(stored_ref, weights_ref, sems.at[1]),
    ]
    for load in loads:
        load.start()
    owners = out_ref.shape[0]
    slots = legendre_ref.shape[1]
    read = write = 0
    for j in range(GROUPS):
        width = modes_ref.shape[2] // (ROWS * (FULL * BLOCKS + UNITS)) * (BLOCKS if j < FULL else 1)
        slab = jnp.concatenate(
            [
                jnp.concatenate(
                    [
                        modes_ref[p, :, read + k * width : read + (k + 1) * width]
                        for p in range(2)
                    ],
                    axis=1,
                )
                for k in range(ROWS)
            ],
            axis=0,
        )
        coeffs = jnp.dot(legendre_ref[j], slab, preferred_element_type=F32)
        lane = lax.broadcasted_iota(jnp.int32, (slots, 2 * width), 1)
        cotangent = lane // (width // 2) % 2 == 1
        doubled = jnp.where(rank_ref[0] + j == 0, 1.0, 2.0)
        coeffs = jnp.where(cotangent, coeffs * doubled, coeffs)
        out_ref[:, :, write : write + 2 * width] = coeffs.astype(BF16).reshape(
            owners, 2, 2 * width
        )
        read += ROWS * width
        write += 2 * width
    for load in loads:
        load.wait()


def side(coeffs_ref, s, w):
    chans = coeffs_ref.shape[1]
    third = coeffs_ref.shape[3] // (4 * (FULL * BLOCKS + UNITS))
    narrow = BLOCKS * third
    rows = [
        jnp.concatenate(
            [
                coeffs_ref[s, y, :, (2 * jp + w) * narrow : (2 * jp + w + 1) * narrow]
                for y in range(chans)
            ],
            axis=1,
        )
        for jp in range(2 * FULL)
    ]
    for p in range(2):
        at = 4 * FULL * narrow + (2 * p + w) * third
        pieces = []
        for y in range(chans):
            pieces += block_rows(
                [
                    coeffs_ref[s, y, :, at + u * 4 * third : at + u * 4 * third + third]
                    for u in range(UNITS)
                ]
            )
        rows.append(jnp.concatenate(pieces, axis=1))
    return jnp.concatenate(rows, axis=0)


def degree_kernel(coeffs_ref, weights_ref, back_ref):
    chans, lat_count = coeffs_ref.shape[1:3]
    third = coeffs_ref.shape[3] // (4 * (FULL * BLOCKS + UNITS))
    narrow = BLOCKS * third
    full = 2 * FULL * lat_count
    last = M - FULL * lat_count
    for s in range(2):
        back = lax.dot_general(
            side(coeffs_ref, s, 1),
            weights_ref[s],
            (((1,), (1,)), ((), ())),
            preferred_element_type=F32,
        ).astype(BF16)
        for y in range(chans):
            lanes = slice(y * narrow, (y + 1) * narrow)
            pieces = [back[jp * lat_count : (jp + 1) * lat_count, lanes] for jp in range(2 * FULL)]
            units = []
            for p in range(2):
                rows = slice(full + p * last, full + (p + 1) * last)
                units.append(
                    unit_rows(
                        [
                            back[rows, y * narrow + b * third : y * narrow + (b + 1) * third]
                            for b in range(BLOCKS)
                        ],
                        lat_count,
                    )
                )
            pieces += [units[p][u] for u in range(UNITS) for p in range(2)]
            back_ref[y * lat_count : (y + 1) * lat_count, s, :] = jnp.concatenate(pieces, axis=1)


def backward_kernel(back_ref, legendre_ref, out_ref):
    slots = legendre_ref.shape[2]
    lat_count = out_ref.shape[0]
    third = back_ref.shape[2] // (2 * (FULL * BLOCKS + UNITS))
    half = ROWS // 2
    read = write = 0
    for j in range(GROUPS):
        span = 2 * third * (BLOCKS if j < FULL else 1)
        held = back_ref[:, :, read : read + span].reshape(slots, span)
        modes = jnp.dot(legendre_ref[j], held, preferred_element_type=F32).astype(BF16)
        for k in range(half):
            out_ref[:, :, write + k * span : write + (k + 1) * span] = modes[
                2 * lat_count * k : 2 * lat_count * (k + 1)
            ].reshape(lat_count, 2, span)
        read += span
        write += half * span


def synthesis_kernel(modes_ref, fourier_ref, out_ref):
    narrow = out_ref.shape[1]
    third = narrow // BLOCKS
    half = ROWS // 2

    def piece(k, p, j):
        width = narrow if j < FULL else third
        start = (j if j < FULL else FULL) * half * 2 * narrow + max(j - FULL, 0) * half * 2 * third
        at = start + (2 * (k // 2) + p) * width
        return modes_ref[k % 2, :, at : at + width]

    rows = [
        jnp.concatenate([piece(k, p, j) for k in range(ROWS)], axis=1)
        for j in range(FULL)
        for p in range(2)
    ]
    for p in range(2):
        blocks = []
        for k in range(ROWS):
            blocks += block_rows([piece(k, p, FULL + u) for u in range(UNITS)])
        rows.append(jnp.concatenate(blocks, axis=1))
    grad = lax.dot_general(
        jnp.concatenate(rows, axis=0),
        fourier_ref[...],
        (((0,), (0,)), ((), ())),
        preferred_element_type=F32,
    ).astype(BF16)
    for k in range(ROWS):
        out_ref[k] = grad[k * narrow : (k + 1) * narrow, :]


def held_rows(counts_ref, rank_ref):
    rank = rank_ref[0]
    odd = rank % 2
    first = counts_ref[rank - odd]
    count = jnp.where(odd == 1, 2 * ROWS - first, first)
    slots = []
    for r in range(2 * ROWS):
        at = odd * first + r
        slots.append((r < count, (at // ROWS) == odd, jnp.clip(at % ROWS, 0, ROWS - 1)))
    return slots


def gradient_kernel(
    counts_ref, rank_ref, coeffs_ref, mine_ref, grad_ref, out_ref, held_ref, empty_ref, sems, grad_sems
):
    empty_ref[...] = jnp.zeros_like(empty_ref)
    rows = []
    for r, (live, own, at) in enumerate(held_rows(counts_ref, rank_ref)):
        target, sem = out_ref.at[r], sems.at[r]
        near = pltpu.make_async_copy(mine_ref.at[at], target, sem)
        dead = pltpu.make_async_copy(empty_ref, target, sem)
        pl.when(live & own)(near.start)
        pl.when(jnp.logical_not(live))(dead.start)
        rows.append((jnp.logical_not(live) | own, near))
    stores = []
    for s in range(2):
        held_ref[s] = lax.dot_general(
            side(coeffs_ref, s, 0),
            side(coeffs_ref, s, 1),
            (((0,), (0,)), ((), ())),
            preferred_element_type=F32,
        )
        stores.append(pltpu.make_async_copy(held_ref.at[s], grad_ref.at[s], grad_sems.at[s]))
        stores[-1].start()
    for started, row in rows:
        pl.when(started)(row.wait)
    for store in stores:
        store.wait()


def placing_kernel(counts_ref, rank_ref, theirs_ref, placed_ref, out_ref, sems):
    rows = []
    for r, (live, own, at) in enumerate(held_rows(counts_ref, rank_ref)):
        wanted = live & jnp.logical_not(own)
        row = pltpu.make_async_copy(theirs_ref.at[at], out_ref.at[r], sems.at[r])
        pl.when(wanted)(row.start)
        rows.append((wanted, row))
    for wanted, row in rows:
        pl.when(wanted)(row.wait)


def on_device(field_in, cotangent, weights, row_counts, slot_degree):
    lat_count = lax.axis_size("lat")
    chan_count = lax.axis_size("chan")
    rank = lax.axis_index("lat")
    narrow = field_in.shape[1]
    held, full = weights.shape[:2]
    devices = lat_count * chan_count
    pairs = [(i, i ^ 1) for i in range(lat_count)]
    odd = rank % 2
    at_rank = jnp.reshape(rank, (1,)).astype(jnp.int32)
    by_rank, by_part = (jnp.asarray(table) for table in fourier_tables(lat_count))
    pieces = FULL * BLOCKS + UNITS
    third = narrow // BLOCKS
    everyone = ("chan", "lat")

    field_send = lax.dynamic_slice_in_dim(field_in, (1 - odd) * ROWS, ROWS)
    cotan_send = lax.dynamic_slice_in_dim(cotangent, (1 - odd) * ROWS, ROWS)
    field_send, cotan_send, by_rank = lax.optimization_barrier((field_send, cotan_send, by_rank))
    field_swap = lax.ppermute(field_send, "lat", pairs)
    cotan_swap = lax.ppermute(cotan_send, "lat", pairs)
    by_rank = loaded(by_rank, "fourier")
    width = 2 * ROWS * narrow
    modes = run(
        analysis_kernel,
        "analysis",
        [pltpu.HBM((lat_count, 2, pieces * width // BLOCKS), BF16)],
        [row_counts, at_rank, field_in, cotangent, field_swap, cotan_swap, by_rank],
        [
            pltpu.VMEM((width, NLON), BF16),
            pltpu.VMEM((lat_count, 2, pieces * width // BLOCKS), BF16),
            pltpu.SemaphoreType.DMA((GROUPS,)),
        ],
        home=pltpu.HBM,
    )
    modes = lax.all_to_all(modes, "lat", split_axis=0, concat_axis=0, tiled=True)
    modes = modes.transpose(1, 0, 2)
    slot_rows = slot_degree.reshape(lat_count, chan_count, held).transpose(1, 0, 2).reshape(-1)
    legendre, legendre_pairs = legendre_slots(at_rank, lat_count, slot_rows)
    coeffs, weights, legendre_pairs = run(
        forward_kernel,
        "forward",
        [
            pltpu.VMEM((devices, held, 4 * pieces * third), BF16),
            pltpu.VMEM(weights.shape, BF16),
            pltpu.VMEM(legendre_pairs.shape, BF16),
        ],
        [at_rank, modes, legendre, weights, legendre_pairs],
        [pltpu.SemaphoreType.DMA((2,))],
        far=(3, 4),
    )
    coeffs = lax.all_to_all(coeffs, everyone, split_axis=0, concat_axis=0, tiled=True)
    coeffs = coeffs.transpose(1, 0, 2).reshape(held, chan_count, lat_count, 4 * pieces * third)
    back = run(
        degree_kernel,
        "degree",
        [pltpu.VMEM((devices, held, 2 * pieces * third), BF16)],
        [coeffs, weights],
    )
    back = lax.all_to_all(back, everyone, split_axis=0, concat_axis=0, tiled=True)
    modes_back = run(
        backward_kernel,
        "backward",
        [pltpu.VMEM((lat_count, 2, ROWS * pieces * third), BF16)],
        [back, legendre_pairs],
    )
    modes_back = lax.all_to_all(modes_back, "lat", split_axis=0, concat_axis=0, tiled=True)
    grad = run(
        synthesis_kernel,
        "synthesis",
        [pltpu.VMEM((ROWS, narrow, NLON), BF16)],
        [modes_back.transpose(1, 0, 2), by_part],
    )
    grad, coeffs = lax.optimization_barrier((grad, coeffs))
    grad_swap = lax.ppermute(grad, "lat", pairs)
    weight_grad, placed = run(
        gradient_kernel,
        "gradient",
        [pltpu.HBM((held, full, full), F32), pltpu.HBM(field_in.shape, BF16)],
        [row_counts, at_rank, coeffs, grad],
        [
            pltpu.VMEM((held, full, full), F32),
            pltpu.VMEM((narrow, NLON), BF16),
            pltpu.SemaphoreType.DMA((2 * ROWS,)),
            pltpu.SemaphoreType.DMA((held,)),
        ],
        home=pltpu.HBM,
    )
    grad_swap, placed = lax.optimization_barrier((grad_swap, placed))
    field_grad = run(
        placing_kernel,
        "placing",
        [pltpu.HBM(field_in.shape, BF16)],
        [row_counts, at_rank, grad_swap, placed],
        [pltpu.SemaphoreType.DMA((2 * ROWS,))],
        home=pltpu.HBM,
        far=(3,),
        aliases={3: 0},
    )
    return field_grad, weight_grad


def solution(mesh):
    placed = (
        P("lat", "chan", None),
        P("lat", "chan", None),
        P(("lat", "chan"), None, None),
        P(),
        P(),
    )
    return jax.shard_map(
        on_device,
        mesh=mesh,
        in_specs=placed,
        out_specs=(P("lat", "chan", None), P(("lat", "chan"), None, None)),
        check_vma=False,
    )
```

```python
import math

import jax
import jax.numpy as jnp
import ml_dtypes
import numpy as np
from jax import lax
from jax.experimental import pallas as pl
from jax.experimental.pallas import tpu as pltpu
from jax.sharding import PartitionSpec as P

NLON = 720
L = 360
M = 360
LPAD = 384
ROWS = 6
FULL = 5
UNITS = 2
BLOCKS = 3
GROUPS = FULL + UNITS
RESCALE = 2.0**40
RESCALE_LOG = 40.0 * math.log(2.0)
BF16 = jnp.bfloat16
F32 = jnp.float32
VMEM_BYTES = 30 * 1024 * 1024


def block_rows(units):
    lat_count = units[0].shape[0]
    last = M - FULL * lat_count
    parts = []
    for at in range(0, BLOCKS * last, last):
        ends = [(max(at, u * lat_count), min(at + last, (u + 1) * lat_count)) for u in range(UNITS)]
        pieces = [
            units[u][lo - u * lat_count : hi - u * lat_count]
            for u, (lo, hi) in enumerate(ends)
            if lo < hi
        ]
        parts.append(pieces[0] if len(pieces) == 1 else jnp.concatenate(pieces, axis=0))
    return parts


def unit_rows(blocks, lat_count, height=1):
    last = M - FULL * lat_count
    units = []
    for u in range(UNITS):
        pieces = []
        for b in range(BLOCKS):
            lo, hi = max(b * last, u * lat_count), min((b + 1) * last, (u + 1) * lat_count)
            if lo < hi:
                pieces.append(blocks[b][(lo - b * last) * height : (hi - b * last) * height])
        dead = (u + 1) * lat_count - max(BLOCKS * last, u * lat_count)
        if dead > 0:
            pieces.append(jnp.zeros((dead * height, blocks[0].shape[1]), blocks[0].dtype))
        units.append(jnp.concatenate(pieces, axis=0))
    return units


def fourier_rows(orders):
    turns = orders[:, None] * np.arange(NLON)[None, :] % NLON
    angles = turns * (2.0 * math.pi / NLON)
    parts = np.stack([np.cos(angles), -np.sin(angles)], axis=1) / math.sqrt(NLON)
    return parts.astype(ml_dtypes.bfloat16)


def fourier_tables(lat_count):
    first = fourier_rows(np.arange(FULL * lat_count)).reshape(FULL, lat_count, 2, NLON)
    last = fourier_rows(np.arange(FULL * lat_count, M))
    by_rank = np.concatenate([first.reshape(-1, NLON), last.reshape(-1, NLON)])
    by_part = np.concatenate(
        [first.transpose(0, 2, 1, 3).reshape(-1, NLON), last.transpose(1, 0, 2).reshape(-1, NLON)]
    )
    return by_rank, by_part


def order_tables(lat_count):
    rank = np.arange(lat_count)[:, None]
    unit = np.arange(UNITS)[None, :] * lat_count + rank
    last = M - FULL * lat_count
    units = np.where(unit < BLOCKS * last, FULL * lat_count + unit % last, 10**6)
    firsts = np.arange(FULL)[None, :] * lat_count + rank
    dead = np.full((lat_count, 8 - GROUPS), 10**6)
    orders = np.concatenate([firsts, units, dead], axis=1)
    logs = [
        0.5 * math.log((2.0 * m + 1.0) / (4.0 * math.pi))
        + 0.5 * math.lgamma(2.0 * m + 1.0)
        - m * math.log(2.0)
        - math.lgamma(m + 1.0)
        for m in np.minimum(orders, M).reshape(-1).tolist()
    ]
    latitudes = ROWS * lat_count
    norms = np.array(logs).reshape(orders.shape) + 0.5 * math.log(2.0 * math.pi**2 / latitudes)
    shape = orders.shape + (128,)
    return tuple(np.broadcast_to(t[:, :, None], shape).astype(np.float32) for t in (orders, norms))


def latitude_rows(lat_count):
    grid = np.arange(lat_count)[None, :] * ROWS + np.arange(ROWS)[:, None]
    paired = grid.reshape(ROWS // 2, 2, lat_count).transpose(0, 2, 1)
    order = np.concatenate([grid.reshape(-1), paired.reshape(-1)])[None, :]
    theta = (order + 0.5) * (math.pi / (ROWS * lat_count))
    return np.cos(theta).astype(np.float32), np.log(np.sin(theta)).astype(np.float32)


def run(kernel, name, outs, args, scratch=(), home=pltpu.VMEM, far=(), aliases={}):
    specs, operands = [], []
    for at, arg in enumerate(args):
        if arg.dtype == jnp.int32 and arg.ndim == 1:
            space = pltpu.SMEM
        else:
            space = pltpu.HBM if at in far else pltpu.VMEM
            arg = pltpu.with_memory_space_constraint(arg, space)
        specs.append(pl.BlockSpec(memory_space=space))
        operands.append(arg)
    results = pl.pallas_call(
        kernel,
        out_shape=tuple(outs),
        in_specs=specs,
        out_specs=tuple(pl.BlockSpec(memory_space=home) for _ in outs),
        scratch_shapes=list(scratch),
        input_output_aliases=aliases,
        compiler_params=pltpu.CompilerParams(vmem_limit_bytes=VMEM_BYTES),
        name=name,
    )(*operands)
    return results if len(outs) > 1 else results[0]


def loading_kernel(stored_ref, out_ref, sem):
    copy = pltpu.make_async_copy(stored_ref, out_ref, sem)
    copy.start()
    copy.wait()


def loaded(array, name):
    return run(
        loading_kernel,
        name,
        [pltpu.VMEM(array.shape, array.dtype)],
        [array],
        [pltpu.SemaphoreType.DMA],
        far=(0,),
    )


def legendre_kernel(
    rank_ref, cosine_ref, logsine_ref, order_ref, norm_ref, slot_ref,
    rows_out_ref, pairs_out_ref, rows_ref,
):
    rank = rank_ref[0]
    latitudes = rows_out_ref.shape[2]
    shape = (8, 128)
    order = order_ref[rank]
    square = order * order
    tiles = cosine_ref.shape[1] // 128
    cosines, scales = [], []
    for t in range(tiles):
        lanes = slice(128 * t, 128 * (t + 1))
        cosines.append(jnp.broadcast_to(cosine_ref[:, lanes], shape))
        logsine = jnp.broadcast_to(logsine_ref[:, lanes], shape)
        scales.append(norm_ref[rank] + order * logsine + 0.5 * logsine)
    zero = jnp.zeros(shape, F32)
    one = jnp.ones(shape, F32)

    def advance(l, carry):
        degree = l.astype(F32)
        below = degree - 1.0
        upper = jnp.sqrt(
            jnp.maximum(4.0 * degree * degree - 1.0, 1.0)
            / jnp.maximum(degree * degree - square, 1.0)
        )
        lower = jnp.sqrt(
            jnp.maximum(below * below - square, 0.0)
            / jnp.maximum(4.0 * below * below - 1.0, 1.0)
        )
        rising = degree > order
        reached = degree >= order
        fresh = []
        for t in range(tiles):
            previous, current, scale = carry[3 * t : 3 * t + 3]
            value = upper * (cosines[t] * current - lower * previous)
            previous = jnp.where(rising, current, previous)
            current = jnp.where(rising, value, current)
            too_large = jnp.abs(current) > RESCALE
            factor = jnp.where(too_large, 1.0 / RESCALE, 1.0)
            previous = previous * factor
            current = current * factor
            scale = scale + jnp.where(too_large, RESCALE_LOG, 0.0)
            rows_ref[l, :, 128 * t : 128 * (t + 1)] = jnp.where(
                reached, current * jnp.exp(scale), 0.0
            )
            fresh += [previous, current, scale]
        return tuple(fresh)

    start = []
    for t in range(tiles):
        start += [zero, one, scales[t]]
    lax.fori_loop(0, L, advance, tuple(start), unroll=4)
    rows_ref[L:, :, :] = jnp.zeros((LPAD - L,) + rows_ref.shape[1:], F32)
    slots = slot_ref.shape[0]
    degrees = lax.broadcasted_iota(jnp.int32, (slots, LPAD), 1)
    pick = jnp.where((degrees == slot_ref[...]) & (degrees < L), 1.0, 0.0).astype(BF16)
    for j in range(GROUPS):
        table = rows_ref[:, j, :latitudes].astype(BF16)
        rows_out_ref[j] = jnp.dot(pick, table, preferred_element_type=F32).astype(BF16)
        table = rows_ref[:, j, latitudes:].astype(BF16)
        pairs_out_ref[j] = lax.dot_general(
            table, pick, (((0,), (1,)), ((), ())), preferred_element_type=F32
        ).astype(BF16)


def legendre_slots(at_rank, lat_count, slot_rows):
    slots = slot_rows.shape[0]
    latitudes = ROWS * lat_count
    cosine, logsine = latitude_rows(lat_count)
    orders, norms = order_tables(lat_count)
    return run(
        legendre_kernel,
        "legendre",
        [pltpu.VMEM((GROUPS, slots, latitudes), BF16), pltpu.HBM((GROUPS, latitudes, slots), BF16)],
        [
            at_rank,
            jnp.asarray(cosine),
            jnp.asarray(logsine),
            jnp.asarray(orders),
            jnp.asarray(norms),
            slot_rows[:, None],
        ],
        [pltpu.VMEM((LPAD, 8, 2 * latitudes), F32)],
    )


def analysis_kernel(
    counts_ref, rank_ref, field_ref, cotan_ref, field_in_ref, cotan_in_ref, fourier_ref,
    out_ref, rows_ref, held_ref, sems,
):
    narrow = field_ref.shape[1]
    lat_count = out_ref.shape[0]
    width = 2 * ROWS * narrow
    rank = rank_ref[0]
    odd = rank % 2
    first = counts_ref[rank - odd]
    for k in range(ROWS):
        own = k + odd * (ROWS - first)
        mine = (own >= 0) & ((odd == 1) | (k < first))
        theirs = jnp.where(odd == 1, k, k - first)
        for w, (here, there) in enumerate(((field_ref, field_in_ref), (cotan_ref, cotan_in_ref))):
            at = slice((2 * k + w) * narrow, (2 * k + w + 1) * narrow)

            @pl.when(mine)
            def _():
                rows_ref[at, :] = here[jnp.clip(own, 0, 2 * ROWS - 1)]

            @pl.when(jnp.logical_not(mine))
            def _():
                rows_ref[at, :] = there[jnp.clip(theirs, 0, ROWS - 1)]

    contract = (((1,), (1,)), ((), ()))
    full = 2 * lat_count * FULL
    stores = []

    def send(lo, hi):
        lanes = pl.ds(lo, hi - lo)
        store = pltpu.make_async_copy(
            held_ref.at[:, :, lanes], out_ref.at[:, :, lanes], sems.at[len(stores)]
        )
        store.start()
        stores.append(store)

    third = narrow // BLOCKS
    blocks = []
    for b in range(BLOCKS):
        rows = jnp.concatenate(
            [
                rows_ref[i * narrow + b * third : i * narrow + (b + 1) * third, :]
                for i in range(2 * ROWS)
            ],
            axis=0,
        )
        blocks.append(
            lax.dot_general(
                fourier_ref[full:, :], rows, contract, preferred_element_type=F32
            ).astype(BF16)
        )
    for u, unit in enumerate(unit_rows(blocks, lat_count, 2)):
        at = FULL * width + u * (width // BLOCKS)
        held_ref[:, :, at : at + width // BLOCKS] = unit.reshape(lat_count, 2, width // BLOCKS)
    send(FULL * width, out_ref.shape[2])
    for j0, j1 in ((0, 3), (3, FULL)):
        modes = lax.dot_general(
            fourier_ref[2 * lat_count * j0 : 2 * lat_count * j1, :],
            rows_ref[...],
            contract,
            preferred_element_type=F32,
        ).astype(BF16)
        for j in range(j0, j1):
            held_ref[:, :, j * width : (j + 1) * width] = modes[
                2 * lat_count * (j - j0) : 2 * lat_count * (j - j0 + 1)
            ].reshape(lat_count, 2, width)
        send(j0 * width, j1 * width)
    for store in stores:
        store.wait()


def forward_kernel(
    rank_ref, modes_ref, legendre_ref, stored_ref, stored_pairs_ref,
    out_ref, weights_ref, pairs_ref, sems,
):
    loads = [
        pltpu.make_async_copy(stored_pairs_ref, pairs_ref, sems.at[0]),
        pltpu.make_async_copy(stored_ref, weights_ref, sems.at[1]),
    ]
    for load in loads:
        load.start()
    owners = out_ref.shape[0]
    slots = legendre_ref.shape[1]
    read = write = 0
    for j in range(GROUPS):
        width = modes_ref.shape[2] // (ROWS * (FULL * BLOCKS + UNITS)) * (BLOCKS if j < FULL else 1)
        slab = jnp.concatenate(
            [
                jnp.concatenate(
                    [
                        modes_ref[p, :, read + k * width : read + (k + 1) * width]
                        for p in range(2)
                    ],
                    axis=1,
                )
                for k in range(ROWS)
            ],
            axis=0,
        )
        coeffs = jnp.dot(legendre_ref[j], slab, preferred_element_type=F32)
        lane = lax.broadcasted_iota(jnp.int32, (slots, 2 * width), 1)
        cotangent = lane // (width // 2) % 2 == 1
        doubled = jnp.where(rank_ref[0] + j == 0, 1.0, 2.0)
        coeffs = jnp.where(cotangent, coeffs * doubled, coeffs)
        out_ref[:, :, write : write + 2 * width] = coeffs.astype(BF16).reshape(
            owners, 2, 2 * width
        )
        read += ROWS * width
        write += 2 * width
    for load in loads:
        load.wait()


def side(coeffs_ref, s, w):
    chans = coeffs_ref.shape[1]
    third = coeffs_ref.shape[3] // (4 * (FULL * BLOCKS + UNITS))
    narrow = BLOCKS * third
    rows = [
        jnp.concatenate(
            [
                coeffs_ref[s, y, :, (2 * jp + w) * narrow : (2 * jp + w + 1) * narrow]
                for y in range(chans)
            ],
            axis=1,
        )
        for jp in range(2 * FULL)
    ]
    for p in range(2):
        at = 4 * FULL * narrow + (2 * p + w) * third
        pieces = []
        for y in range(chans):
            pieces += block_rows(
                [
                    coeffs_ref[s, y, :, at + u * 4 * third : at + u * 4 * third + third]
                    for u in range(UNITS)
                ]
            )
        rows.append(jnp.concatenate(pieces, axis=1))
    return jnp.concatenate(rows, axis=0)


def degree_kernel(coeffs_ref, weights_ref, back_ref):
    chans, lat_count = coeffs_ref.shape[1:3]
    third = coeffs_ref.shape[3] // (4 * (FULL * BLOCKS + UNITS))
    narrow = BLOCKS * third
    full = 2 * FULL * lat_count
    last = M - FULL * lat_count
    for s in range(2):
        back = lax.dot_general(
            side(coeffs_ref, s, 1),
            weights_ref[s],
            (((1,), (1,)), ((), ())),
            preferred_element_type=F32,
        ).astype(BF16)
        for y in range(chans):
            lanes = slice(y * narrow, (y + 1) * narrow)
            pieces = [back[jp * lat_count : (jp + 1) * lat_count, lanes] for jp in range(2 * FULL)]
            units = []
            for p in range(2):
                rows = slice(full + p * last, full + (p + 1) * last)
                units.append(
                    unit_rows(
                        [
                            back[rows, y * narrow + b * third : y * narrow + (b + 1) * third]
                            for b in range(BLOCKS)
                        ],
                        lat_count,
                    )
                )
            pieces += [units[p][u] for u in range(UNITS) for p in range(2)]
            back_ref[y * lat_count : (y + 1) * lat_count, s, :] = jnp.concatenate(pieces, axis=1)


def backward_kernel(back_ref, legendre_ref, out_ref):
    slots = legendre_ref.shape[2]
    lat_count = out_ref.shape[0]
    third = back_ref.shape[2] // (2 * (FULL * BLOCKS + UNITS))
    half = ROWS // 2
    read = write = 0
    for j in range(GROUPS):
        span = 2 * third * (BLOCKS if j < FULL else 1)
        held = back_ref[:, :, read : read + span].reshape(slots, span)
        modes = jnp.dot(legendre_ref[j], held, preferred_element_type=F32).astype(BF16)
        for k in range(half):
            out_ref[:, :, write + k * span : write + (k + 1) * span] = modes[
                2 * lat_count * k : 2 * lat_count * (k + 1)
            ].reshape(lat_count, 2, span)
        read += span
        write += half * span


def synthesis_kernel(modes_ref, fourier_ref, out_ref):
    narrow = out_ref.shape[1]
    third = narrow // BLOCKS
    half = ROWS // 2

    def piece(k, p, j):
        width = narrow if j < FULL else third
        start = (j if j < FULL else FULL) * half * 2 * narrow + max(j - FULL, 0) * half * 2 * third
        at = start + (2 * (k // 2) + p) * width
        return modes_ref[k % 2, :, at : at + width]

    rows = [
        jnp.concatenate([piece(k, p, j) for k in range(ROWS)], axis=1)
        for j in range(FULL)
        for p in range(2)
    ]
    for p in range(2):
        blocks = []
        for k in range(ROWS):
            blocks += block_rows([piece(k, p, FULL + u) for u in range(UNITS)])
        rows.append(jnp.concatenate(blocks, axis=1))
    grad = lax.dot_general(
        jnp.concatenate(rows, axis=0),
        fourier_ref[...],
        (((0,), (0,)), ((), ())),
        preferred_element_type=F32,
    ).astype(BF16)
    for k in range(ROWS):
        out_ref[k] = grad[k * narrow : (k + 1) * narrow, :]


def held_rows(counts_ref, rank_ref):
    rank = rank_ref[0]
    odd = rank % 2
    first = counts_ref[rank - odd]
    count = jnp.where(odd == 1, 2 * ROWS - first, first)
    slots = []
    for r in range(2 * ROWS):
        at = odd * first + r
        slots.append((r < count, (at // ROWS) == odd, jnp.clip(at % ROWS, 0, ROWS - 1)))
    return slots


def gradient_kernel(
    counts_ref, rank_ref, coeffs_ref, mine_ref, grad_ref, out_ref, held_ref, empty_ref, sems, grad_sems
):
    empty_ref[...] = jnp.zeros_like(empty_ref)
    rows = []
    for r, (live, own, at) in enumerate(held_rows(counts_ref, rank_ref)):
        target, sem = out_ref.at[r], sems.at[r]
        near = pltpu.make_async_copy(mine_ref.at[at], target, sem)
        dead = pltpu.make_async_copy(empty_ref, target, sem)
        pl.when(live & own)(near.start)
        pl.when(jnp.logical_not(live))(dead.start)
        rows.append((jnp.logical_not(live) | own, near))
    stores = []
    for s in range(2):
        held_ref[s] = lax.dot_general(
            side(coeffs_ref, s, 0),
            side(coeffs_ref, s, 1),
            (((0,), (0,)), ((), ())),
            preferred_element_type=F32,
        )
        stores.append(pltpu.make_async_copy(held_ref.at[s], grad_ref.at[s], grad_sems.at[s]))
        stores[-1].start()
    for started, row in rows:
        pl.when(started)(row.wait)
    for store in stores:
        store.wait()


def placing_kernel(counts_ref, rank_ref, theirs_ref, placed_ref, out_ref, sems):
    rows = []
    for r, (live, own, at) in enumerate(held_rows(counts_ref, rank_ref)):
        wanted = live & jnp.logical_not(own)
        row = pltpu.make_async_copy(theirs_ref.at[at], out_ref.at[r], sems.at[r])
        pl.when(wanted)(row.start)
        rows.append((wanted, row))
    for wanted, row in rows:
        pl.when(wanted)(row.wait)


def on_device(field_in, cotangent, weights, row_counts, slot_degree):
    lat_count = lax.axis_size("lat")
    chan_count = lax.axis_size("chan")
    rank = lax.axis_index("lat")
    narrow = field_in.shape[1]
    held, full = weights.shape[:2]
    devices = lat_count * chan_count
    pairs = [(i, i ^ 1) for i in range(lat_count)]
    odd = rank % 2
    at_rank = jnp.reshape(rank, (1,)).astype(jnp.int32)
    by_rank, by_part = (jnp.asarray(table) for table in fourier_tables(lat_count))
    pieces = FULL * BLOCKS + UNITS
    third = narrow // BLOCKS
    everyone = ("chan", "lat")

    field_send = lax.dynamic_slice_in_dim(field_in, (1 - odd) * ROWS, ROWS)
    cotan_send = lax.dynamic_slice_in_dim(cotangent, (1 - odd) * ROWS, ROWS)
    field_send, by_rank = lax.optimization_barrier((field_send, by_rank))
    field_swap = lax.ppermute(field_send, "lat", pairs)
    cotan_swap = lax.ppermute(cotan_send, "lat", pairs)
    by_rank = loaded(by_rank, "fourier")
    width = 2 * ROWS * narrow
    modes = run(
        analysis_kernel,
        "analysis",
        [pltpu.HBM((lat_count, 2, pieces * width // BLOCKS), BF16)],
        [row_counts, at_rank, field_in, cotangent, field_swap, cotan_swap, by_rank],
        [
            pltpu.VMEM((width, NLON), BF16),
            pltpu.VMEM((lat_count, 2, pieces * width // BLOCKS), BF16),
            pltpu.SemaphoreType.DMA((GROUPS,)),
        ],
        home=pltpu.HBM,
    )
    modes = lax.all_to_all(modes, "lat", split_axis=0, concat_axis=0, tiled=True)
    modes = modes.transpose(1, 0, 2)
    slot_rows = slot_degree.reshape(lat_count, chan_count, held).transpose(1, 0, 2).reshape(-1)
    legendre, legendre_pairs = legendre_slots(at_rank, lat_count, slot_rows)
    coeffs, weights, legendre_pairs = run(
        forward_kernel,
        "forward",
        [
            pltpu.VMEM((devices, held, 4 * pieces * third), BF16),
            pltpu.VMEM(weights.shape, BF16),
            pltpu.VMEM(legendre_pairs.shape, BF16),
        ],
        [at_rank, modes, legendre, weights, legendre_pairs],
        [pltpu.SemaphoreType.DMA((2,))],
        far=(3, 4),
    )
    coeffs = lax.all_to_all(coeffs, everyone, split_axis=0, concat_axis=0, tiled=True)
    coeffs = coeffs.transpose(1, 0, 2).reshape(held, chan_count, lat_count, 4 * pieces * third)
    back = run(
        degree_kernel,
        "degree",
        [pltpu.VMEM((devices, held, 2 * pieces * third), BF16)],
        [coeffs, weights],
    )
    back = lax.all_to_all(back, everyone, split_axis=0, concat_axis=0, tiled=True)
    modes_back = run(
        backward_kernel,
        "backward",
        [pltpu.VMEM((lat_count, 2, ROWS * pieces * third), BF16)],
        [back, legendre_pairs],
    )
    modes_back = lax.all_to_all(modes_back, "lat", split_axis=0, concat_axis=0, tiled=True)
    grad = run(
        synthesis_kernel,
        "synthesis",
        [pltpu.VMEM((ROWS, narrow, NLON), BF16)],
        [modes_back.transpose(1, 0, 2), by_part],
    )
    grad, coeffs = lax.optimization_barrier((grad, coeffs))
    grad_swap = lax.ppermute(grad, "lat", pairs)
    weight_grad, placed = run(
        gradient_kernel,
        "gradient",
        [pltpu.HBM((held, full, full), F32), pltpu.HBM(field_in.shape, BF16)],
        [row_counts, at_rank, coeffs, grad],
        [
            pltpu.VMEM((held, full, full), F32),
            pltpu.VMEM((narrow, NLON), BF16),
            pltpu.SemaphoreType.DMA((2 * ROWS,)),
            pltpu.SemaphoreType.DMA((held,)),
        ],
        home=pltpu.HBM,
    )
    grad_swap, placed = lax.optimization_barrier((grad_swap, placed))
    field_grad = run(
        placing_kernel,
        "placing",
        [pltpu.HBM(field_in.shape, BF16)],
        [row_counts, at_rank, grad_swap, placed],
        [pltpu.SemaphoreType.DMA((2 * ROWS,))],
        home=pltpu.HBM,
        far=(3,),
        aliases={3: 0},
    )
    return field_grad, weight_grad


def solution(mesh):
    placed = (
        P("lat", "chan", None),
        P("lat", "chan", None),
        P(("lat", "chan"), None, None),
        P(),
        P(),
    )
    return jax.shard_map(
        on_device,
        mesh=mesh,
        in_specs=placed,
        out_specs=(P("lat", "chan", None), P(("lat", "chan"), None, None)),
        check_vma=False,
    )
```
